128 devices in a mesh: row: 8 (over z, x_lo), col: 16 (over y, x_hi, core).
Axes of the slice: x: 4 (x_hi: 2, x_lo: 2; x = x_hi * 2 + x_lo), y: 4, z: 4, core: 2. Of those that a mesh axis runs over, the one named last changes fastest.
Arguments:
- kernel: float32 [16384, 16384], P(('row', 'col')), may hold values from -1 to 6, as said below
- start_block: float32 [16384, 128], P(('row', 'col')), may hold values from -6 to 6
- test_kernel: float32 [16384, 256], P(('row', 'col')), may hold values from -67.88225 to 67.88225
- cutoff: int32 [1], replicated, may hold values from 32 to 128
Outputs:
- subspace: float32 [16384, 128], P(('row', 'col'))
- projection: float32 [16384, 256], P(('row', 'col'))
The draws below stay inside these ranges and needn't reach their ends.
Inputs may be any that keep to these rules, and one draw needn't show every extreme that they name: `kernel`: symmetric.
All inputs are finite; a program needn't handle non-finite values.
Results may differ from the reference program's by a relative error of at most 0.0003.
Values sent between devices are 32-bit elements; how exact they have to be, the bound alone decides.
A program may use at most 128 MiB of HBM per device.

```python
import math
import jax
import jax.numpy as jnp
from jax import lax

KERNEL_ORDER = 16384
BLOCK_WIDTH = 128
TEST_IMAGES = 256
ITERATIONS = 4


def draw_kernel(key, part):
    key = jax.random.fold_in(key, 7)
    noise_key, diagonal_key = jax.random.split(key)
    noise = jnp.clip(jax.random.normal(noise_key, (KERNEL_ORDER, KERNEL_ORDER), jnp.float32), -6.0, 6.0)
    symmetric = (noise + noise.T) * 0.5
    position = jnp.arange(KERNEL_ORDER)
    on_diagonal = position[:, None] == position[None, :]
    spread = 0.7 / math.sqrt(KERNEL_ORDER)
    diagonal = jax.random.uniform(diagonal_key, (KERNEL_ORDER,), jnp.float32, 3.0, 5.0)
    return jnp.where(on_diagonal, diagonal[:, None], symmetric * spread)


def block_scale(key, dims, cuts, low, high):
    level = 1.0
    for dim, shards_of in cuts:
        draws = jax.random.uniform(jax.random.fold_in(jax.random.fold_in(key, 6), dim), (shards_of,), jnp.float32, low / len(cuts), high / len(cuts))
        level = level * jnp.repeat(jnp.exp(draws), dims[dim] // shards_of).reshape((-1,) + (1,) * (len(dims) - 1 - dim))
    return level


def gaussian(stream_key, dims, scale, most, shards=(), kind=jnp.bfloat16):
    factor_of = block_scale(stream_key, dims, shards, -0.22, 0.18) if shards else 1.0
    result = jax.random.normal(stream_key, dims, jnp.float32) * scale * factor_of
    return jnp.minimum(jnp.maximum(result, -most), most).astype(kind)


def setup_inputs(seed: int = 0) -> dict:
    key_list = jax.random.split(jax.random.key(seed), 5)
    kernel = draw_kernel(jax.random.fold_in(key_list[4], 71), 0)
    start_block = gaussian(key_list[1], (KERNEL_ORDER, BLOCK_WIDTH), 1.0, 6.0, ((0, 128),), jnp.float32)
    test_kernel = gaussian(key_list[2], (KERNEL_ORDER, TEST_IMAGES), ((KERNEL_ORDER // BLOCK_WIDTH) ** 0.5), 67.88225, ((0, 128),), jnp.float32)
    cutoff = jax.random.randint(key_list[3], (1,), BLOCK_WIDTH // 4, BLOCK_WIDTH + 1).astype(jnp.int32)
    return dict(kernel=kernel, start_block=start_block, test_kernel=test_kernel, cutoff=cutoff)


def orthonormal(image, gram):
    lower = jnp.linalg.cholesky(gram)
    identity = jnp.eye(gram.shape[0], dtype=jnp.float32)
    inverse = lax.linalg.triangular_solve(lower, identity, left_side=True, lower=True)
    return jnp.dot(image.astype(jnp.float32), inverse.T.astype(jnp.float32), precision=lax.Precision.HIGHEST, preferred_element_type=jnp.float32)

def reference(kernel, start_block, test_kernel, cutoff):
    block = start_block
    for step in range(ITERATIONS):
        image = jnp.dot(kernel.astype(jnp.float32), block.astype(jnp.float32), precision=lax.Precision.HIGHEST, preferred_element_type=jnp.float32)
        gram = jnp.dot(image.T.astype(jnp.float32), image.astype(jnp.float32), precision=lax.Precision.HIGHEST, preferred_element_type=jnp.float32)
        block = orthonormal(image, gram)
    coefficients = jnp.dot(block.T.astype(jnp.float32), test_kernel.astype(jnp.float32), precision=lax.Precision.HIGHEST, preferred_element_type=jnp.float32)
    keep = (jnp.arange(BLOCK_WIDTH) < cutoff[0]).astype(jnp.float32)
    coefficients = coefficients * keep[:, None]
    projection = jnp.dot(block.astype(jnp.float32), coefficients.astype(jnp.float32), precision=lax.Precision.HIGHEST, preferred_element_type=jnp.float32)
    return (block, projection)
```

```python
import functools
import itertools

import jax
import jax.numpy as jnp
from jax import lax
from jax.experimental import pallas as pl
from jax.experimental.pallas import tpu as pltpu
from jax.sharding import PartitionSpec as P

BLOCK = 128
TEST = 256
ITERATIONS = 4
RING = 4
SLOTS = RING**3
CHUNK = 8
HALF = BLOCK // 2
MESH = pl.DeviceIdType.MESH
HIGHEST = lax.Precision.HIGHEST
STEPS = [(axis, sign) for axis in range(3) for sign in (1, -1)]


def spanning_tree():
    depth = lambda d: sum(min(c, RING - c) for c in d)

    def options(d):
        found = []
        for label, (axis, sign) in enumerate(STEPS):
            before = list(d)
            before[axis] = (before[axis] - sign) % RING
            if depth(before) == depth(d) - 1:
                found.append((label, tuple(before)))
        return found

    points = sorted(itertools.product(range(RING), repeat=3), key=lambda d: (depth(d), d))
    choice = {d: options(d)[0] for d in points[1:]}

    def cost():
        whole, level, degree = {}, {}, {}
        for d, (label, parent) in choice.items():
            whole[label] = whole.get(label, 0) + 1
            level[depth(d), label] = level.get((depth(d), label), 0) + 1
            degree[parent] = degree.get(parent, 0) + 1
        square = lambda counts: sum(v * v for v in counts.values())
        return 4 * square(whole) + 2 * square(level) + square(degree)

    best, changed = cost(), True
    while changed:
        changed = False
        for d in points[1:]:
            for option in options(d):
                kept = choice[d]
                choice[d] = option
                now = cost()
                if now < best:
                    best, changed = now, True
                else:
                    choice[d] = kept
    order = points[:1]
    for level in range(1, 7):
        rest = [d for d in points if depth(d) == level]
        seen = {}
        ranked = []
        for d in rest:
            label = choice[d][0]
            seen[label] = seen.get(label, 0) + 1
            ranked.append((order.index(choice[d][1]), seen[label], label, d))
        order += [d for *_, d in sorted(ranked)]
    slot = {d: i for i, d in enumerate(order)}
    children = [[] for _ in order]
    for d in order[1:]:
        label, parent = choice[d]
        children[slot[parent]].append((slot[d], label))
    return order, children


ORDER, CHILDREN = spanning_tree()


def exact_dot(a, b, dims=(((1,), (0,)), ((), ()))):
    return lax.dot_general(a, b, dims, precision=HIGHEST, preferred_element_type=jnp.float32)


def eliminate(m, inverse, panel):
    base = 8 * panel
    wide = (8, BLOCK)
    lane = lax.broadcasted_iota(jnp.int32, wide, 1)
    within = (lane >= base) & (lane < base + 8)
    top = m[base : base + 8, :]
    raw = [jnp.broadcast_to(top[k : k + 1, :], wide) for k in range(8)]
    a = {
        (k, i): jnp.broadcast_to(raw[k][:, base + i : base + i + 1], wide) for k in range(8) for i in range(k, 8)
    }
    rows = [jnp.where(within, jnp.where(lane == base + k, 1.0, 0.0), raw[k]) for k in range(8)]
    over, factor = [], {}
    for k in range(8):
        over.append(1.0 / a[k, k])
        for i in range(k + 1, 8):
            factor[k, i] = a[k, i] * over[k]
            for j in range(i, 8):
                a[i, j] = a[i, j] - factor[k, i] * a[k, j]
            rows[i] = rows[i] - factor[k, i] * rows[k]
    for k in range(8):
        done = jnp.where(lane < base + 8, rows[k] * (over[k] * jnp.sqrt(a[k, k])), 0.0)
        inverse[base + k : base + k + 1, :] = done[0:1, :]
    if panel == BLOCK // 8 - 1:
        return
    solved = [rows[k] * over[k] for k in range(8)]
    for k in reversed(range(8)):
        for i in range(k):
            solved[i] = solved[i] - factor[i, k] * solved[k]
    for r in range(base + 8, BLOCK, 8):
        rest = m[r : r + 8, :]
        terms = [jnp.broadcast_to(rest[:, base + k : base + k + 1], wide) * solved[k] for k in range(8)]
        while len(terms) > 1:
            terms = [x + y for x, y in zip(terms[::2], terms[1::2])]
        m[r : r + 8, :] = jnp.where(within, 0.0, rest) - terms[0]


def kernel(
    kernel_hbm, start, test, cutoff, subspace, projection,
    buf, kf, khl, acc, m, inverse, loc, sib, lines, full, cloc, csib, clines, cfull, psend, precv,
    ag_recv, ag_send, k_local, k_recv, k_send, ar_recv, ar_send, cr_recv, cr_send, p_recv, p_send,
):
    row, col = lax.axis_index("row"), lax.axis_index("col")
    core = lax.rem(col, 2)
    here = (
        lax.rem(lax.div(col, 2), 2) * 2 + lax.rem(row, 2),
        lax.div(col, 4),
        lax.div(row, 2),
    )

    def device(x, y, z, c):
        return (z * 2 + lax.rem(x, 2), (y * 2 + lax.div(x, 2)) * 2 + c)

    def moved(axis, by):
        place = list(here)
        place[axis] = lax.rem(place[axis] + by, RING)
        return device(*place, core)

    sibling = device(*here, 1 - core)
    neighbours = [moved(axis, 1 if sign > 0 else RING - 1) for axis, sign in STEPS]

    barrier = pltpu.get_barrier_semaphore()
    greet = [moved(axis, by) for axis in range(3) for by in (1, 2, 3)] + [sibling]
    for other in greet:
        pl.semaphore_signal(barrier, inc=1, device_id=other, device_id_type=MESH)
    pl.semaphore_wait(barrier, len(greet))

    def remote(src, dst, send, recv, to):
        return pltpu.make_async_remote_copy(
            src_ref=src, dst_ref=dst, send_sem=send, recv_sem=recv, device_id=to, device_id_type=MESH
        )

    def block(par, s):
        return buf.at[par, pl.ds(s * BLOCK, BLOCK)]

    def forward(par, s):
        for child, label in CHILDREN[s]:
            remote(
                block(par, s), block(par, child), ag_send, ag_recv.at[par, child], neighbours[label]
            ).start()

    def arrived(par, s):
        pltpu.make_async_copy(block(par, s), block(par, s), ag_recv.at[par, s]).wait()

    def columns(s, c):
        x, y, z = [lax.rem(p + RING - d, RING) for p, d in zip(here, ORDER[s])]
        r, q = device(x, y, z, c)
        return pl.ds(pl.multiple_of((r * 16 + q) * BLOCK, BLOCK), BLOCK)

    def lanes(c):
        return pl.ds(c * CHUNK * BLOCK, CHUNK * BLOCK)

    def start_kernel_copies(s):
        c, there = s // CHUNK, pl.ds(s * BLOCK, BLOCK)
        remote(
            kernel_hbm.at[:, columns(s, 1 - core)], kf.at[pl.ds(BLOCK, BLOCK), there],
            k_send.at[c], k_recv.at[c], sibling,
        ).start()
        pltpu.make_async_copy(
            kernel_hbm.at[:, columns(s, core)], kf.at[pl.ds(0, BLOCK), there], k_local.at[c]
        ).start()

    def split_kernel(c):
        own, other = kf.at[pl.ds(0, BLOCK), lanes(c)], kf.at[pl.ds(BLOCK, BLOCK), lanes(c)]
        pltpu.make_async_copy(own, own, k_local.at[c]).wait()
        pltpu.make_async_copy(other, other, k_recv.at[c]).wait()
        value = kf[:, lanes(c)]
        high = value.astype(jnp.bfloat16)
        khl[0 : 2 * BLOCK, lanes(c)] = high
        khl[2 * BLOCK : 4 * BLOCK, lanes(c)] = (value - high.astype(jnp.float32)).astype(jnp.bfloat16)

    def multiply(par, c):
        x = buf[par, pl.ds(c * CHUNK * BLOCK, CHUNK * BLOCK), :]
        high = x.astype(jnp.bfloat16)
        low = (x - high.astype(jnp.float32)).astype(jnp.bfloat16)
        term = jnp.dot(
            khl[:, lanes(c)], jnp.concatenate([high, low], axis=1), preferred_element_type=jnp.float32
        )
        if c == 0:
            acc[...] = term
        else:
            acc[...] += term

    def sum_stages(loc, sib, lines, full, recv, send):
        kept = pl.ds(pl.multiple_of(core * HALF, HALF), HALF)
        given = pl.ds(pl.multiple_of((1 - core) * HALF, HALF), HALF)
        sent = []

        def start(src, dst, index, to):
            copy = remote(src, dst, send.at[index], recv.at[index], to)
            copy.start()
            sent.append(copy)

        def wait(ref, index):
            pltpu.make_async_copy(ref, ref, recv.at[index]).wait()

        def to_line(axis, value):
            mine = lines.at[axis, here[axis]]
            mine[...] = value
            for by in (1, 2, 3):
                start(mine, mine, 1 + 3 * axis + by - 1, moved(axis, by))

        def from_line(axis):
            for by in (1, 2, 3):
                wait(lines.at[axis, lax.rem(here[axis] + RING - by, RING)], 1 + 3 * axis + by - 1)
            return (lines[axis, 0] + lines[axis, 1]) + (lines[axis, 2] + lines[axis, 3])

        def first():
            start(loc.at[given], sib, 0, sibling)

        def second():
            wait(sib, 0)
            to_line(0, loc[kept, :] + sib[...])

        def fifth():
            full[kept, :] = from_line(2)
            start(full.at[kept], full.at[kept], 10, sibling)

        def last():
            wait(full.at[given], 10)
            for copy in sent:
                copy.wait_send()

        return [
            first, second, lambda: to_line(1, from_line(0)), lambda: to_line(2, from_line(1)), fifth, last
        ]

    def factor_panel(p):
        if p == 0:
            m[...] = full_now[0][...]
        eliminate(m, inverse, p)

    full_now = [None]

    def gather_and_multiply(par, tasks):
        forward(par, 0)
        for s in range(SLOTS):
            if s:
                arrived(par, s)
                forward(par, s)
            for task in tasks.get(s, ()):
                task()
        value = acc[...]
        value = value[:, :BLOCK] + value[:, BLOCK:]
        value = value[: 2 * BLOCK] + value[2 * BLOCK :]
        psend[...] = value[BLOCK:]
        copy = remote(psend, precv.at[par], p_send, p_recv.at[par], sibling)
        copy.start()
        whole = buf.at[par, pl.ds(BLOCK, (SLOTS - 1) * BLOCK)]
        pltpu.make_async_copy(whole, whole, ag_send).wait()
        copy.wait()
        return value[:BLOCK] + precv[par]

    def local_gram(par):
        y = buf[par, pl.ds(0, BLOCK), :]
        loc[...] = exact_dot(y.T, y)

    buf[0, pl.ds(0, BLOCK), :] = start[...]
    tasks = {}
    for s in range(SLOTS):
        tasks.setdefault((s * 2) // 5, []).append(lambda s=s: start_kernel_copies(s))
    for c in range(SLOTS // CHUNK):
        tasks.setdefault(35 + 4 * c, []).extend([lambda c=c: split_kernel(c), lambda c=c: multiply(0, c)])
    image = gather_and_multiply(0, tasks)
    buf[1, pl.ds(0, BLOCK), :] = image
    for c in range(SLOTS // CHUNK):
        given = kf.at[pl.ds(0, BLOCK), lanes(c)]
        pltpu.make_async_copy(given, given, k_send.at[c]).wait()

    def step(t, carry):
        par = lax.rem(t, 2)
        stages = sum_stages(loc, sib.at[par], lines.at[par], full.at[par], ar_recv.at[par], ar_send)
        full_now[0] = full.at[par]
        tasks = {0: [lambda: local_gram(par), stages[0]]}
        for at, stage in zip((0, 12, 26, 38, 44), stages[1:]):
            tasks.setdefault(at, []).append(stage)
        for p in range(16):
            tasks.setdefault(45 + p, []).append(lambda p=p: factor_panel(p))
        for c in range(SLOTS // CHUNK):
            tasks.setdefault((c + 1) * CHUNK - 1, []).append(lambda c=c: multiply(par, c))
        image = gather_and_multiply(par, tasks)
        buf[1 - par, pl.ds(0, BLOCK), :] = exact_dot(image, inverse[...], (((1,), (1,)), ((), ())))
        return carry

    lax.fori_loop(1, ITERATIONS, step, 0)

    par = ITERATIONS % 2
    stages = sum_stages(loc, sib.at[par], lines.at[par], full.at[par], ar_recv.at[par], ar_send)
    late = sum_stages(cloc, csib, clines, cfull, cr_recv, cr_send)
    full_now[0] = full.at[par]
    local_gram(par)
    stages[0]()
    last = buf[par, pl.ds(0, BLOCK), :]
    cloc[...] = exact_dot(last.T, test[...])
    stages[1]()
    for one, two in zip(late[:4], stages[2:]):
        one()
        two()
    for p in range(16):
        if p == 4:
            late[4]()
        if p == 8:
            late[5]()
        factor_panel(p)
    result = exact_dot(buf[par, pl.ds(0, BLOCK), :], inverse[...], (((1,), (1,)), ((), ())))
    subspace[...] = result
    keep = lax.broadcasted_iota(jnp.int32, (BLOCK, TEST), 0) < cutoff[0]
    coefficients = exact_dot(inverse[...], cfull[...]) * jnp.where(keep, 1.0, 0.0)
    projection[...] = exact_dot(result, coefficients)


def per_device(kernel_rows, start_block, test_kernel, cutoff):
    f32 = jnp.float32
    vmem = pl.BlockSpec(memory_space=pltpu.VMEM)
    dma = pltpu.SemaphoreType.DMA
    chunks = SLOTS // CHUNK
    return pl.pallas_call(
        kernel,
        out_shape=(
            jax.ShapeDtypeStruct((BLOCK, BLOCK), f32),
            jax.ShapeDtypeStruct((BLOCK, TEST), f32),
        ),
        in_specs=[pl.BlockSpec(memory_space=pl.ANY), vmem, vmem, pl.BlockSpec(memory_space=pltpu.SMEM)],
        out_specs=(vmem, vmem),
        scratch_shapes=[
            pltpu.VMEM((2, SLOTS * BLOCK, BLOCK), f32),
            pltpu.VMEM((2 * BLOCK, SLOTS * BLOCK), f32),
            pltpu.VMEM((4 * BLOCK, SLOTS * BLOCK), jnp.bfloat16),
            pltpu.VMEM((4 * BLOCK, 2 * BLOCK), f32),
            pltpu.VMEM((BLOCK, BLOCK), f32),
            pltpu.VMEM((BLOCK, BLOCK), f32),
            pltpu.VMEM((BLOCK, BLOCK), f32),
            pltpu.VMEM((2, HALF, BLOCK), f32),
            pltpu.VMEM((2, 3, RING, HALF, BLOCK), f32),
            pltpu.VMEM((2, BLOCK, BLOCK), f32),
            pltpu.VMEM((BLOCK, TEST), f32),
            pltpu.VMEM((HALF, TEST), f32),
            pltpu.VMEM((3, RING, HALF, TEST), f32),
            pltpu.VMEM((BLOCK, TEST), f32),
            pltpu.VMEM((BLOCK, BLOCK), f32),
            pltpu.VMEM((2, BLOCK, BLOCK), f32),
            dma((2, SLOTS)),
            dma,
            dma((chunks,)),
            dma((chunks,)),
            dma((chunks,)),
            dma((2, 11)),
            dma((11,)),
            dma((11,)),
            dma((11,)),
            dma((2,)),
            dma,
        ],
        compiler_params=pltpu.CompilerParams(
            collective_id=0, has_side_effects=True, vmem_limit_bytes=56 * 1024 * 1024
        ),
        cost_estimate=pl.CostEstimate(
            flops=4 * 2 * 512 * 8192 * 256, bytes_accessed=16 * 2**20, transcendentals=0
        ),
        name="iterate",
    )(kernel_rows, start_block, test_kernel, cutoff)


def solution(mesh):
    in_specs = (P(("row", "col"), None), P(("row", "col"), None), P(("row", "col"), None), P())
    out_specs = (P(("row", "col"), None), P(("row", "col"), None))
    return jax.shard_map(
        per_device, mesh=mesh, in_specs=in_specs, out_specs=out_specs, check_vma=False
    )
```

```python
import functools

import jax
import jax.numpy as jnp
from jax import lax
from jax.experimental import pallas as pl
from jax.experimental.pallas import tpu as pltpu
from jax.sharding import PartitionSpec as P

BLOCK = 128
TEST = 256
ITERATIONS = 4
RING = 4
SLOTS = RING**3
CHUNK = 8
HALF = BLOCK // 2
MESH = pl.DeviceIdType.MESH
HIGHEST = lax.Precision.HIGHEST
STEPS = [(axis, sign) for axis in range(3) for sign in (1, -1)]


TREE = (
    0, 75, 10, 96, 26, 23, 289, 51, 95, 168, 295, 32, 16, 81, 102, 307,
    122, 363, 47, 192, 58, 369, 71, 126, 199, 177, 332, 343, 41, 376, 355, 267,
    138, 208, 247, 184, 119, 314, 379, 304, 320, 191, 108, 88, 339, 216, 146, 215,
    152, 65, 162, 224, 351, 277, 329, 132, 274, 243, 230, 259, 287, 234, 256, 159,
)


def spanning_tree():
    order = [(code // 96, code // 24 % 4, code // 6 % 4) for code in TREE]
    slot = {d: s for s, d in enumerate(order)}
    children = [[] for _ in order]
    height = [0] * len(order)
    depth = lambda s: sum(min(c, RING - c) for c in order[s])
    for s in sorted(range(1, len(order)), key=depth, reverse=True):
        axis, sign = STEPS[TREE[s] % 6]
        before = list(order[s])
        before[axis] = (before[axis] - sign) % RING
        parent = slot[tuple(before)]
        children[parent].append((s, TREE[s] % 6))
        height[parent] = max(height[parent], height[s] + 1)
    for found in children:
        found.sort(key=lambda child: -height[child[0]])
    return order, children


ORDER, CHILDREN = spanning_tree()
INNER = sum(1 for found in CHILDREN if found)
GROUP = [s if s < INNER else max(INNER, s // CHUNK * CHUNK) for s in range(SLOTS)]


def exact_dot(a, b, dims=(((1,), (0,)), ((), ()))):
    return lax.dot_general(a, b, dims, precision=HIGHEST, preferred_element_type=jnp.float32)


def reciprocal(x):
    r = pl.reciprocal(x, approx=True)
    r = r * (2.0 - x * r)
    return r * (2.0 - x * r)


def eliminate(m, inverse, scale, panel):
    base = 8 * panel
    wide = (8, BLOCK)
    lane = lax.broadcasted_iota(jnp.int32, wide, 1)
    within = (lane >= base) & (lane < base + 8)
    top = m[base : base + 8, :]
    raw = [jnp.broadcast_to(top[k : k + 1, :], wide) for k in range(8)]
    a = {
        (k, i): jnp.broadcast_to(raw[k][:, base + i : base + i + 1], wide) for k in range(8) for i in range(k, 8)
    }
    rows = [jnp.where(within, jnp.where(lane == base + k, 1.0, 0.0), raw[k]) for k in range(8)]
    over, factor = {}, {}
    for k in range(0, 8, 2):
        p, q, r = a[k, k], a[k, k + 1], a[k + 1, k + 1]
        over[k] = reciprocal(p * r - q * q)
        for i in range(k + 2, 8):
            factor[k, i] = (r * a[k, i] - q * a[k + 1, i]) * over[k]
            factor[k + 1, i] = (p * a[k + 1, i] - q * a[k, i]) * over[k]
            for j in range(i, 8):
                a[i, j] = a[i, j] - (factor[k, i] * a[k, j] + factor[k + 1, i] * a[k + 1, j])
            rows[i] = rows[i] - (factor[k, i] * rows[k] + factor[k + 1, i] * rows[k + 1])
    if panel < BLOCK // 8 - 1:
        solved = [None] * 8
        for k in range(0, 8, 2):
            p, q, r = a[k, k] * over[k], a[k, k + 1] * over[k], a[k + 1, k + 1] * over[k]
            solved[k] = r * rows[k] - q * rows[k + 1]
            solved[k + 1] = p * rows[k + 1] - q * rows[k]
        for k in (6, 4, 2):
            for i in range(k):
                solved[i] = solved[i] - (factor[i, k] * solved[k] + factor[i, k + 1] * solved[k + 1])
        for r in range(base + 8, BLOCK, 8):
            rest = m[r : r + 8, :]
            terms = [jnp.broadcast_to(rest[:, base + k : base + k + 1], wide) * solved[k] for k in range(8)]
            while len(terms) > 1:
                terms = [x + y for x, y in zip(terms[::2], terms[1::2])]
            m[r : r + 8, :] = jnp.where(within, 0.0, rest) - terms[0]
    for k in range(0, 8, 2):
        p, q = a[k, k], a[k, k + 1]
        first = rows[k] * (scale[...] / jnp.sqrt(p))
        second = (rows[k + 1] - rows[k] * (q / p)) * (scale[...] * jnp.sqrt(p * over[k]))
        for j, done in ((base + k, first), (base + k + 1, second)):
            inverse[j : j + 1, :] = jnp.where(lane < base + 8, done, 0.0)[0:1, :]


def load_scaled(gram, m, scale):
    value = gram[...]
    rows = lax.broadcasted_iota(jnp.int32, value.shape, 0)
    lanes = lax.broadcasted_iota(jnp.int32, value.shape, 1)
    diagonal = jnp.sum(jnp.where(rows == lanes, value, 0.0), axis=0, keepdims=True)
    over = 1.0 / jnp.broadcast_to(jnp.sum(diagonal, axis=1, keepdims=True), (8, BLOCK))
    m[...] = value * over[0:1, :]
    scale[...] = jnp.sqrt(over)


def kernel(
    kernel_hbm, start, test, cutoff, subspace, projection,
    buf, kf, khl, acc, m, inverse, scale, loc, sib, lines, full, cloc, csib, clines, cfull, psend, precv,
    ag_recv, ag_send, k_local, k_recv, k_send, ar_recv, ar_send, cr_recv, cr_send, p_recv, p_send,
):
    row, col = lax.axis_index("row"), lax.axis_index("col")
    core = lax.rem(col, 2)
    here = (
        lax.rem(lax.div(col, 2), 2) * 2 + lax.rem(row, 2),
        lax.div(col, 4),
        lax.div(row, 2),
    )

    def device(x, y, z, c):
        return (z * 2 + lax.rem(x, 2), (y * 2 + lax.div(x, 2)) * 2 + c)

    def moved(axis, by):
        place = list(here)
        place[axis] = lax.rem(place[axis] + by, RING)
        return device(*place, core)

    sibling = device(*here, 1 - core)
    neighbours = [moved(axis, 1 if sign > 0 else RING - 1) for axis, sign in STEPS]

    barrier = pltpu.get_barrier_semaphore()
    greet = [moved(axis, by) for axis in range(3) for by in (1, 2, 3)] + [sibling]
    for other in greet:
        pl.semaphore_signal(barrier, inc=1, device_id=other, device_id_type=MESH)
    pl.semaphore_wait(barrier, len(greet))

    def remote(src, dst, send, recv, to):
        return pltpu.make_async_remote_copy(
            src_ref=src, dst_ref=dst, send_sem=send, recv_sem=recv, device_id=to, device_id_type=MESH
        )

    def block(par, s, count=1):
        return buf.at[par, pl.ds(s * BLOCK, count * BLOCK)]

    def forward(par, s):
        for child, label in CHILDREN[s]:
            remote(
                block(par, s), block(par, child), ag_send, ag_recv.at[par, GROUP[child]], neighbours[label]
            ).start()

    def arrived(par, group):
        whole = block(par, group, GROUP.count(group))
        pltpu.make_async_copy(whole, whole, ag_recv.at[par, group]).wait()

    def columns(s, c):
        x, y, z = [lax.rem(p + RING - d, RING) for p, d in zip(here, ORDER[s])]
        r, q = device(x, y, z, c)
        return pl.ds(pl.multiple_of((r * 16 + q) * BLOCK, BLOCK), BLOCK)

    def lanes(c):
        return pl.ds(c * CHUNK * BLOCK, CHUNK * BLOCK)

    def start_kernel_copies(s):
        c, there = s // CHUNK, pl.ds(s * BLOCK, BLOCK)
        remote(
            kernel_hbm.at[:, columns(s, 1 - core)], kf.at[pl.ds(BLOCK, BLOCK), there],
            k_send.at[c], k_recv.at[c], sibling,
        ).start()
        pltpu.make_async_copy(
            kernel_hbm.at[:, columns(s, core)], kf.at[pl.ds(0, BLOCK), there], k_local.at[c]
        ).start()

    def split_kernel(c):
        own, other = kf.at[pl.ds(0, BLOCK), lanes(c)], kf.at[pl.ds(BLOCK, BLOCK), lanes(c)]
        pltpu.make_async_copy(own, own, k_local.at[c]).wait()
        pltpu.make_async_copy(other, other, k_recv.at[c]).wait()
        value = kf[:, lanes(c)]
        high = value.astype(jnp.bfloat16)
        khl[0 : 2 * BLOCK, lanes(c)] = high
        khl[2 * BLOCK : 4 * BLOCK, lanes(c)] = (value - high.astype(jnp.float32)).astype(jnp.bfloat16)

    def multiply(par, c):
        for group in sorted(set(GROUP[c * CHUNK : (c + 1) * CHUNK])):
            if group >= INNER:
                arrived(par, group)
        x = buf[par, pl.ds(c * CHUNK * BLOCK, CHUNK * BLOCK), :]
        high = x.astype(jnp.bfloat16)
        low = (x - high.astype(jnp.float32)).astype(jnp.bfloat16)
        term = jnp.dot(
            khl[:, lanes(c)], jnp.concatenate([high, low], axis=1), preferred_element_type=jnp.float32
        )
        if c == 0:
            acc[...] = term
        else:
            acc[...] += term

    def sum_stages(loc, sib, lines, full, recv, send):
        kept = pl.ds(pl.multiple_of(core * HALF, HALF), HALF)
        given = pl.ds(pl.multiple_of((1 - core) * HALF, HALF), HALF)
        sent = []

        def start(src, dst, index, to):
            copy = remote(src, dst, send.at[index], recv.at[index], to)
            copy.start()
            sent.append(copy)

        def wait(ref, index):
            pltpu.make_async_copy(ref, ref, recv.at[index]).wait()

        def to_line(axis, value):
            mine = lines.at[axis, here[axis]]
            mine[...] = value
            for by in (1, 2, 3):
                start(mine, mine, 1 + 3 * axis + by - 1, moved(axis, by))

        def from_line(axis):
            for by in (1, 2, 3):
                wait(lines.at[axis, lax.rem(here[axis] + RING - by, RING)], 1 + 3 * axis + by - 1)
            return (lines[axis, 0] + lines[axis, 1]) + (lines[axis, 2] + lines[axis, 3])

        def first():
            start(loc.at[given], sib, 0, sibling)

        def second():
            wait(sib, 0)
            to_line(0, loc[kept, :] + sib[...])

        def fifth():
            full[kept, :] = from_line(2)
            start(full.at[kept], full.at[kept], 10, sibling)

        def last():
            wait(full.at[given], 10)
            for copy in sent:
                copy.wait_send()

        return [
            first, second, lambda: to_line(1, from_line(0)), lambda: to_line(2, from_line(1)), fifth, last
        ]

    def factor_panel(p):
        if p == 0:
            load_scaled(full_now[0], m, scale)
        eliminate(m, inverse, scale, p)

    full_now = [None]

    def gather_and_multiply(par, tasks, work, beside):
        forward(par, 0)
        for s in range(INNER):
            if s:
                arrived(par, s)
                forward(par, s)
            for task in tasks.get(s, ()):
                task()
        for task in work:
            task()
        value = acc[...]
        value = value[:, :BLOCK] + value[:, BLOCK:]
        value = value[: 2 * BLOCK] + value[2 * BLOCK :]
        psend[...] = value[BLOCK:]
        copy = remote(psend, precv.at[par], p_send, p_recv.at[par], sibling)
        copy.start()
        for task in beside:
            task()
        whole = block(par, 1, SLOTS - 1)
        pltpu.make_async_copy(whole, whole, ag_send).wait()
        copy.wait()
        return value[:BLOCK] + precv[par]

    def local_gram(par):
        y = buf[par, pl.ds(0, BLOCK), :]
        loc[...] = exact_dot(y.T, y)

    buf[0, pl.ds(0, BLOCK), :] = start[...]
    tasks = {}
    for s in range(SLOTS):
        tasks.setdefault((s * 2) // 5, []).append(lambda s=s: start_kernel_copies(s))
    work = []
    for c in range(SLOTS // CHUNK):
        into = tasks.setdefault((26, 28, 31, 33)[c], []) if c < 4 else work
        into += [lambda c=c: split_kernel(c), lambda c=c: multiply(0, c)]
    image = gather_and_multiply(0, tasks, work, [])
    buf[1, pl.ds(0, BLOCK), :] = image
    for c in range(SLOTS // CHUNK):
        given = kf.at[pl.ds(0, BLOCK), lanes(c)]
        pltpu.make_async_copy(given, given, k_send.at[c]).wait()

    def step(t, carry):
        par = lax.rem(t, 2)
        stages = sum_stages(loc, sib.at[par], lines.at[par], full.at[par], ar_recv.at[par], ar_send)
        full_now[0] = full.at[par]
        tasks = {0: [lambda: local_gram(par), stages[0]]}
        for at, stage in zip((0, 6, 20, 35), stages[1:5]):
            tasks.setdefault(at, []).append(stage)
        product = [lambda c=c: multiply(par, c) for c in range(SLOTS // CHUNK)]
        panel = [lambda p=p: factor_panel(p) for p in range(16)]
        for at, c in ((20, 0), (26, 1), (33, 2)):
            tasks.setdefault(at, []).append(product[c])
        work = [product[3], product[4], stages[5]]
        work += panel[0:4] + [product[5]] + panel[4:8] + [product[6]] + panel[8:12] + [product[7]]
        image = gather_and_multiply(par, tasks, work, panel[12:])
        buf[1 - par, pl.ds(0, BLOCK), :] = exact_dot(image, inverse[...], (((1,), (1,)), ((), ())))
        return carry

    lax.fori_loop(1, ITERATIONS, step, 0)

    par = ITERATIONS % 2
    stages = sum_stages(loc, sib.at[par], lines.at[par], full.at[par], ar_recv.at[par], ar_send)
    late = sum_stages(cloc, csib, clines, cfull, cr_recv, cr_send)
    full_now[0] = full.at[par]
    local_gram(par)
    stages[0]()
    last = buf[par, pl.ds(0, BLOCK), :]
    cloc[...] = exact_dot(last.T, test[...])
    stages[1]()
    for one, two in zip(late[:4], stages[2:]):
        one()
        two()
    for p in range(16):
        if p == 4:
            late[4]()
        if p == 8:
            late[5]()
        factor_panel(p)
    result = exact_dot(buf[par, pl.ds(0, BLOCK), :], inverse[...], (((1,), (1,)), ((), ())))
    subspace[...] = result
    keep = lax.broadcasted_iota(jnp.int32, (BLOCK, TEST), 0) < cutoff[0]
    coefficients = exact_dot(inverse[...], cfull[...]) * jnp.where(keep, 1.0, 0.0)
    projection[...] = exact_dot(result, coefficients)


def per_device(kernel_rows, start_block, test_kernel, cutoff):
    f32 = jnp.float32
    vmem = pl.BlockSpec(memory_space=pltpu.VMEM)
    dma = pltpu.SemaphoreType.DMA
    chunks = SLOTS // CHUNK
    return pl.pallas_call(
        kernel,
        out_shape=(
            jax.ShapeDtypeStruct((BLOCK, BLOCK), f32),
            jax.ShapeDtypeStruct((BLOCK, TEST), f32),
        ),
        in_specs=[pl.BlockSpec(memory_space=pl.ANY), vmem, vmem, pl.BlockSpec(memory_space=pltpu.SMEM)],
        out_specs=(vmem, vmem),
        scratch_shapes=[
            pltpu.VMEM((2, SLOTS * BLOCK, BLOCK), f32),
            pltpu.VMEM((2 * BLOCK, SLOTS * BLOCK), f32),
            pltpu.VMEM((4 * BLOCK, SLOTS * BLOCK), jnp.bfloat16),
            pltpu.VMEM((4 * BLOCK, 2 * BLOCK), f32),
            pltpu.VMEM((BLOCK, BLOCK), f32),
            pltpu.VMEM((BLOCK, BLOCK), f32),
            pltpu.VMEM((8, BLOCK), f32),
            pltpu.VMEM((BLOCK, BLOCK), f32),
            pltpu.VMEM((2, HALF, BLOCK), f32),
            pltpu.VMEM((2, 3, RING, HALF, BLOCK), f32),
            pltpu.VMEM((2, BLOCK, BLOCK), f32),
            pltpu.VMEM((BLOCK, TEST), f32),
            pltpu.VMEM((HALF, TEST), f32),
            pltpu.VMEM((3, RING, HALF, TEST), f32),
            pltpu.VMEM((BLOCK, TEST), f32),
            pltpu.VMEM((BLOCK, BLOCK), f32),
            pltpu.VMEM((2, BLOCK, BLOCK), f32),
            dma((2, SLOTS)),
            dma,
            dma((chunks,)),
            dma((chunks,)),
            dma((chunks,)),
            dma((2, 11)),
            dma((11,)),
            dma((11,)),
            dma((11,)),
            dma((2,)),
            dma,
        ],
        compiler_params=pltpu.CompilerParams(
            collective_id=0, has_side_effects=True, vmem_limit_bytes=56 * 1024 * 1024
        ),
        cost_estimate=pl.CostEstimate(
            flops=4 * 2 * 512 * 8192 * 256, bytes_accessed=16 * 2**20, transcendentals=0
        ),
        name="iterate",
    )(kernel_rows, start_block, test_kernel, cutoff)


def solution(mesh):
    in_specs = (P(("row", "col"), None), P(("row", "col"), None), P(("row", "col"), None), P())
    out_specs = (P(("row", "col"), None), P(("row", "col"), None))
    return jax.shard_map(
        per_device, mesh=mesh, in_specs=in_specs, out_specs=out_specs, check_vma=False
    )
```

```python
import functools

import jax
import jax.numpy as jnp
from jax import lax
from jax.experimental import pallas as pl
from jax.experimental.pallas import tpu as pltpu
from jax.sharding import PartitionSpec as P

BLOCK = 128
TEST = 256
ITERATIONS = 4
RING = 4
SLOTS = RING**3
CHUNK = 8
HALF = BLOCK // 2
GROUPED = 32
MESH = pl.DeviceIdType.MESH
HIGHEST = lax.Precision.HIGHEST
STEPS = [(axis, sign) for axis in range(3) for sign in (1, -1)]


TREE = (
    0, 75, 10, 96, 26, 23, 289, 51, 95, 168, 295, 32, 16, 81, 102, 307,
    122, 363, 47, 192, 58, 369, 71, 126, 199, 177, 332, 343, 41, 376, 355, 267,
    138, 208, 247, 184, 119, 314, 379, 304, 320, 191, 108, 88, 339, 216, 146, 215,
    152, 65, 162, 224, 351, 277, 329, 132, 274, 243, 230, 259, 287, 234, 256, 159,
)


def spanning_tree():
    order = [(code // 96, code // 24 % 4, code // 6 % 4) for code in TREE]
    slot = {d: s for s, d in enumerate(order)}
    children = [[] for _ in order]
    height = [0] * len(order)
    depth = lambda s: sum(min(c, RING - c) for c in order[s])
    for s in sorted(range(1, len(order)), key=depth, reverse=True):
        axis, sign = STEPS[TREE[s] % 6]
        before = list(order[s])
        before[axis] = (before[axis] - sign) % RING
        parent = slot[tuple(before)]
        children[parent].append((s, TREE[s] % 6))
        height[parent] = max(height[parent], height[s] + 1)
    for found in children:
        found.sort(key=lambda child: -height[child[0]])
    return order, children


ORDER, CHILDREN = spanning_tree()
INNER = sum(1 for found in CHILDREN if found)
GROUP = [s if s < INNER else max(INNER, s // CHUNK * CHUNK) for s in range(SLOTS)]


def exact_dot(a, b, dims=(((1,), (0,)), ((), ()))):
    return lax.dot_general(a, b, dims, precision=HIGHEST, preferred_element_type=jnp.float32)


def reciprocal(x):
    r = pl.reciprocal(x, approx=True)
    r = r * (2.0 - x * r)
    return r * (2.0 - x * r)


def eliminate(m, inverse, scale, scaled, panel):
    base = 8 * panel
    end = base // GROUPED * GROUPED + GROUPED
    wide = (8, BLOCK)
    lane = lax.broadcasted_iota(jnp.int32, wide, 1)
    within = (lane >= base) & (lane < base + 8)
    top = m[base : base + 8, :]
    raw = [jnp.broadcast_to(top[k : k + 1, :], wide) for k in range(8)]
    a = {
        (k, i): jnp.broadcast_to(raw[k][:, base + i : base + i + 1], wide) for k in range(8) for i in range(k, 8)
    }
    rows = [jnp.where(within, jnp.where(lane == base + k, 1.0, 0.0), raw[k]) for k in range(8)]
    over, factor = {}, {}
    for k in range(0, 8, 2):
        p, q, r = a[k, k], a[k, k + 1], a[k + 1, k + 1]
        over[k] = reciprocal(p * r - q * q)
        for i in range(k + 2, 8):
            factor[k, i] = (r * a[k, i] - q * a[k + 1, i]) * over[k]
            factor[k + 1, i] = (p * a[k + 1, i] - q * a[k, i]) * over[k]
            for j in range(i, 8):
                a[i, j] = a[i, j] - (factor[k, i] * a[k, j] + factor[k + 1, i] * a[k + 1, j])
            rows[i] = rows[i] - (factor[k, i] * rows[k] + factor[k + 1, i] * rows[k + 1])
    if base + 8 < end:
        solved = [None] * 8
        for k in range(0, 8, 2):
            p, q, r = a[k, k] * over[k], a[k, k + 1] * over[k], a[k + 1, k + 1] * over[k]
            solved[k] = r * rows[k] - q * rows[k + 1]
            solved[k + 1] = p * rows[k + 1] - q * rows[k]
        for k in (6, 4, 2):
            for i in range(k):
                solved[i] = solved[i] - (factor[i, k] * solved[k] + factor[i, k + 1] * solved[k + 1])
        for r in range(base + 8, end, 8):
            rest = m[r : r + 8, :]
            terms = [jnp.broadcast_to(rest[:, base + k : base + k + 1], wide) * solved[k] for k in range(8)]
            while len(terms) > 1:
                terms = [x + y for x, y in zip(terms[::2], terms[1::2])]
            m[r : r + 8, :] = jnp.where(within, 0.0, rest) - terms[0]
    for k in range(0, 8, 2):
        p, q = a[k, k], a[k, k + 1]
        first = rows[k] * (1.0 / jnp.sqrt(p))
        second = (rows[k + 1] - rows[k] * (q / p)) * jnp.sqrt(p * over[k])
        for j, done in ((base + k, first), (base + k + 1, second)):
            inverse[j : j + 1, :] = jnp.where(lane < base + 8, done * scale[...], 0.0)[0:1, :]
            if end < BLOCK:
                kept = (lane < base + 8) | (lane >= end)
                scaled[j % GROUPED : j % GROUPED + 1, :] = jnp.where(kept, done, 0.0)[0:1, :]
    if base + 8 == end and end < BLOCK:
        done = scaled[...]
        lanes = lax.broadcasted_iota(jnp.int32, (BLOCK - end, BLOCK), 1)
        rest = jnp.where((lanes >= end - GROUPED) & (lanes < end), 0.0, m[end:, :])
        m[end:, :] = rest - exact_dot(done.T[end:, :], done)


def load_scaled(gram, m, scale):
    value = gram[...]
    rows = lax.broadcasted_iota(jnp.int32, value.shape, 0)
    lanes = lax.broadcasted_iota(jnp.int32, value.shape, 1)
    diagonal = jnp.sum(jnp.where(rows == lanes, value, 0.0), axis=0, keepdims=True)
    over = 1.0 / jnp.broadcast_to(jnp.sum(diagonal, axis=1, keepdims=True), (8, BLOCK))
    m[...] = value * over[0:1, :]
    scale[...] = jnp.sqrt(over)


def kernel(
    kernel_hbm, start, test, cutoff, image_out, inverse, kept_out,
    buf, kf, khl, acc, m, scale, scaled, loc, sib, lines, full, cloc, csib, clines, cfull, psend, precv,
    ag_recv, ag_send, k_local, k_recv, k_send, ar_recv, ar_send, cr_recv, cr_send, p_recv, p_send,
):
    row, col = lax.axis_index("row"), lax.axis_index("col")
    core = lax.rem(col, 2)
    here = (
        lax.rem(lax.div(col, 2), 2) * 2 + lax.rem(row, 2),
        lax.div(col, 4),
        lax.div(row, 2),
    )

    def device(x, y, z, c):
        return (z * 2 + lax.rem(x, 2), (y * 2 + lax.div(x, 2)) * 2 + c)

    def moved(axis, by):
        place = list(here)
        place[axis] = lax.rem(place[axis] + by, RING)
        return device(*place, core)

    sibling = device(*here, 1 - core)
    neighbours = [moved(axis, 1 if sign > 0 else RING - 1) for axis, sign in STEPS]

    barrier = pltpu.get_barrier_semaphore()
    greet = [moved(axis, by) for axis in range(3) for by in (1, 2, 3)] + [sibling]
    for other in greet:
        pl.semaphore_signal(barrier, inc=1, device_id=other, device_id_type=MESH)
    pl.semaphore_wait(barrier, len(greet))

    def remote(src, dst, send, recv, to):
        return pltpu.make_async_remote_copy(
            src_ref=src, dst_ref=dst, send_sem=send, recv_sem=recv, device_id=to, device_id_type=MESH
        )

    def block(par, s, count=1):
        return buf.at[par, pl.ds(s * BLOCK, count * BLOCK)]

    def forward(par, s):
        for child, label in CHILDREN[s]:
            remote(
                block(par, s), block(par, child), ag_send, ag_recv.at[par, GROUP[child]], neighbours[label]
            ).start()

    def arrived(par, group):
        whole = block(par, group, GROUP.count(group))
        pltpu.make_async_copy(whole, whole, ag_recv.at[par, group]).wait()

    def columns(s, c):
        x, y, z = [lax.rem(p + RING - d, RING) for p, d in zip(here, ORDER[s])]
        r, q = device(x, y, z, c)
        return pl.ds(pl.multiple_of((r * 16 + q) * BLOCK, BLOCK), BLOCK)

    def lanes(c):
        return pl.ds(c * CHUNK * BLOCK, CHUNK * BLOCK)

    def start_kernel_copies(s):
        c, there = s // CHUNK, pl.ds(s * BLOCK, BLOCK)
        remote(
            kernel_hbm.at[:, columns(s, 1 - core)], kf.at[pl.ds(BLOCK, BLOCK), there],
            k_send.at[c], k_recv.at[c], sibling,
        ).start()
        pltpu.make_async_copy(
            kernel_hbm.at[:, columns(s, core)], kf.at[pl.ds(0, BLOCK), there], k_local.at[c]
        ).start()

    def split_kernel(c):
        own, other = kf.at[pl.ds(0, BLOCK), lanes(c)], kf.at[pl.ds(BLOCK, BLOCK), lanes(c)]
        pltpu.make_async_copy(own, own, k_local.at[c]).wait()
        pltpu.make_async_copy(other, other, k_recv.at[c]).wait()
        value = kf[:, lanes(c)]
        high = value.astype(jnp.bfloat16)
        khl[0 : 2 * BLOCK, lanes(c)] = high
        khl[2 * BLOCK : 4 * BLOCK, lanes(c)] = (value - high.astype(jnp.float32)).astype(jnp.bfloat16)

    def multiply(par, c):
        for group in sorted(set(GROUP[c * CHUNK : (c + 1) * CHUNK])):
            if group >= INNER:
                arrived(par, group)
        x = buf[par, pl.ds(c * CHUNK * BLOCK, CHUNK * BLOCK), :]
        high = x.astype(jnp.bfloat16)
        low = (x - high.astype(jnp.float32)).astype(jnp.bfloat16)
        term = jnp.dot(
            khl[:, lanes(c)], jnp.concatenate([high, low], axis=1), preferred_element_type=jnp.float32
        )
        if c == 0:
            acc[...] = term
        else:
            acc[...] += term

    def sum_stages(loc, sib, lines, full, recv, send):
        kept = pl.ds(pl.multiple_of(core * HALF, HALF), HALF)
        given = pl.ds(pl.multiple_of((1 - core) * HALF, HALF), HALF)
        sent = []

        def start(src, dst, index, to):
            copy = remote(src, dst, send.at[index], recv.at[index], to)
            copy.start()
            sent.append(copy)

        def wait(ref, index):
            pltpu.make_async_copy(ref, ref, recv.at[index]).wait()

        def to_line(axis, value):
            mine = lines.at[axis, here[axis]]
            mine[...] = value
            for by in (1, 2, 3):
                start(mine, mine, 1 + 3 * axis + by - 1, moved(axis, by))

        def from_line(axis):
            for by in (1, 2, 3):
                wait(lines.at[axis, lax.rem(here[axis] + RING - by, RING)], 1 + 3 * axis + by - 1)
            return (lines[axis, 0] + lines[axis, 1]) + (lines[axis, 2] + lines[axis, 3])

        def first():
            start(loc.at[given], sib, 0, sibling)

        def second():
            wait(sib, 0)
            to_line(0, loc[kept, :] + sib[...])

        def fifth():
            full[kept, :] = from_line(2)
            start(full.at[kept], full.at[kept], 10, sibling)

        def last():
            wait(full.at[given], 10)
            for copy in sent:
                copy.wait_send()

        return [
            first, second, lambda: to_line(1, from_line(0)), lambda: to_line(2, from_line(1)), fifth, last
        ]

    def factor_panel(p):
        if p == 0:
            load_scaled(full_now[0], m, scale)
        eliminate(m, inverse, scale, scaled, p)

    full_now = [None]

    def gather_and_multiply(par, tasks, work, beside):
        forward(par, 0)
        for s in range(INNER):
            if s:
                arrived(par, s)
                forward(par, s)
            for task in tasks.get(s, ()):
                task()
        for task in work:
            task()
        value = acc[...]
        value = value[:, :BLOCK] + value[:, BLOCK:]
        value = value[: 2 * BLOCK] + value[2 * BLOCK :]
        psend[...] = value[BLOCK:]
        copy = remote(psend, precv.at[par], p_send, p_recv.at[par], sibling)
        copy.start()
        for task in beside:
            task()
        whole = block(par, 1, SLOTS - 1)
        pltpu.make_async_copy(whole, whole, ag_send).wait()
        copy.wait()
        return value[:BLOCK] + precv[par]

    def local_gram(par):
        y = buf[par, pl.ds(0, BLOCK), :]
        loc[...] = exact_dot(y.T, y)

    buf[0, pl.ds(0, BLOCK), :] = start[...]
    tasks = {}
    for s in range(SLOTS):
        tasks.setdefault((s * 2) // 5, []).append(lambda s=s: start_kernel_copies(s))
    work = []
    for c in range(SLOTS // CHUNK):
        into = tasks.setdefault((26, 28, 31, 33)[c], []) if c < 4 else work
        into += [lambda c=c: split_kernel(c), lambda c=c: multiply(0, c)]
    image = gather_and_multiply(0, tasks, work, [])
    buf[1, pl.ds(0, BLOCK), :] = image
    for c in range(SLOTS // CHUNK):
        given = kf.at[pl.ds(0, BLOCK), lanes(c)]
        pltpu.make_async_copy(given, given, k_send.at[c]).wait()

    def step(t, carry):
        par = lax.rem(t, 2)
        stages = sum_stages(loc, sib.at[par], lines.at[par], full.at[par], ar_recv.at[par], ar_send)
        full_now[0] = full.at[par]
        tasks = {0: [lambda: local_gram(par), stages[0]]}
        for at, stage in zip((0, 6, 20, 35), stages[1:5]):
            tasks.setdefault(at, []).append(stage)
        product = [lambda c=c: multiply(par, c) for c in range(SLOTS // CHUNK)]
        panel = [lambda p=p: factor_panel(p) for p in range(16)]
        for at, c in ((20, 0), (26, 1), (33, 2)):
            tasks.setdefault(at, []).append(product[c])
        work = [product[3], product[4], stages[5]]
        work += panel[0:4] + [product[5]] + panel[4:8] + [product[6]] + panel[8:12] + [product[7]]
        image = gather_and_multiply(par, tasks, work, panel[12:])
        buf[1 - par, pl.ds(0, BLOCK), :] = exact_dot(image, inverse[...], (((1,), (1,)), ((), ())))
        return carry

    lax.fori_loop(1, ITERATIONS, step, 0)

    par = ITERATIONS % 2
    stages = sum_stages(loc, sib.at[par], lines.at[par], full.at[par], ar_recv.at[par], ar_send)
    late = sum_stages(cloc, csib, clines, cfull, cr_recv, cr_send)
    full_now[0] = full.at[par]
    local_gram(par)
    stages[0]()
    last = buf[par, pl.ds(0, BLOCK), :]
    cloc[...] = exact_dot(last.T, test[...])
    stages[1]()
    for one, two in zip(late[:4], stages[2:]):
        one()
        two()
    for p in range(16):
        if p == 4:
            late[4]()
        if p == 8:
            late[5]()
        factor_panel(p)
    image_out[...] = buf[par, pl.ds(0, BLOCK), :]
    keep = lax.broadcasted_iota(jnp.int32, (BLOCK, TEST), 0) < cutoff[0]
    kept_out[...] = exact_dot(inverse[...], cfull[...]) * jnp.where(keep, 1.0, 0.0)


def project(image, inverse, kept, subspace, projection):
    block = exact_dot(image[...], inverse[...], (((1,), (1,)), ((), ())))
    subspace[...] = block
    projection[...] = exact_dot(block, kept[...])


def per_device(kernel_rows, start_block, test_kernel, cutoff):
    f32 = jnp.float32
    vmem = pl.BlockSpec(memory_space=pltpu.VMEM)
    dma = pltpu.SemaphoreType.DMA
    chunks = SLOTS // CHUNK
    narrow = jax.ShapeDtypeStruct((BLOCK, BLOCK), f32)
    broad = jax.ShapeDtypeStruct((BLOCK, TEST), f32)
    image, inverse, kept = pl.pallas_call(
        kernel,
        out_shape=(narrow, narrow, broad),
        in_specs=[pl.BlockSpec(memory_space=pl.ANY), vmem, vmem, pl.BlockSpec(memory_space=pltpu.SMEM)],
        out_specs=(vmem, vmem, vmem),
        scratch_shapes=[
            pltpu.VMEM((2, SLOTS * BLOCK, BLOCK), f32),
            pltpu.VMEM((2 * BLOCK, SLOTS * BLOCK), f32),
            pltpu.VMEM((4 * BLOCK, SLOTS * BLOCK), jnp.bfloat16),
            pltpu.VMEM((4 * BLOCK, 2 * BLOCK), f32),
            pltpu.VMEM((BLOCK, BLOCK), f32),
            pltpu.VMEM((8, BLOCK), f32),
            pltpu.VMEM((GROUPED, BLOCK), f32),
            pltpu.VMEM((BLOCK, BLOCK), f32),
            pltpu.VMEM((2, HALF, BLOCK), f32),
            pltpu.VMEM((2, 3, RING, HALF, BLOCK), f32),
            pltpu.VMEM((2, BLOCK, BLOCK), f32),
            pltpu.VMEM((BLOCK, TEST), f32),
            pltpu.VMEM((HALF, TEST), f32),
            pltpu.VMEM((3, RING, HALF, TEST), f32),
            pltpu.VMEM((BLOCK, TEST), f32),
            pltpu.VMEM((BLOCK, BLOCK), f32),
            pltpu.VMEM((2, BLOCK, BLOCK), f32),
            dma((2, SLOTS)),
            dma,
            dma((chunks,)),
            dma((chunks,)),
            dma((chunks,)),
            dma((2, 11)),
            dma((11,)),
            dma((11,)),
            dma((11,)),
            dma((2,)),
            dma,
        ],
        compiler_params=pltpu.CompilerParams(
            collective_id=0, has_side_effects=True, vmem_limit_bytes=56 * 1024 * 1024
        ),
        cost_estimate=pl.CostEstimate(
            flops=4 * 2 * 512 * 8192 * 256, bytes_accessed=16 * 2**20, transcendentals=0
        ),
        name="iterate",
    )(kernel_rows, start_block, test_kernel, cutoff)
    return pl.pallas_call(project, out_shape=(narrow, broad), name="project")(image, inverse, kept)


def solution(mesh):
    in_specs = (P(("row", "col"), None), P(("row", "col"), None), P(("row", "col"), None), P())
    out_specs = (P(("row", "col"), None), P(("row", "col"), None))
    return jax.shard_map(
        per_device, mesh=mesh, in_specs=in_specs, out_specs=out_specs, check_vma=False
    )
```

```python
import functools

import jax
import jax.numpy as jnp
from jax import lax
from jax.experimental import pallas as pl
from jax.experimental.pallas import tpu as pltpu
from jax.sharding import PartitionSpec as P

BLOCK = 128
TEST = 256
ITERATIONS = 4
RING = 4
SLOTS = RING**3
CHUNK = 8
HALF = BLOCK // 2
GROUPED = BLOCK
MESH = pl.DeviceIdType.MESH
HIGHEST = lax.Precision.HIGHEST
STEPS = [(axis, sign) for axis in range(3) for sign in (1, -1)]


TREE = (
    0, 75, 10, 96, 26, 23, 289, 51, 95, 168, 295, 32, 16, 81, 102, 307,
    122, 363, 47, 192, 58, 369, 71, 126, 199, 177, 332, 343, 41, 376, 355, 267,
    138, 208, 247, 184, 119, 314, 379, 304, 320, 191, 108, 88, 339, 216, 146, 215,
    152, 65, 162, 224, 351, 277, 329, 132, 274, 243, 230, 259, 287, 234, 256, 159,
)


def spanning_tree():
    order = [(code // 96, code // 24 % 4, code // 6 % 4) for code in TREE]
    slot = {d: s for s, d in enumerate(order)}
    children = [[] for _ in order]
    height = [0] * len(order)
    depth = lambda s: sum(min(c, RING - c) for c in order[s])
    for s in sorted(range(1, len(order)), key=depth, reverse=True):
        axis, sign = STEPS[TREE[s] % 6]
        before = list(order[s])
        before[axis] = (before[axis] - sign) % RING
        parent = slot[tuple(before)]
        children[parent].append((s, TREE[s] % 6))
        height[parent] = max(height[parent], height[s] + 1)
    for found in children:
        found.sort(key=lambda child: -height[child[0]])
    return order, children


ORDER, CHILDREN = spanning_tree()
INNER = sum(1 for found in CHILDREN if found)
GROUP = [s if s < INNER else max(INNER, s // CHUNK * CHUNK) for s in range(SLOTS)]


def exact_dot(a, b, dims=(((1,), (0,)), ((), ()))):
    return lax.dot_general(a, b, dims, precision=HIGHEST, preferred_element_type=jnp.float32)


def reciprocal(x):
    r = pl.reciprocal(x, approx=True)
    r = r * (2.0 - x * r)
    return r * (2.0 - x * r)


def eliminate(m, inverse, scale, scaled, panel):
    base = 8 * panel
    end = base // GROUPED * GROUPED + GROUPED
    wide = (8, BLOCK)
    lane = lax.broadcasted_iota(jnp.int32, wide, 1)
    within = (lane >= base) & (lane < base + 8)
    top = m[base : base + 8, :]
    raw = [jnp.broadcast_to(top[k : k + 1, :], wide) for k in range(8)]
    a = {
        (k, i): jnp.broadcast_to(raw[k][:, base + i : base + i + 1], wide) for k in range(8) for i in range(k, 8)
    }
    rows = [jnp.where(within, jnp.where(lane == base + k, 1.0, 0.0), raw[k]) for k in range(8)]
    over, factor = {}, {}
    for k in range(0, 8, 2):
        p, q, r = a[k, k], a[k, k + 1], a[k + 1, k + 1]
        over[k] = reciprocal(p * r - q * q)
        for i in range(k + 2, 8):
            factor[k, i] = (r * a[k, i] - q * a[k + 1, i]) * over[k]
            factor[k + 1, i] = (p * a[k + 1, i] - q * a[k, i]) * over[k]
            for j in range(i, 8):
                a[i, j] = a[i, j] - (factor[k, i] * a[k, j] + factor[k + 1, i] * a[k + 1, j])
            rows[i] = rows[i] - (factor[k, i] * rows[k] + factor[k + 1, i] * rows[k + 1])
    if base + 8 < end:
        solved = [None] * 8
        for k in range(0, 8, 2):
            p, q, r = a[k, k] * over[k], a[k, k + 1] * over[k], a[k + 1, k + 1] * over[k]
            solved[k] = r * rows[k] - q * rows[k + 1]
            solved[k + 1] = p * rows[k + 1] - q * rows[k]
        for k in (6, 4, 2):
            for i in range(k):
                solved[i] = solved[i] - (factor[i, k] * solved[k] + factor[i, k + 1] * solved[k + 1])
        for r in range(base + 8, end, 8):
            rest = m[r : r + 8, :]
            terms = [jnp.broadcast_to(rest[:, base + k : base + k + 1], wide) * solved[k] for k in range(8)]
            while len(terms) > 1:
                terms = [x + y for x, y in zip(terms[::2], terms[1::2])]
            m[r : r + 8, :] = jnp.where(within, 0.0, rest) - terms[0]
    for k in range(0, 8, 2):
        p, q = a[k, k], a[k, k + 1]
        first = rows[k] * (1.0 / jnp.sqrt(p))
        second = (rows[k + 1] - rows[k] * (q / p)) * jnp.sqrt(p * over[k])
        for j, done in ((base + k, first), (base + k + 1, second)):
            inverse[j : j + 1, :] = jnp.where(lane < base + 8, done * scale[...], 0.0)[0:1, :]
            if end < BLOCK:
                kept = (lane < base + 8) | (lane >= end)
                scaled[j % GROUPED : j % GROUPED + 1, :] = jnp.where(kept, done, 0.0)[0:1, :]
    if base + 8 == end and end < BLOCK:
        done = scaled[...]
        lanes = lax.broadcasted_iota(jnp.int32, (BLOCK - end, BLOCK), 1)
        rest = jnp.where((lanes >= end - GROUPED) & (lanes < end), 0.0, m[end:, :])
        m[end:, :] = rest - exact_dot(done.T[end:, :], done)


def load_scaled(gram, m, scale):
    value = gram[...]
    rows = lax.broadcasted_iota(jnp.int32, value.shape, 0)
    lanes = lax.broadcasted_iota(jnp.int32, value.shape, 1)
    diagonal = jnp.sum(jnp.where(rows == lanes, value, 0.0), axis=0, keepdims=True)
    over = 1.0 / jnp.broadcast_to(jnp.sum(diagonal, axis=1, keepdims=True), (8, BLOCK))
    m[...] = value * over[0:1, :]
    scale[...] = jnp.sqrt(over)


def kernel(
    kernel_hbm, start, test, cutoff, image_out, inverse, kept_out,
    buf, kf, khl, acc, m, scale, scaled, loc, sib, lines, full, cloc, csib, clines, cfull, psend, precv,
    ag_recv, ag_send, k_local, k_recv, k_send, ar_recv, ar_send, cr_recv, cr_send, p_recv, p_send,
):
    row, col = lax.axis_index("row"), lax.axis_index("col")
    core = lax.rem(col, 2)
    here = (
        lax.rem(lax.div(col, 2), 2) * 2 + lax.rem(row, 2),
        lax.div(col, 4),
        lax.div(row, 2),
    )

    def device(x, y, z, c):
        return (z * 2 + lax.rem(x, 2), (y * 2 + lax.div(x, 2)) * 2 + c)

    def moved(axis, by):
        place = list(here)
        place[axis] = lax.rem(place[axis] + by, RING)
        return device(*place, core)

    sibling = device(*here, 1 - core)
    neighbours = [moved(axis, 1 if sign > 0 else RING - 1) for axis, sign in STEPS]

    barrier = pltpu.get_barrier_semaphore()
    greet = [moved(axis, by) for axis in range(3) for by in (1, 2, 3)] + [sibling]
    for other in greet:
        pl.semaphore_signal(barrier, inc=1, device_id=other, device_id_type=MESH)
    pl.semaphore_wait(barrier, len(greet))

    def remote(src, dst, send, recv, to):
        return pltpu.make_async_remote_copy(
            src_ref=src, dst_ref=dst, send_sem=send, recv_sem=recv, device_id=to, device_id_type=MESH
        )

    def block(par, s, count=1):
        return buf.at[par, pl.ds(s * BLOCK, count * BLOCK)]

    def forward(par, s):
        for child, label in CHILDREN[s]:
            remote(
                block(par, s), block(par, child), ag_send, ag_recv.at[par, GROUP[child]], neighbours[label]
            ).start()

    def arrived(par, group):
        whole = block(par, group, GROUP.count(group))
        pltpu.make_async_copy(whole, whole, ag_recv.at[par, group]).wait()

    def columns(s, c):
        x, y, z = [lax.rem(p + RING - d, RING) for p, d in zip(here, ORDER[s])]
        r, q = device(x, y, z, c)
        return pl.ds(pl.multiple_of((r * 16 + q) * BLOCK, BLOCK), BLOCK)

    def lanes(c):
        return pl.ds(c * CHUNK * BLOCK, CHUNK * BLOCK)

    def start_kernel_copies(s):
        c, there = s // CHUNK, pl.ds(s * BLOCK, BLOCK)
        remote(
            kernel_hbm.at[:, columns(s, 1 - core)], kf.at[pl.ds(BLOCK, BLOCK), there],
            k_send.at[c], k_recv.at[c], sibling,
        ).start()
        pltpu.make_async_copy(
            kernel_hbm.at[:, columns(s, core)], kf.at[pl.ds(0, BLOCK), there], k_local.at[c]
        ).start()

    def split_kernel(c):
        own, other = kf.at[pl.ds(0, BLOCK), lanes(c)], kf.at[pl.ds(BLOCK, BLOCK), lanes(c)]
        pltpu.make_async_copy(own, own, k_local.at[c]).wait()
        pltpu.make_async_copy(other, other, k_recv.at[c]).wait()
        value = kf[:, lanes(c)]
        high = value.astype(jnp.bfloat16)
        khl[0 : 2 * BLOCK, lanes(c)] = high
        khl[2 * BLOCK : 4 * BLOCK, lanes(c)] = (value - high.astype(jnp.float32)).astype(jnp.bfloat16)

    def leaves(par, c):
        for group in sorted(set(GROUP[c * CHUNK : (c + 1) * CHUNK])):
            if group >= INNER:
                arrived(par, group)

    def multiply(par, c):
        x = buf[par, pl.ds(c * CHUNK * BLOCK, CHUNK * BLOCK), :]
        high = x.astype(jnp.bfloat16)
        low = (x - high.astype(jnp.float32)).astype(jnp.bfloat16)
        term = jnp.dot(
            khl[:, lanes(c)], jnp.concatenate([high, low], axis=1), preferred_element_type=jnp.float32
        )
        if c == 0:
            acc[...] = term
        else:
            acc[...] += term

    def sum_stages(loc, sib, lines, full, recv, send):
        kept = pl.ds(pl.multiple_of(core * HALF, HALF), HALF)
        given = pl.ds(pl.multiple_of((1 - core) * HALF, HALF), HALF)
        sent = []

        def start(src, dst, index, to):
            copy = remote(src, dst, send.at[index], recv.at[index], to)
            copy.start()
            sent.append(copy)

        def wait(ref, index):
            pltpu.make_async_copy(ref, ref, recv.at[index]).wait()

        def to_line(axis, value):
            mine = lines.at[axis, here[axis]]
            mine[...] = value
            for by in (1, 2, 3):
                start(mine, mine, 1 + 3 * axis + by - 1, moved(axis, by))

        def from_line(axis):
            for by in (1, 2, 3):
                wait(lines.at[axis, lax.rem(here[axis] + RING - by, RING)], 1 + 3 * axis + by - 1)
            return (lines[axis, 0] + lines[axis, 1]) + (lines[axis, 2] + lines[axis, 3])

        def first():
            start(loc.at[given], sib, 0, sibling)

        def second():
            wait(sib, 0)
            to_line(0, loc[kept, :] + sib[...])

        def fifth():
            full[kept, :] = from_line(2)
            start(full.at[kept], full.at[kept], 10, sibling)

        def last():
            wait(full.at[given], 10)
            for copy in sent:
                copy.wait_send()

        return [
            first, second, lambda: to_line(1, from_line(0)), lambda: to_line(2, from_line(1)), fifth, last
        ]

    def factor_panel(p):
        if p == 0:
            load_scaled(full_now[0], m, scale)
        eliminate(m, inverse, scale, scaled, p)

    full_now = [None]

    def gather_and_multiply(par, tasks, work, beside):
        forward(par, 0)
        for s in range(INNER):
            if s:
                arrived(par, s)
                forward(par, s)
            for task in tasks.get(s, ()):
                task()
        for task in work:
            task()
        value = acc[...]
        value = value[:, :BLOCK] + value[:, BLOCK:]
        value = value[: 2 * BLOCK] + value[2 * BLOCK :]
        psend[...] = value[BLOCK:]
        copy = remote(psend, precv.at[par], p_send, p_recv.at[par], sibling)
        copy.start()
        for task in beside:
            task()
        whole = block(par, 1, SLOTS - 1)
        pltpu.make_async_copy(whole, whole, ag_send).wait()
        copy.wait()
        return value[:BLOCK] + precv[par]

    def local_gram(par):
        y = buf[par, pl.ds(0, BLOCK), :]
        loc[...] = exact_dot(y.T, y)

    buf[0, pl.ds(0, BLOCK), :] = start[...]
    tasks = {}
    for s in range(SLOTS):
        tasks.setdefault((s * 2) // 5, []).append(lambda s=s: start_kernel_copies(s))
    work = []
    for c in range(SLOTS // CHUNK):
        into = tasks.setdefault((26, 28, 31, 33)[c], []) if c < 4 else work
        into += [lambda c=c: split_kernel(c), lambda c=c: leaves(0, c), lambda c=c: multiply(0, c)]
    image = gather_and_multiply(0, tasks, work, [])
    buf[1, pl.ds(0, BLOCK), :] = image
    for c in range(SLOTS // CHUNK):
        given = kf.at[pl.ds(0, BLOCK), lanes(c)]
        pltpu.make_async_copy(given, given, k_send.at[c]).wait()

    def step(t, carry):
        par = lax.rem(t, 2)
        stages = sum_stages(loc, sib.at[par], lines.at[par], full.at[par], ar_recv.at[par], ar_send)
        full_now[0] = full.at[par]
        tasks = {0: [lambda: local_gram(par), stages[0]]}
        for at, stage in zip((0, 6, 20, 35), stages[1:5]):
            tasks.setdefault(at, []).append(stage)
        product = [lambda c=c: multiply(par, c) for c in range(SLOTS // CHUNK)]
        panel = [lambda p=p: factor_panel(p) for p in range(16)]
        for at, c in ((20, 0), (26, 1), (33, 2)):
            tasks.setdefault(at, []).append(product[c])
        work = [product[3], lambda: leaves(par, 4), product[4], stages[5]]
        work += [lambda: leaves(par, 5), lambda: leaves(par, 6)]
        work += [product[5]] + panel[0:4] + [product[6]] + panel[4:8]
        work += [lambda: leaves(par, 7), product[7]]
        image = gather_and_multiply(par, tasks, work, panel[8:])
        buf[1 - par, pl.ds(0, BLOCK), :] = exact_dot(image, inverse[...], (((1,), (1,)), ((), ())))
        return carry

    lax.fori_loop(1, ITERATIONS, step, 0)

    par = ITERATIONS % 2
    stages = sum_stages(loc, sib.at[par], lines.at[par], full.at[par], ar_recv.at[par], ar_send)
    late = sum_stages(cloc, csib, clines, cfull, cr_recv, cr_send)
    full_now[0] = full.at[par]
    local_gram(par)
    stages[0]()
    last = buf[par, pl.ds(0, BLOCK), :]
    cloc[...] = exact_dot(last.T, test[...])
    stages[1]()
    for one, two in zip(late[:4], stages[2:]):
        one()
        two()
    for p in range(16):
        if p == 4:
            late[4]()
        if p == 8:
            late[5]()
        factor_panel(p)
    image_out[...] = buf[par, pl.ds(0, BLOCK), :]
    keep = lax.broadcasted_iota(jnp.int32, (BLOCK, TEST), 0) < cutoff[0]
    kept_out[...] = exact_dot(inverse[...], cfull[...]) * jnp.where(keep, 1.0, 0.0)


def project(image, inverse, kept, subspace, projection):
    block = exact_dot(image[...], inverse[...], (((1,), (1,)), ((), ())))
    subspace[...] = block
    projection[...] = exact_dot(block, kept[...])


def per_device(kernel_rows, start_block, test_kernel, cutoff):
    f32 = jnp.float32
    vmem = pl.BlockSpec(memory_space=pltpu.VMEM)
    dma = pltpu.SemaphoreType.DMA
    chunks = SLOTS // CHUNK
    narrow = jax.ShapeDtypeStruct((BLOCK, BLOCK), f32)
    broad = jax.ShapeDtypeStruct((BLOCK, TEST), f32)
    image, inverse, kept = pl.pallas_call(
        kernel,
        out_shape=(narrow, narrow, broad),
        in_specs=[pl.BlockSpec(memory_space=pl.ANY), vmem, vmem, pl.BlockSpec(memory_space=pltpu.SMEM)],
        out_specs=(vmem, vmem, vmem),
        scratch_shapes=[
            pltpu.VMEM((2, SLOTS * BLOCK, BLOCK), f32),
            pltpu.VMEM((2 * BLOCK, SLOTS * BLOCK), f32),
            pltpu.VMEM((4 * BLOCK, SLOTS * BLOCK), jnp.bfloat16),
            pltpu.VMEM((4 * BLOCK, 2 * BLOCK), f32),
            pltpu.VMEM((BLOCK, BLOCK), f32),
            pltpu.VMEM((8, BLOCK), f32),
            pltpu.VMEM((GROUPED, BLOCK), f32),
            pltpu.VMEM((BLOCK, BLOCK), f32),
            pltpu.VMEM((2, HALF, BLOCK), f32),
            pltpu.VMEM((2, 3, RING, HALF, BLOCK), f32),
            pltpu.VMEM((2, BLOCK, BLOCK), f32),
            pltpu.VMEM((BLOCK, TEST), f32),
            pltpu.VMEM((HALF, TEST), f32),
            pltpu.VMEM((3, RING, HALF, TEST), f32),
            pltpu.VMEM((BLOCK, TEST), f32),
            pltpu.VMEM((BLOCK, BLOCK), f32),
            pltpu.VMEM((2, BLOCK, BLOCK), f32),
            dma((2, SLOTS)),
            dma,
            dma((chunks,)),
            dma((chunks,)),
            dma((chunks,)),
            dma((2, 11)),
            dma((11,)),
            dma((11,)),
            dma((11,)),
            dma((2,)),
            dma,
        ],
        compiler_params=pltpu.CompilerParams(
            collective_id=0, has_side_effects=True, vmem_limit_bytes=56 * 1024 * 1024
        ),
        cost_estimate=pl.CostEstimate(
            flops=4 * 2 * 512 * 8192 * 256, bytes_accessed=16 * 2**20, transcendentals=0
        ),
        name="iterate",
    )(kernel_rows, start_block, test_kernel, cutoff)
    return pl.pallas_call(project, out_shape=(narrow, broad), name="project")(image, inverse, kept)


def solution(mesh):
    in_specs = (P(("row", "col"), None), P(("row", "col"), None), P(("row", "col"), None), P())
    out_specs = (P(("row", "col"), None), P(("row", "col"), None))
    return jax.shard_map(
        per_device, mesh=mesh, in_specs=in_specs, out_specs=out_specs, check_vma=False
    )
```

```python
import functools

import jax
import jax.numpy as jnp
from jax import lax
from jax.experimental import pallas as pl
from jax.experimental.pallas import tpu as pltpu
from jax.sharding import PartitionSpec as P

BLOCK = 128
TEST = 256
ITERATIONS = 4
RING = 4
SLOTS = RING**3
CHUNK = 8
TEAM = 2 * RING
PIECE = BLOCK // TEAM
GROUPED = BLOCK
MESH = pl.DeviceIdType.MESH
HIGHEST = lax.Precision.HIGHEST
STEPS = [(axis, sign) for axis in range(3) for sign in (1, -1)]


TREE = (
    0, 75, 10, 96, 26, 23, 289, 51, 95, 168, 295, 32, 16, 81, 102, 307,
    122, 363, 47, 192, 58, 369, 71, 126, 199, 177, 332, 343, 41, 376, 355, 267,
    138, 208, 247, 184, 119, 314, 379, 304, 320, 191, 108, 88, 339, 216, 146, 215,
    152, 65, 162, 224, 351, 277, 329, 132, 274, 243, 230, 259, 287, 234, 256, 159,
)


def spanning_tree():
    order = [(code // 96, code // 24 % 4, code // 6 % 4) for code in TREE]
    slot = {d: s for s, d in enumerate(order)}
    children = [[] for _ in order]
    height = [0] * len(order)
    depth = lambda s: sum(min(c, RING - c) for c in order[s])
    for s in sorted(range(1, len(order)), key=depth, reverse=True):
        axis, sign = STEPS[TREE[s] % 6]
        before = list(order[s])
        before[axis] = (before[axis] - sign) % RING
        parent = slot[tuple(before)]
        children[parent].append((s, TREE[s] % 6))
        height[parent] = max(height[parent], height[s] + 1)
    for found in children:
        found.sort(key=lambda child: -height[child[0]])
    return order, children


ORDER, CHILDREN = spanning_tree()
INNER = sum(1 for found in CHILDREN if found)
GROUP = [s if s < INNER else max(INNER, s // CHUNK * CHUNK) for s in range(SLOTS)]


def exact_dot(a, b, dims=(((1,), (0,)), ((), ()))):
    return lax.dot_general(a, b, dims, precision=HIGHEST, preferred_element_type=jnp.float32)


def reciprocal(x):
    r = pl.reciprocal(x, approx=True)
    r = r * (2.0 - x * r)
    return r * (2.0 - x * r)


def eliminate(m, inverse, scale, scaled, panel):
    base = 8 * panel
    end = base // GROUPED * GROUPED + GROUPED
    wide = (8, BLOCK)
    lane = lax.broadcasted_iota(jnp.int32, wide, 1)
    within = (lane >= base) & (lane < base + 8)
    top = m[base : base + 8, :]
    raw = [jnp.broadcast_to(top[k : k + 1, :], wide) for k in range(8)]
    a = {
        (k, i): jnp.broadcast_to(raw[k][:, base + i : base + i + 1], wide) for k in range(8) for i in range(k, 8)
    }
    rows = [jnp.where(within, jnp.where(lane == base + k, 1.0, 0.0), raw[k]) for k in range(8)]
    over, factor = {}, {}
    for k in range(0, 8, 2):
        p, q, r = a[k, k], a[k, k + 1], a[k + 1, k + 1]
        over[k] = reciprocal(p * r - q * q)
        for i in range(k + 2, 8):
            factor[k, i] = (r * a[k, i] - q * a[k + 1, i]) * over[k]
            factor[k + 1, i] = (p * a[k + 1, i] - q * a[k, i]) * over[k]
            for j in range(i, 8):
                a[i, j] = a[i, j] - (factor[k, i] * a[k, j] + factor[k + 1, i] * a[k + 1, j])
            rows[i] = rows[i] - (factor[k, i] * rows[k] + factor[k + 1, i] * rows[k + 1])
    if base + 8 < end:
        solved = [None] * 8
        for k in range(0, 8, 2):
            p, q, r = a[k, k] * over[k], a[k, k + 1] * over[k], a[k + 1, k + 1] * over[k]
            solved[k] = r * rows[k] - q * rows[k + 1]
            solved[k + 1] = p * rows[k + 1] - q * rows[k]
        for k in (6, 4, 2):
            for i in range(k):
                solved[i] = solved[i] - (factor[i, k] * solved[k] + factor[i, k + 1] * solved[k + 1])
        for r in range(base + 8, end, 8):
            rest = m[r : r + 8, :]
            terms = [jnp.broadcast_to(rest[:, base + k : base + k + 1], wide) * solved[k] for k in range(8)]
            while len(terms) > 1:
                terms = [x + y for x, y in zip(terms[::2], terms[1::2])]
            m[r : r + 8, :] = jnp.where(within, 0.0, rest) - terms[0]
    for k in range(0, 8, 2):
        p, q = a[k, k], a[k, k + 1]
        first = rows[k] * (1.0 / jnp.sqrt(p))
        second = (rows[k + 1] - rows[k] * (q / p)) * jnp.sqrt(p * over[k])
        for j, done in ((base + k, first), (base + k + 1, second)):
            inverse[j : j + 1, :] = jnp.where(lane < base + 8, done * scale[...], 0.0)[0:1, :]
            if end < BLOCK:
                kept = (lane < base + 8) | (lane >= end)
                scaled[j % GROUPED : j % GROUPED + 1, :] = jnp.where(kept, done, 0.0)[0:1, :]
    if base + 8 == end and end < BLOCK:
        done = scaled[...]
        lanes = lax.broadcasted_iota(jnp.int32, (BLOCK - end, BLOCK), 1)
        rest = jnp.where((lanes >= end - GROUPED) & (lanes < end), 0.0, m[end:, :])
        m[end:, :] = rest - exact_dot(done.T[end:, :], done)


def load_scaled(gram, m, scale):
    value = gram[...]
    rows = lax.broadcasted_iota(jnp.int32, value.shape, 0)
    lanes = lax.broadcasted_iota(jnp.int32, value.shape, 1)
    diagonal = jnp.sum(jnp.where(rows == lanes, value, 0.0), axis=0, keepdims=True)
    over = 1.0 / jnp.broadcast_to(jnp.sum(diagonal, axis=1, keepdims=True), (8, BLOCK))
    m[...] = value * over[0:1, :]
    scale[...] = jnp.sqrt(over)


def kernel(
    kernel_hbm, start, test, cutoff, image_out, inverse, kept_out,
    buf, kf, khl, acc, m, scale, scaled, loc, pieces, lines, full, cloc, cpieces, clines, cfull, psend, precv,
    ag_recv, ag_send, k_local, k_recv, k_send, ar_recv, ar_send, cr_recv, cr_send, p_recv, p_send,
):
    row, col = lax.axis_index("row"), lax.axis_index("col")
    core = lax.rem(col, 2)
    here = (
        lax.rem(lax.div(col, 2), 2) * 2 + lax.rem(row, 2),
        lax.div(col, 4),
        lax.div(row, 2),
    )

    def device(x, y, z, c):
        return (z * 2 + lax.rem(x, 2), (y * 2 + lax.div(x, 2)) * 2 + c)

    def moved(axis, by):
        place = list(here)
        place[axis] = lax.rem(place[axis] + by, RING)
        return device(*place, core)

    sibling = device(*here, 1 - core)
    neighbours = [moved(axis, 1 if sign > 0 else RING - 1) for axis, sign in STEPS]

    barrier = pltpu.get_barrier_semaphore()
    greet = [moved(axis, by) for axis in range(3) for by in (1, 2, 3)]
    greet += [device(lax.rem(here[0] + by, RING), here[1], here[2], 1 - core) for by in range(RING)]
    for other in greet:
        pl.semaphore_signal(barrier, inc=1, device_id=other, device_id_type=MESH)
    pl.semaphore_wait(barrier, len(greet))

    def remote(src, dst, send, recv, to):
        return pltpu.make_async_remote_copy(
            src_ref=src, dst_ref=dst, send_sem=send, recv_sem=recv, device_id=to, device_id_type=MESH
        )

    def block(par, s, count=1):
        return buf.at[par, pl.ds(s * BLOCK, count * BLOCK)]

    def forward(par, s):
        for child, label in CHILDREN[s]:
            remote(
                block(par, s), block(par, child), ag_send, ag_recv.at[par, GROUP[child]], neighbours[label]
            ).start()

    def arrived(par, group):
        whole = block(par, group, GROUP.count(group))
        pltpu.make_async_copy(whole, whole, ag_recv.at[par, group]).wait()

    def columns(s, c):
        x, y, z = [lax.rem(p + RING - d, RING) for p, d in zip(here, ORDER[s])]
        r, q = device(x, y, z, c)
        return pl.ds(pl.multiple_of((r * 16 + q) * BLOCK, BLOCK), BLOCK)

    def lanes(c):
        return pl.ds(c * CHUNK * BLOCK, CHUNK * BLOCK)

    def start_kernel_copies(s):
        c, there = s // CHUNK, pl.ds(s * BLOCK, BLOCK)
        remote(
            kernel_hbm.at[:, columns(s, 1 - core)], kf.at[pl.ds(BLOCK, BLOCK), there],
            k_send.at[c], k_recv.at[c], sibling,
        ).start()
        pltpu.make_async_copy(
            kernel_hbm.at[:, columns(s, core)], kf.at[pl.ds(0, BLOCK), there], k_local.at[c]
        ).start()

    def split_kernel(c):
        own, other = kf.at[pl.ds(0, BLOCK), lanes(c)], kf.at[pl.ds(BLOCK, BLOCK), lanes(c)]
        pltpu.make_async_copy(own, own, k_local.at[c]).wait()
        pltpu.make_async_copy(other, other, k_recv.at[c]).wait()
        value = kf[:, lanes(c)]
        high = value.astype(jnp.bfloat16)
        khl[0 : 2 * BLOCK, lanes(c)] = high
        khl[2 * BLOCK : 4 * BLOCK, lanes(c)] = (value - high.astype(jnp.float32)).astype(jnp.bfloat16)

    def leaves(par, c):
        for group in sorted(set(GROUP[c * CHUNK : (c + 1) * CHUNK])):
            if group >= INNER:
                arrived(par, group)

    def multiply(par, c):
        x = buf[par, pl.ds(c * CHUNK * BLOCK, CHUNK * BLOCK), :]
        high = x.astype(jnp.bfloat16)
        low = (x - high.astype(jnp.float32)).astype(jnp.bfloat16)
        term = jnp.dot(
            khl[:, lanes(c)], jnp.concatenate([high, low], axis=1), preferred_element_type=jnp.float32
        )
        if c == 0:
            acc[...] = term
        else:
            acc[...] += term

    def sum_stages(loc, pieces, lines, full, recv, send):
        me = here[0] * 2 + core
        sent = []

        def member(by):
            return lax.rem(me + by, TEAM)

        def part(e):
            return pl.ds(pl.multiple_of(e * PIECE, PIECE), PIECE)

        def start(src, dst, index, to):
            copy = remote(src, dst, send.at[index], recv.at[index], to)
            copy.start()
            sent.append(copy)

        def wait(ref, index):
            pltpu.make_async_copy(ref, ref, recv.at[index]).wait()

        def to_team(source, target, first):
            for by in range(1, TEAM):
                e = member(by)
                start(source(e), target(me), first + by - 1, device(lax.div(e, 2), here[1], here[2], lax.rem(e, 2)))

        def from_team(target, first):
            for by in range(1, TEAM):
                wait(target(member(TEAM - by)), first + by - 1)

        def to_line(axis, value):
            mine = lines.at[axis - 1, here[axis]]
            mine[...] = value
            for by in (1, 2, 3):
                start(mine, mine, 3 + 3 * axis + by, moved(axis, by))

        def from_line(axis):
            for by in (1, 2, 3):
                wait(lines.at[axis - 1, lax.rem(here[axis] + RING - by, RING)], 3 + 3 * axis + by)
            got = [lines[axis - 1, p] for p in range(RING)]
            return (got[0] + got[1]) + (got[2] + got[3])

        def scatter():
            to_team(lambda e: loc.at[part(e)], lambda e: pieces.at[e], 0)
            pieces[me] = loc[part(me), :]

        def along_y():
            from_team(lambda e: pieces.at[e], 0)
            got = [pieces[e] for e in range(TEAM)]
            to_line(1, ((got[0] + got[1]) + (got[2] + got[3])) + ((got[4] + got[5]) + (got[6] + got[7])))

        def along_z():
            to_line(2, from_line(1))

        def gather():
            full[part(me), :] = from_line(2)
            to_team(lambda e: full.at[part(me)], lambda e: full.at[part(e)], 13)

        def finish():
            from_team(lambda e: full.at[part(e)], 13)
            for copy in sent:
                copy.wait_send()

        return [scatter, along_y, along_z, gather, finish]

    def factor_panel(p):
        if p == 0:
            load_scaled(full_now[0], m, scale)
        eliminate(m, inverse, scale, scaled, p)

    full_now = [None]

    def gather_and_multiply(par, tasks, work, beside):
        forward(par, 0)
        for s in range(INNER):
            if s:
                arrived(par, s)
                forward(par, s)
            for task in tasks.get(s, ()):
                task()
        for task in work:
            task()
        value = acc[...]
        value = value[:, :BLOCK] + value[:, BLOCK:]
        value = value[: 2 * BLOCK] + value[2 * BLOCK :]
        psend[...] = value[BLOCK:]
        copy = remote(psend, precv.at[par], p_send, p_recv.at[par], sibling)
        copy.start()
        for task in beside:
            task()
        whole = block(par, 1, SLOTS - 1)
        pltpu.make_async_copy(whole, whole, ag_send).wait()
        copy.wait()
        return value[:BLOCK] + precv[par]

    def local_gram(par):
        y = buf[par, pl.ds(0, BLOCK), :]
        loc[...] = exact_dot(y.T, y)

    buf[0, pl.ds(0, BLOCK), :] = start[...]
    tasks = {}
    for s in range(SLOTS):
        tasks.setdefault((s * 2) // 5, []).append(lambda s=s: start_kernel_copies(s))
    work = []
    for c in range(SLOTS // CHUNK):
        into = tasks.setdefault((26, 28, 31, 33)[c], []) if c < 4 else work
        into += [lambda c=c: split_kernel(c), lambda c=c: leaves(0, c), lambda c=c: multiply(0, c)]
    image = gather_and_multiply(0, tasks, work, [])
    buf[1, pl.ds(0, BLOCK), :] = image
    for c in range(SLOTS // CHUNK):
        given = kf.at[pl.ds(0, BLOCK), lanes(c)]
        pltpu.make_async_copy(given, given, k_send.at[c]).wait()

    def step(t, carry):
        par = lax.rem(t, 2)
        stages = sum_stages(loc, pieces.at[par], lines.at[par], full.at[par], ar_recv.at[par], ar_send)
        full_now[0] = full.at[par]
        tasks = {0: [lambda: local_gram(par), stages[0]]}
        for at, stage in zip((0, 6, 18, 28), stages[1:]):
            tasks.setdefault(at, []).append(stage)
        product = [lambda c=c: multiply(par, c) for c in range(SLOTS // CHUNK)]
        panel = [lambda p=p: factor_panel(p) for p in range(16)]
        for at, task in [(20, product[0]), (26, product[1])] + [(28 + p, panel[p]) for p in range(8)]:
            tasks.setdefault(at, []).append(task)
        work = [product[2], product[3], lambda: leaves(par, 4), product[4]]
        work += [lambda: leaves(par, 5), lambda: leaves(par, 6), product[5], product[6]] + panel[8:12]
        work += [lambda: leaves(par, 7), product[7]]
        image = gather_and_multiply(par, tasks, work, panel[12:])
        buf[1 - par, pl.ds(0, BLOCK), :] = exact_dot(image, inverse[...], (((1,), (1,)), ((), ())))
        return carry

    lax.fori_loop(1, ITERATIONS, step, 0)

    par = ITERATIONS % 2
    stages = sum_stages(loc, pieces.at[par], lines.at[par], full.at[par], ar_recv.at[par], ar_send)
    late = sum_stages(cloc, cpieces, clines, cfull, cr_recv, cr_send)
    full_now[0] = full.at[par]
    local_gram(par)
    stages[0]()
    last = buf[par, pl.ds(0, BLOCK), :]
    cloc[...] = exact_dot(last.T, test[...])
    stages[1]()
    for one, two in zip(late[:3], stages[2:]):
        one()
        two()
    for p in range(16):
        if p == 4:
            late[3]()
        if p == 10:
            late[4]()
        factor_panel(p)
    image_out[...] = buf[par, pl.ds(0, BLOCK), :]
    keep = lax.broadcasted_iota(jnp.int32, (BLOCK, TEST), 0) < cutoff[0]
    kept_out[...] = exact_dot(inverse[...], cfull[...]) * jnp.where(keep, 1.0, 0.0)


def project(image, inverse, kept, subspace, projection):
    block = exact_dot(image[...], inverse[...], (((1,), (1,)), ((), ())))
    subspace[...] = block
    projection[...] = exact_dot(block, kept[...])


def per_device(kernel_rows, start_block, test_kernel, cutoff):
    f32 = jnp.float32
    vmem = pl.BlockSpec(memory_space=pltpu.VMEM)
    dma = pltpu.SemaphoreType.DMA
    chunks = SLOTS // CHUNK
    narrow = jax.ShapeDtypeStruct((BLOCK, BLOCK), f32)
    broad = jax.ShapeDtypeStruct((BLOCK, TEST), f32)
    image, inverse, kept = pl.pallas_call(
        kernel,
        out_shape=(narrow, narrow, broad),
        in_specs=[pl.BlockSpec(memory_space=pl.ANY), vmem, vmem, pl.BlockSpec(memory_space=pltpu.SMEM)],
        out_specs=(vmem, vmem, vmem),
        scratch_shapes=[
            pltpu.VMEM((2, SLOTS * BLOCK, BLOCK), f32),
            pltpu.VMEM((2 * BLOCK, SLOTS * BLOCK), f32),
            pltpu.VMEM((4 * BLOCK, SLOTS * BLOCK), jnp.bfloat16),
            pltpu.VMEM((4 * BLOCK, 2 * BLOCK), f32),
            pltpu.VMEM((BLOCK, BLOCK), f32),
            pltpu.VMEM((8, BLOCK), f32),
            pltpu.VMEM((GROUPED, BLOCK), f32),
            pltpu.VMEM((BLOCK, BLOCK), f32),
            pltpu.VMEM((2, TEAM, PIECE, BLOCK), f32),
            pltpu.VMEM((2, 2, RING, PIECE, BLOCK), f32),
            pltpu.VMEM((2, BLOCK, BLOCK), f32),
            pltpu.VMEM((BLOCK, TEST), f32),
            pltpu.VMEM((TEAM, PIECE, TEST), f32),
            pltpu.VMEM((2, RING, PIECE, TEST), f32),
            pltpu.VMEM((BLOCK, TEST), f32),
            pltpu.VMEM((BLOCK, BLOCK), f32),
            pltpu.VMEM((2, BLOCK, BLOCK), f32),
            dma((2, SLOTS)),
            dma,
            dma((chunks,)),
            dma((chunks,)),
            dma((chunks,)),
            dma((2, 20)),
            dma((20,)),
            dma((20,)),
            dma((20,)),
            dma((2,)),
            dma,
        ],
        compiler_params=pltpu.CompilerParams(
            collective_id=0, has_side_effects=True, vmem_limit_bytes=56 * 1024 * 1024
        ),
        cost_estimate=pl.CostEstimate(
            flops=4 * 2 * 512 * 8192 * 256, bytes_accessed=16 * 2**20, transcendentals=0
        ),
        name="iterate",
    )(kernel_rows, start_block, test_kernel, cutoff)
    return pl.pallas_call(project, out_shape=(narrow, broad), name="project")(image, inverse, kept)


def solution(mesh):
    in_specs = (P(("row", "col"), None), P(("row", "col"), None), P(("row", "col"), None), P())
    out_specs = (P(("row", "col"), None), P(("row", "col"), None))
    return jax.shard_map(
        per_device, mesh=mesh, in_specs=in_specs, out_specs=out_specs, check_vma=False
    )
```

```python
import functools

import jax
import jax.numpy as jnp
from jax import lax
from jax.experimental import pallas as pl
from jax.experimental.pallas import tpu as pltpu
from jax.sharding import PartitionSpec as P

BLOCK = 128
TEST = 256
ITERATIONS = 4
RING = 4
SLOTS = RING**3
CHUNK = 8
TEAM = RING * RING
LINE = 2 * RING
PIECE = BLOCK // TEAM
GROUPED = BLOCK
MESH = pl.DeviceIdType.MESH
HIGHEST = lax.Precision.HIGHEST

TREE = (
    0, 768, 3072, 64, 448, 256, 1088, 1024, 3840, 832, 320, 961, 708, 2050, 3138, 4033,
    1732, 3333, 131, 1223, 3592, 1287, 3913, 1354, 2182, 585, 2317, 1995, 1158, 652, 2768, 3218,
    192, 3264, 513, 1793, 1862, 907, 2126, 2829, 394, 1491, 3791, 3983, 2259, 3409, 2580, 1557,
    3670, 3537, 1431, 1625, 2902, 2456, 2968, 2522, 3035, 2394, 3741, 1948, 2718, 1693, 2650, 3487,
)
ORDER = [(code // 1024, code // 256 % 4, code // 64 % 4) for code in TREE]
PARENT = [code % 64 for code in TREE]


def passed_on():
    children = [[] for _ in TREE]
    height = [0] * SLOTS
    for s in reversed(range(1, SLOTS)):
        children[PARENT[s]].append(s)
        height[PARENT[s]] = max(height[PARENT[s]], height[s] + 1)
    for found in children:
        found.sort(key=lambda s: -height[s])
    return children


CHILDREN = passed_on()
INNER = sum(1 for found in CHILDREN if found)
GROUP = [s if s < INNER else max(INNER, s // CHUNK * CHUNK) for s in range(SLOTS)]


def exact_dot(a, b, dims=(((1,), (0,)), ((), ()))):
    return lax.dot_general(a, b, dims, precision=HIGHEST, preferred_element_type=jnp.float32)


def reciprocal(x):
    r = pl.reciprocal(x, approx=True)
    r = r * (2.0 - x * r)
    return r * (2.0 - x * r)


def eliminate(m, inverse, scale, scaled, panel):
    base = 8 * panel
    end = base // GROUPED * GROUPED + GROUPED
    wide = (8, BLOCK)
    lane = lax.broadcasted_iota(jnp.int32, wide, 1)
    within = (lane >= base) & (lane < base + 8)
    top = m[base : base + 8, :]
    raw = [jnp.broadcast_to(top[k : k + 1, :], wide) for k in range(8)]
    a = {
        (k, i): jnp.broadcast_to(raw[k][:, base + i : base + i + 1], wide) for k in range(8) for i in range(k, 8)
    }
    rows = [jnp.where(within, jnp.where(lane == base + k, 1.0, 0.0), raw[k]) for k in range(8)]
    over, factor = {}, {}
    for k in range(0, 8, 2):
        p, q, r = a[k, k], a[k, k + 1], a[k + 1, k + 1]
        over[k] = reciprocal(p * r - q * q)
        for i in range(k + 2, 8):
            factor[k, i] = (r * a[k, i] - q * a[k + 1, i]) * over[k]
            factor[k + 1, i] = (p * a[k + 1, i] - q * a[k, i]) * over[k]
            for j in range(i, 8):
                a[i, j] = a[i, j] - (factor[k, i] * a[k, j] + factor[k + 1, i] * a[k + 1, j])
            rows[i] = rows[i] - (factor[k, i] * rows[k] + factor[k + 1, i] * rows[k + 1])
    if base + 8 < end:
        solved = [None] * 8
        for k in range(0, 8, 2):
            p, q, r = a[k, k] * over[k], a[k, k + 1] * over[k], a[k + 1, k + 1] * over[k]
            solved[k] = r * rows[k] - q * rows[k + 1]
            solved[k + 1] = p * rows[k + 1] - q * rows[k]
        for k in (6, 4, 2):
            for i in range(k):
                solved[i] = solved[i] - (factor[i, k] * solved[k] + factor[i, k + 1] * solved[k + 1])
        for r in range(base + 8, end, 8):
            rest = m[r : r + 8, :]
            terms = [jnp.broadcast_to(rest[:, base + k : base + k + 1], wide) * solved[k] for k in range(8)]
            while len(terms) > 1:
                terms = [x + y for x, y in zip(terms[::2], terms[1::2])]
            m[r : r + 8, :] = jnp.where(within, 0.0, rest) - terms[0]
    for k in range(0, 8, 2):
        p, q = a[k, k], a[k, k + 1]
        first = rows[k] * (1.0 / jnp.sqrt(p))
        second = (rows[k + 1] - rows[k] * (q / p)) * jnp.sqrt(p * over[k])
        for j, done in ((base + k, first), (base + k + 1, second)):
            inverse[j : j + 1, :] = jnp.where(lane < base + 8, done * scale[...], 0.0)[0:1, :]
            if end < BLOCK:
                kept = (lane < base + 8) | (lane >= end)
                scaled[j % GROUPED : j % GROUPED + 1, :] = jnp.where(kept, done, 0.0)[0:1, :]
    if base + 8 == end and end < BLOCK:
        done = scaled[...]
        lanes = lax.broadcasted_iota(jnp.int32, (BLOCK - end, BLOCK), 1)
        rest = jnp.where((lanes >= end - GROUPED) & (lanes < end), 0.0, m[end:, :])
        m[end:, :] = rest - exact_dot(done.T[end:, :], done)


def load_scaled(value, m, scale):
    rows = lax.broadcasted_iota(jnp.int32, value.shape, 0)
    lanes = lax.broadcasted_iota(jnp.int32, value.shape, 1)
    diagonal = jnp.sum(jnp.where(rows == lanes, value, 0.0), axis=0, keepdims=True)
    over = 1.0 / jnp.broadcast_to(jnp.sum(diagonal, axis=1, keepdims=True), (8, BLOCK))
    m[...] = value * over[0:1, :]
    scale[...] = jnp.sqrt(over)


def kernel(
    kernel_hbm, start, test, cutoff, image_out, inverse, kept_out,
    buf, kf, khl, acc, m, scale, scaled, loc, pieces, lines, full, cloc, cpieces, clines, cfull, psend, precv,
    ag_recv, ag_send, k_local, k_recv, k_send, ar_recv, ar_send, cr_recv, cr_send, p_recv, p_send,
):
    row, col = lax.axis_index("row"), lax.axis_index("col")
    core = lax.rem(col, 2)
    here = (
        lax.rem(lax.div(col, 2), 2) * 2 + lax.rem(row, 2),
        lax.div(col, 4),
        lax.div(row, 2),
    )

    def device(x, y, z, c):
        return (z * 2 + lax.rem(x, 2), (y * 2 + lax.div(x, 2)) * 2 + c)

    def moved(by, core=core):
        return device(*[lax.rem(p + b, RING) for p, b in zip(here, by)], core)

    def hop(s):
        return tuple((a - b) % RING for a, b in zip(ORDER[s], ORDER[PARENT[s]]))

    sibling = device(*here, 1 - core)
    near = {hop(s) for s in range(1, SLOTS)}
    near |= {tuple(-b % RING for b in by) for by in near}
    near |= {(x, y, 0) for x in range(RING) for y in range(RING)} | {(0, 0, z) for z in range(RING)}
    greet = [moved(by) for by in sorted(near - {(0, 0, 0)})]
    greet += [moved((0, 0, z), 1 - core) for z in range(RING)]

    barrier = pltpu.get_barrier_semaphore()
    for other in greet:
        pl.semaphore_signal(barrier, inc=1, device_id=other, device_id_type=MESH)
    pl.semaphore_wait(barrier, len(greet))

    def remote(src, dst, send, recv, to):
        return pltpu.make_async_remote_copy(
            src_ref=src, dst_ref=dst, send_sem=send, recv_sem=recv, device_id=to, device_id_type=MESH
        )

    def block(par, s, count=1):
        return buf.at[par, pl.ds(s * BLOCK, count * BLOCK)]

    def forward(par, s):
        for child in CHILDREN[s]:
            remote(
                block(par, s), block(par, child), ag_send, ag_recv.at[par, GROUP[child]], moved(hop(child))
            ).start()

    def arrived(par, group):
        whole = block(par, group, GROUP.count(group))
        pltpu.make_async_copy(whole, whole, ag_recv.at[par, group]).wait()

    def columns(s, c):
        x, y, z = [lax.rem(p + RING - d, RING) for p, d in zip(here, ORDER[s])]
        r, q = device(x, y, z, c)
        return pl.ds(pl.multiple_of((r * 16 + q) * BLOCK, BLOCK), BLOCK)

    def lanes(c):
        return pl.ds(c * CHUNK * BLOCK, CHUNK * BLOCK)

    def start_kernel_copies(s):
        c, there = s // CHUNK, pl.ds(s * BLOCK, BLOCK)
        remote(
            kernel_hbm.at[:, columns(s, 1 - core)], kf.at[pl.ds(BLOCK, BLOCK), there],
            k_send.at[c], k_recv.at[c], sibling,
        ).start()
        pltpu.make_async_copy(
            kernel_hbm.at[:, columns(s, core)], kf.at[pl.ds(0, BLOCK), there], k_local.at[c]
        ).start()

    def split_kernel(c):
        own, other = kf.at[pl.ds(0, BLOCK), lanes(c)], kf.at[pl.ds(BLOCK, BLOCK), lanes(c)]
        pltpu.make_async_copy(own, own, k_local.at[c]).wait()
        pltpu.make_async_copy(other, other, k_recv.at[c]).wait()
        value = kf[:, lanes(c)]
        high = value.astype(jnp.bfloat16)
        khl[0 : 2 * BLOCK, lanes(c)] = high
        khl[2 * BLOCK : 4 * BLOCK, lanes(c)] = (value - high.astype(jnp.float32)).astype(jnp.bfloat16)

    def leaves(par, c):
        for group in sorted(set(GROUP[c * CHUNK : (c + 1) * CHUNK])):
            if group >= INNER:
                arrived(par, group)

    def multiply(par, c):
        x = buf[par, pl.ds(c * CHUNK * BLOCK, CHUNK * BLOCK), :]
        high = x.astype(jnp.bfloat16)
        low = (x - high.astype(jnp.float32)).astype(jnp.bfloat16)
        term = jnp.dot(
            khl[:, lanes(c)], jnp.concatenate([high, low], axis=1), preferred_element_type=jnp.float32
        )
        if c == 0:
            acc[...] = term
        else:
            acc[...] += term

    def sum_stages(loc, pieces, line, full, recv, send):
        me = here[0] * RING + here[1]
        spot = here[2] * 2 + core

        def part(e):
            return pl.ds(pl.multiple_of(e * PIECE, PIECE), PIECE)

        def to_team(source, target, stage):
            for by in range(1, TEAM):
                e = lax.rem(me + by, TEAM)
                to = device(lax.div(e, RING), lax.rem(e, RING), here[2], core)
                remote(source(e), target.at[by - 1], send.at[stage], recv.at[stage], to).start()

        def await_all(target, count, semaphore):
            whole = target.at[pl.ds(0, count)]
            pltpu.make_async_copy(whole, whole, semaphore).wait()

        def tree_sum(got):
            while len(got) > 1:
                got = [x + y for x, y in zip(got[::2], got[1::2])]
            return got[0]

        def scatter():
            to_team(lambda e: loc.at[part(e)], pieces, 0)

        def exchange():
            await_all(pieces, TEAM - 1, recv.at[0])
            line[LINE - 1] = tree_sum([pieces[k] for k in range(TEAM - 1)] + [loc[part(me), :]])
            for by in range(1, LINE):
                f = lax.rem(spot + by, LINE)
                to = device(here[0], here[1], lax.div(f, 2), lax.rem(f, 2))
                remote(line.at[LINE - 1], line.at[by - 1], send.at[1], recv.at[1], to).start()

        def gather():
            await_all(line, LINE - 1, recv.at[1])
            full[TEAM - 1] = tree_sum([line[lax.rem(spot - f + 2 * LINE - 1, LINE)] for f in range(LINE)])
            to_team(lambda e: full.at[TEAM - 1], full, 2)

        def finish():
            await_all(full, TEAM - 1, recv.at[2])
            await_all(pieces, TEAM - 1, send.at[0])
            await_all(line, LINE - 1, send.at[1])
            await_all(full, TEAM - 1, send.at[2])

        return [scatter, exchange, gather, finish]

    def whole_sum(full):
        me = here[0] * RING + here[1]
        return jnp.concatenate([full[lax.rem(me - e + 2 * TEAM - 1, TEAM)] for e in range(TEAM)], axis=0)

    def factor_panel(p):
        if p == 0:
            load_scaled(whole_sum(full_now[0]), m, scale)
        eliminate(m, inverse, scale, scaled, p)

    full_now = [None]

    def gather_and_multiply(par, tasks, work, beside):
        forward(par, 0)
        for s in range(INNER):
            if s:
                arrived(par, s)
                forward(par, s)
            for task in tasks.get(s, ()):
                task()
        for task in work:
            task()
        value = acc[...]
        value = value[:, :BLOCK] + value[:, BLOCK:]
        value = value[: 2 * BLOCK] + value[2 * BLOCK :]
        psend[...] = value[BLOCK:]
        copy = remote(psend, precv.at[par], p_send, p_recv.at[par], sibling)
        copy.start()
        for task in beside:
            task()
        whole = block(par, 1, SLOTS - 1)
        pltpu.make_async_copy(whole, whole, ag_send).wait()
        copy.wait()
        return value[:BLOCK] + precv[par]

    def local_gram(par):
        y = buf[par, pl.ds(0, BLOCK), :]
        loc[...] = exact_dot(y.T, y)

    buf[0, pl.ds(0, BLOCK), :] = start[...]
    tasks = {}
    for s in range(SLOTS):
        tasks.setdefault((s * 2) // 5, []).append(lambda s=s: start_kernel_copies(s))
    work = []
    for c in range(SLOTS // CHUNK):
        into = tasks.setdefault((25, 29)[c], []) if c < 2 else work
        into += [lambda c=c: split_kernel(c), lambda c=c: leaves(0, c), lambda c=c: multiply(0, c)]
    image = gather_and_multiply(0, tasks, work, [])
    buf[1, pl.ds(0, BLOCK), :] = image
    for c in range(SLOTS // CHUNK):
        given = kf.at[pl.ds(0, BLOCK), lanes(c)]
        pltpu.make_async_copy(given, given, k_send.at[c]).wait()

    def step(t, carry):
        par = lax.rem(t, 2)
        stages = sum_stages(loc, pieces.at[par], lines.at[par], full.at[par], ar_recv.at[par], ar_send)
        full_now[0] = full.at[par]
        tasks = {0: [lambda: local_gram(par), stages[0]]}
        for at, stage in zip((5, 13), stages[1:3]):
            tasks.setdefault(at, []).append(stage)
        product = [lambda c=c: multiply(par, c) for c in range(SLOTS // CHUNK)]
        panel = [lambda p=p: factor_panel(p) for p in range(16)]
        for at, c in ((20, 0), (25, 1), (29, 2)):
            tasks.setdefault(at, []).append(product[c])
        work = [product[3], stages[3]] + panel[0:4]
        work += [lambda: leaves(par, 4), lambda: leaves(par, 5), product[4], product[5]] + panel[4:8]
        work += [lambda: leaves(par, 6), product[6]] + panel[8:12] + [lambda: leaves(par, 7), product[7]]
        image = gather_and_multiply(par, tasks, work, panel[12:])
        buf[1 - par, pl.ds(0, BLOCK), :] = exact_dot(image, inverse[...], (((1,), (1,)), ((), ())))
        return carry

    lax.fori_loop(1, ITERATIONS, step, 0)

    par = ITERATIONS % 2
    stages = sum_stages(loc, pieces.at[par], lines.at[par], full.at[par], ar_recv.at[par], ar_send)
    late = sum_stages(cloc, cpieces, clines, cfull, cr_recv, cr_send)
    full_now[0] = full.at[par]
    local_gram(par)
    stages[0]()
    last = buf[par, pl.ds(0, BLOCK), :]
    cloc[...] = exact_dot(last.T, test[...])
    late[0]()
    stages[1]()
    late[1]()
    stages[2]()
    late[2]()
    stages[3]()
    for p in range(16):
        if p == 8:
            late[3]()
        factor_panel(p)
    image_out[...] = buf[par, pl.ds(0, BLOCK), :]
    keep = lax.broadcasted_iota(jnp.int32, (BLOCK, TEST), 0) < cutoff[0]
    kept_out[...] = exact_dot(inverse[...], whole_sum(cfull)) * jnp.where(keep, 1.0, 0.0)


def project(image, inverse, kept, subspace, projection):
    block = exact_dot(image[...], inverse[...], (((1,), (1,)), ((), ())))
    subspace[...] = block
    projection[...] = exact_dot(block, kept[...])


def per_device(kernel_rows, start_block, test_kernel, cutoff):
    f32 = jnp.float32
    vmem = pl.BlockSpec(memory_space=pltpu.VMEM)
    dma = pltpu.SemaphoreType.DMA
    chunks = SLOTS // CHUNK
    narrow = jax.ShapeDtypeStruct((BLOCK, BLOCK), f32)
    broad = jax.ShapeDtypeStruct((BLOCK, TEST), f32)
    image, inverse, kept = pl.pallas_call(
        kernel,
        out_shape=(narrow, narrow, broad),
        in_specs=[pl.BlockSpec(memory_space=pl.ANY), vmem, vmem, pl.BlockSpec(memory_space=pltpu.SMEM)],
        out_specs=(vmem, vmem, vmem),
        scratch_shapes=[
            pltpu.VMEM((2, SLOTS * BLOCK, BLOCK), f32),
            pltpu.VMEM((2 * BLOCK, SLOTS * BLOCK), f32),
            pltpu.VMEM((4 * BLOCK, SLOTS * BLOCK), jnp.bfloat16),
            pltpu.VMEM((4 * BLOCK, 2 * BLOCK), f32),
            pltpu.VMEM((BLOCK, BLOCK), f32),
            pltpu.VMEM((8, BLOCK), f32),
            pltpu.VMEM((GROUPED, BLOCK), f32),
            pltpu.VMEM((BLOCK, BLOCK), f32),
            pltpu.VMEM((2, TEAM, PIECE, BLOCK), f32),
            pltpu.VMEM((2, LINE, PIECE, BLOCK), f32),
            pltpu.VMEM((2, TEAM, PIECE, BLOCK), f32),
            pltpu.VMEM((BLOCK, TEST), f32),
            pltpu.VMEM((TEAM, PIECE, TEST), f32),
            pltpu.VMEM((LINE, PIECE, TEST), f32),
            pltpu.VMEM((TEAM, PIECE, TEST), f32),
            pltpu.VMEM((BLOCK, BLOCK), f32),
            pltpu.VMEM((2, BLOCK, BLOCK), f32),
            dma((2, SLOTS)),
            dma,
            dma((chunks,)),
            dma((chunks,)),
            dma((chunks,)),
            dma((2, 3)),
            dma((3,)),
            dma((3,)),
            dma((3,)),
            dma((2,)),
            dma,
        ],
        compiler_params=pltpu.CompilerParams(
            collective_id=0, has_side_effects=True, vmem_limit_bytes=56 * 1024 * 1024
        ),
        cost_estimate=pl.CostEstimate(
            flops=4 * 2 * 512 * 8192 * 256, bytes_accessed=16 * 2**20, transcendentals=0
        ),
        name="iterate",
    )(kernel_rows, start_block, test_kernel, cutoff)
    return pl.pallas_call(project, out_shape=(narrow, broad), name="project")(image, inverse, kept)


def solution(mesh):
    in_specs = (P(("row", "col"), None), P(("row", "col"), None), P(("row", "col"), None), P())
    out_specs = (P(("row", "col"), None), P(("row", "col"), None))
    return jax.shard_map(
        per_device, mesh=mesh, in_specs=in_specs, out_specs=out_specs, check_vma=False
    )
```

```python
import functools

import jax
import jax.numpy as jnp
from jax import lax
from jax.experimental import pallas as pl
from jax.experimental.pallas import tpu as pltpu
from jax.sharding import PartitionSpec as P

BLOCK = 128
TEST = 256
ITERATIONS = 4
RING = 4
SLOTS = RING**3
CHUNK = 8
TEAM = RING * RING
LINE = 2 * RING
PIECE = BLOCK // TEAM
GROUPED = BLOCK
MESH = pl.DeviceIdType.MESH
HIGHEST = lax.Precision.HIGHEST

TREE = (
    0, 3072, 192, 64, 1024, 960, 320, 256, 768, 1088, 3264, 2049, 3841, 3139, 1474, 130,
    835, 3393, 1989, 1796, 4037, 582, 3335, 1161, 520, 2315, 3210, 3916, 2125, 2385, 1742, 3988,
    1220, 455, 390, 1287, 709, 1353, 2510, 2251, 912, 3026, 1875, 1621, 2827, 3669, 1935, 661,
    1431, 3542, 1555, 3608, 2585, 3796, 2782, 2907, 3482, 1694, 2204, 2653, 2718, 2461, 2975, 3743,
)
ORDER = [(code // 1024, code // 256 % 4, code // 64 % 4) for code in TREE]
PARENT = [code % 64 for code in TREE]


def passed_on():
    children = [[] for _ in TREE]
    height = [0] * SLOTS
    for s in reversed(range(1, SLOTS)):
        children[PARENT[s]].append(s)
        height[PARENT[s]] = max(height[PARENT[s]], height[s] + 1)
    for found in children:
        found.sort(key=lambda s: -height[s])
    return children


CHILDREN = passed_on()
INNER = sum(1 for found in CHILDREN if found)
GROUP = [s if s < INNER else max(INNER, s // CHUNK * CHUNK) for s in range(SLOTS)]


def exact_dot(a, b, dims=(((1,), (0,)), ((), ()))):
    return lax.dot_general(a, b, dims, precision=HIGHEST, preferred_element_type=jnp.float32)


def reciprocal(x):
    r = pl.reciprocal(x, approx=True)
    r = r * (2.0 - x * r)
    return r * (2.0 - x * r)


def eliminate(m, inverse, scale, scaled, panel):
    base = 8 * panel
    end = base // GROUPED * GROUPED + GROUPED
    wide = (8, BLOCK)
    lane = lax.broadcasted_iota(jnp.int32, wide, 1)
    within = (lane >= base) & (lane < base + 8)
    top = m[base : base + 8, :]
    raw = [jnp.broadcast_to(top[k : k + 1, :], wide) for k in range(8)]
    a = {
        (k, i): jnp.broadcast_to(raw[k][:, base + i : base + i + 1], wide) for k in range(8) for i in range(k, 8)
    }
    rows = [jnp.where(within, jnp.where(lane == base + k, 1.0, 0.0), raw[k]) for k in range(8)]
    over, factor = {}, {}
    for k in range(0, 8, 2):
        p, q, r = a[k, k], a[k, k + 1], a[k + 1, k + 1]
        over[k] = reciprocal(p * r - q * q)
        for i in range(k + 2, 8):
            factor[k, i] = (r * a[k, i] - q * a[k + 1, i]) * over[k]
            factor[k + 1, i] = (p * a[k + 1, i] - q * a[k, i]) * over[k]
            for j in range(i, 8):
                a[i, j] = a[i, j] - (factor[k, i] * a[k, j] + factor[k + 1, i] * a[k + 1, j])
            rows[i] = rows[i] - (factor[k, i] * rows[k] + factor[k + 1, i] * rows[k + 1])
    if base + 8 < end:
        solved = [None] * 8
        for k in range(0, 8, 2):
            p, q, r = a[k, k] * over[k], a[k, k + 1] * over[k], a[k + 1, k + 1] * over[k]
            solved[k] = r * rows[k] - q * rows[k + 1]
            solved[k + 1] = p * rows[k + 1] - q * rows[k]
        for k in (6, 4, 2):
            for i in range(k):
                solved[i] = solved[i] - (factor[i, k] * solved[k] + factor[i, k + 1] * solved[k + 1])
        for r in range(base + 8, end, 8):
            rest = m[r : r + 8, :]
            terms = [jnp.broadcast_to(rest[:, base + k : base + k + 1], wide) * solved[k] for k in range(8)]
            while len(terms) > 1:
                terms = [x + y for x, y in zip(terms[::2], terms[1::2])]
            m[r : r + 8, :] = jnp.where(within, 0.0, rest) - terms[0]
    for k in range(0, 8, 2):
        p, q = a[k, k], a[k, k + 1]
        first = rows[k] * (1.0 / jnp.sqrt(p))
        second = (rows[k + 1] - rows[k] * (q / p)) * jnp.sqrt(p * over[k])
        for j, done in ((base + k, first), (base + k + 1, second)):
            inverse[j : j + 1, :] = jnp.where(lane < base + 8, done * scale[...], 0.0)[0:1, :]
            if end < BLOCK:
                kept = (lane < base + 8) | (lane >= end)
                scaled[j % GROUPED : j % GROUPED + 1, :] = jnp.where(kept, done, 0.0)[0:1, :]
    if base + 8 == end and end < BLOCK:
        done = scaled[...]
        lanes = lax.broadcasted_iota(jnp.int32, (BLOCK - end, BLOCK), 1)
        rest = jnp.where((lanes >= end - GROUPED) & (lanes < end), 0.0, m[end:, :])
        m[end:, :] = rest - exact_dot(done.T[end:, :], done)


def load_scaled(value, m, scale):
    rows = lax.broadcasted_iota(jnp.int32, value.shape, 0)
    lanes = lax.broadcasted_iota(jnp.int32, value.shape, 1)
    diagonal = jnp.sum(jnp.where(rows == lanes, value, 0.0), axis=0, keepdims=True)
    over = 1.0 / jnp.broadcast_to(jnp.sum(diagonal, axis=1, keepdims=True), (8, BLOCK))
    m[...] = value * over[0:1, :]
    scale[...] = jnp.sqrt(over)


def kernel(
    kernel_hbm, start, test, cutoff, image_out, inverse, kept_out,
    buf, kf, khl, acc, m, scale, scaled, loc, pieces, lines, full, cloc, cpieces, clines, cfull, psend, precv,
    ag_recv, ag_send, k_local, k_recv, k_send, ar_recv, ar_send, cr_recv, cr_send, p_recv, p_send,
):
    row, col = lax.axis_index("row"), lax.axis_index("col")
    core = lax.rem(col, 2)
    here = (
        lax.rem(lax.div(col, 2), 2) * 2 + lax.rem(row, 2),
        lax.div(col, 4),
        lax.div(row, 2),
    )

    def device(x, y, z, c):
        return (z * 2 + lax.rem(x, 2), (y * 2 + lax.div(x, 2)) * 2 + c)

    def moved(by, core=core):
        return device(*[lax.rem(p + b, RING) for p, b in zip(here, by)], core)

    def hop(s):
        return tuple((a - b) % RING for a, b in zip(ORDER[s], ORDER[PARENT[s]]))

    sibling = device(*here, 1 - core)
    near = {hop(s) for s in range(1, SLOTS)}
    near |= {tuple(-b % RING for b in by) for by in near}
    near |= {(x, y, 0) for x in range(RING) for y in range(RING)} | {(0, 0, z) for z in range(RING)}
    greet = [moved(by) for by in sorted(near - {(0, 0, 0)})]
    greet += [moved((0, 0, z), 1 - core) for z in range(RING)]

    barrier = pltpu.get_barrier_semaphore()
    for other in greet:
        pl.semaphore_signal(barrier, inc=1, device_id=other, device_id_type=MESH)
    pl.semaphore_wait(barrier, len(greet))

    def remote(src, dst, send, recv, to):
        return pltpu.make_async_remote_copy(
            src_ref=src, dst_ref=dst, send_sem=send, recv_sem=recv, device_id=to, device_id_type=MESH
        )

    def block(par, s, count=1):
        return buf.at[par, pl.ds(s * BLOCK, count * BLOCK)]

    def forward(par, s):
        for child in CHILDREN[s]:
            remote(
                block(par, s), block(par, child), ag_send, ag_recv.at[par, GROUP[child]], moved(hop(child))
            ).start()

    def arrived(par, group):
        whole = block(par, group, GROUP.count(group))
        pltpu.make_async_copy(whole, whole, ag_recv.at[par, group]).wait()

    def columns(s, c):
        x, y, z = [lax.rem(p + RING - d, RING) for p, d in zip(here, ORDER[s])]
        r, q = device(x, y, z, c)
        return pl.ds(pl.multiple_of((r * 16 + q) * BLOCK, BLOCK), BLOCK)

    def lanes(c):
        return pl.ds(c * CHUNK * BLOCK, CHUNK * BLOCK)

    def start_kernel_copies(s):
        c, there = s // CHUNK, pl.ds(s * BLOCK, BLOCK)
        remote(
            kernel_hbm.at[:, columns(s, 1 - core)], kf.at[pl.ds(BLOCK, BLOCK), there],
            k_send.at[c], k_recv.at[c], sibling,
        ).start()
        pltpu.make_async_copy(
            kernel_hbm.at[:, columns(s, core)], kf.at[pl.ds(0, BLOCK), there], k_local.at[c]
        ).start()

    def split_kernel(c):
        own, other = kf.at[pl.ds(0, BLOCK), lanes(c)], kf.at[pl.ds(BLOCK, BLOCK), lanes(c)]
        pltpu.make_async_copy(own, own, k_local.at[c]).wait()
        pltpu.make_async_copy(other, other, k_recv.at[c]).wait()
        value = kf[:, lanes(c)]
        high = value.astype(jnp.bfloat16)
        khl[0 : 2 * BLOCK, lanes(c)] = high
        khl[2 * BLOCK : 4 * BLOCK, lanes(c)] = (value - high.astype(jnp.float32)).astype(jnp.bfloat16)

    def leaves(par, c):
        for group in sorted(set(GROUP[c * CHUNK : (c + 1) * CHUNK])):
            if group >= INNER:
                arrived(par, group)

    def multiply(par, c):
        x = buf[par, pl.ds(c * CHUNK * BLOCK, CHUNK * BLOCK), :]
        high = x.astype(jnp.bfloat16)
        low = (x - high.astype(jnp.float32)).astype(jnp.bfloat16)
        term = jnp.dot(
            khl[:, lanes(c)], jnp.concatenate([high, low], axis=1), preferred_element_type=jnp.float32
        )
        if c == 0:
            acc[...] = term
        else:
            acc[...] += term

    def sum_stages(loc, pieces, line, full, recv, send):
        me = here[0] * RING + here[1]
        spot = here[2] * 2 + core

        def part(e):
            return pl.ds(pl.multiple_of(e * PIECE, PIECE), PIECE)

        def to_team(source, target, stage):
            for by in range(1, TEAM):
                e = lax.rem(me + by, TEAM)
                to = device(lax.div(e, RING), lax.rem(e, RING), here[2], core)
                remote(source(e), target.at[by - 1], send.at[stage], recv.at[stage], to).start()

        def await_all(target, count, semaphore):
            whole = target.at[pl.ds(0, count)]
            pltpu.make_async_copy(whole, whole, semaphore).wait()

        def tree_sum(got):
            while len(got) > 1:
                got = [x + y for x, y in zip(got[::2], got[1::2])]
            return got[0]

        def scatter():
            to_team(lambda e: loc.at[part(e)], pieces, 0)

        def exchange():
            await_all(pieces, TEAM - 1, recv.at[0])
            line[LINE - 1] = tree_sum([pieces[k] for k in range(TEAM - 1)] + [loc[part(me), :]])
            for by in range(1, LINE):
                f = lax.rem(spot + by, LINE)
                to = device(here[0], here[1], lax.div(f, 2), lax.rem(f, 2))
                remote(line.at[LINE - 1], line.at[by - 1], send.at[1], recv.at[1], to).start()

        def gather():
            await_all(line, LINE - 1, recv.at[1])
            full[TEAM - 1] = tree_sum([line[lax.rem(spot - f + 2 * LINE - 1, LINE)] for f in range(LINE)])
            to_team(lambda e: full.at[TEAM - 1], full, 2)

        def finish():
            await_all(full, TEAM - 1, recv.at[2])
            await_all(pieces, TEAM - 1, send.at[0])
            await_all(line, LINE - 1, send.at[1])
            await_all(full, TEAM - 1, send.at[2])

        return [scatter, exchange, gather, finish]

    def whole_sum(full):
        me = here[0] * RING + here[1]
        return jnp.concatenate([full[lax.rem(me - e + 2 * TEAM - 1, TEAM)] for e in range(TEAM)], axis=0)

    def factor_panel(p):
        if p == 0:
            load_scaled(whole_sum(full_now[0]), m, scale)
        eliminate(m, inverse, scale, scaled, p)

    full_now = [None]

    def gather_and_multiply(par, tasks, work, beside):
        forward(par, 0)
        for s in range(INNER):
            if s:
                arrived(par, s)
                forward(par, s)
            for task in tasks.get(s, ()):
                task()
        for task in work:
            task()
        value = acc[...]
        value = value[:, :BLOCK] + value[:, BLOCK:]
        value = value[: 2 * BLOCK] + value[2 * BLOCK :]
        psend[...] = value[BLOCK:]
        copy = remote(psend, precv.at[par], p_send, p_recv.at[par], sibling)
        copy.start()
        for task in beside:
            task()
        whole = block(par, 1, SLOTS - 1)
        pltpu.make_async_copy(whole, whole, ag_send).wait()
        copy.wait()
        return value[:BLOCK] + precv[par]

    def local_gram(par):
        y = buf[par, pl.ds(0, BLOCK), :]
        loc[...] = exact_dot(y.T, y)

    buf[0, pl.ds(0, BLOCK), :] = start[...]
    tasks = {}
    for s in range(SLOTS):
        tasks.setdefault((s * 2) // 5, []).append(lambda s=s: start_kernel_copies(s))
    work = []
    for c in range(SLOTS // CHUNK):
        into = tasks.setdefault((24, 30)[c], []) if c < 2 else work
        into += [lambda c=c: split_kernel(c), lambda c=c: leaves(0, c), lambda c=c: multiply(0, c)]
    image = gather_and_multiply(0, tasks, work, [])
    buf[1, pl.ds(0, BLOCK), :] = image
    for c in range(SLOTS // CHUNK):
        given = kf.at[pl.ds(0, BLOCK), lanes(c)]
        pltpu.make_async_copy(given, given, k_send.at[c]).wait()

    def step(t, carry):
        par = lax.rem(t, 2)
        stages = sum_stages(loc, pieces.at[par], lines.at[par], full.at[par], ar_recv.at[par], ar_send)
        full_now[0] = full.at[par]
        tasks = {0: [lambda: local_gram(par), stages[0]]}
        for at, stage in zip((8, 23), stages[1:3]):
            tasks.setdefault(at, []).append(stage)
        product = [lambda c=c: multiply(par, c) for c in range(SLOTS // CHUNK)]
        panel = [lambda p=p: factor_panel(p) for p in range(16)]
        for at, c in ((24, 0), (28, 1), (30, 2)):
            tasks.setdefault(at, []).append(product[c])
        work = [product[3], lambda: leaves(par, 4), product[4], lambda: leaves(par, 5), product[5], stages[3]]
        work += panel[0:4] + [lambda: leaves(par, 6), product[6]] + panel[4:6] + [lambda: leaves(par, 7), product[7]]
        image = gather_and_multiply(par, tasks, work, panel[6:])
        buf[1 - par, pl.ds(0, BLOCK), :] = exact_dot(image, inverse[...], (((1,), (1,)), ((), ())))
        return carry

    lax.fori_loop(1, ITERATIONS, step, 0)

    par = ITERATIONS % 2
    stages = sum_stages(loc, pieces.at[par], lines.at[par], full.at[par], ar_recv.at[par], ar_send)
    late = sum_stages(cloc, cpieces, clines, cfull, cr_recv, cr_send)
    full_now[0] = full.at[par]
    local_gram(par)
    stages[0]()
    last = buf[par, pl.ds(0, BLOCK), :]
    cloc[...] = exact_dot(last.T, test[...])
    late[0]()
    stages[1]()
    late[1]()
    stages[2]()
    late[2]()
    stages[3]()
    for p in range(16):
        if p == 8:
            late[3]()
        factor_panel(p)
    image_out[...] = buf[par, pl.ds(0, BLOCK), :]
    keep = lax.broadcasted_iota(jnp.int32, (BLOCK, TEST), 0) < cutoff[0]
    kept_out[...] = exact_dot(inverse[...], whole_sum(cfull)) * jnp.where(keep, 1.0, 0.0)


def project(image, inverse, kept, subspace, projection):
    block = exact_dot(image[...], inverse[...], (((1,), (1,)), ((), ())))
    subspace[...] = block
    projection[...] = exact_dot(block, kept[...])


def per_device(kernel_rows, start_block, test_kernel, cutoff):
    f32 = jnp.float32
    vmem = pl.BlockSpec(memory_space=pltpu.VMEM)
    dma = pltpu.SemaphoreType.DMA
    chunks = SLOTS // CHUNK
    narrow = jax.ShapeDtypeStruct((BLOCK, BLOCK), f32)
    broad = jax.ShapeDtypeStruct((BLOCK, TEST), f32)
    image, inverse, kept = pl.pallas_call(
        kernel,
        out_shape=(narrow, narrow, broad),
        in_specs=[pl.BlockSpec(memory_space=pl.ANY), vmem, vmem, pl.BlockSpec(memory_space=pltpu.SMEM)],
        out_specs=(vmem, vmem, vmem),
        scratch_shapes=[
            pltpu.VMEM((2, SLOTS * BLOCK, BLOCK), f32),
            pltpu.VMEM((2 * BLOCK, SLOTS * BLOCK), f32),
            pltpu.VMEM((4 * BLOCK, SLOTS * BLOCK), jnp.bfloat16),
            pltpu.VMEM((4 * BLOCK, 2 * BLOCK), f32),
            pltpu.VMEM((BLOCK, BLOCK), f32),
            pltpu.VMEM((8, BLOCK), f32),
            pltpu.VMEM((GROUPED, BLOCK), f32),
            pltpu.VMEM((BLOCK, BLOCK), f32),
            pltpu.VMEM((2, TEAM, PIECE, BLOCK), f32),
            pltpu.VMEM((2, LINE, PIECE, BLOCK), f32),
            pltpu.VMEM((2, TEAM, PIECE, BLOCK), f32),
            pltpu.VMEM((BLOCK, TEST), f32),
            pltpu.VMEM((TEAM, PIECE, TEST), f32),
            pltpu.VMEM((LINE, PIECE, TEST), f32),
            pltpu.VMEM((TEAM, PIECE, TEST), f32),
            pltpu.VMEM((BLOCK, BLOCK), f32),
            pltpu.VMEM((2, BLOCK, BLOCK), f32),
            dma((2, SLOTS)),
            dma,
            dma((chunks,)),
            dma((chunks,)),
            dma((chunks,)),
            dma((2, 3)),
            dma((3,)),
            dma((3,)),
            dma((3,)),
            dma((2,)),
            dma,
        ],
        compiler_params=pltpu.CompilerParams(
            collective_id=0, has_side_effects=True, vmem_limit_bytes=56 * 1024 * 1024
        ),
        cost_estimate=pl.CostEstimate(
            flops=4 * 2 * 512 * 8192 * 256, bytes_accessed=16 * 2**20, transcendentals=0
        ),
        name="iterate",
    )(kernel_rows, start_block, test_kernel, cutoff)
    return pl.pallas_call(project, out_shape=(narrow, broad), name="project")(image, inverse, kept)


def solution(mesh):
    in_specs = (P(("row", "col"), None), P(("row", "col"), None), P(("row", "col"), None), P())
    out_specs = (P(("row", "col"), None), P(("row", "col"), None))
    return jax.shard_map(
        per_device, mesh=mesh, in_specs=in_specs, out_specs=out_specs, check_vma=False
    )
```

```python
import functools

import jax
import jax.numpy as jnp
from jax import lax
from jax.experimental import pallas as pl
from jax.experimental.pallas import tpu as pltpu
from jax.sharding import PartitionSpec as P

BLOCK = 128
TEST = 256
ITERATIONS = 4
RING = 4
SLOTS = RING**3
CHUNK = 8
TEAM = RING * RING
LINE = 2 * RING
PIECE = BLOCK // TEAM
WIDTH = 16
PANELS = BLOCK // WIDTH
MESH = pl.DeviceIdType.MESH
HIGHEST = lax.Precision.HIGHEST

TREE = (
    0, 768, 3072, 64, 448, 256, 1088, 1024, 3840, 832, 320, 961, 708, 2050, 3138, 4033,
    1732, 3333, 131, 1223, 3592, 1287, 3913, 1354, 2182, 585, 2317, 1995, 1158, 652, 2768, 3218,
    192, 3264, 513, 1793, 1862, 907, 2126, 2829, 394, 1491, 3791, 3983, 2259, 3409, 2580, 1557,
    3670, 3537, 1431, 1625, 2902, 2456, 2968, 2522, 3035, 2394, 3741, 1948, 2718, 1693, 2650, 3487,
)
ORDER = [(code // 1024, code // 256 % 4, code // 64 % 4) for code in TREE]
PARENT = [code % 64 for code in TREE]


def passed_on():
    children = [[] for _ in TREE]
    height = [0] * SLOTS
    for s in reversed(range(1, SLOTS)):
        children[PARENT[s]].append(s)
        height[PARENT[s]] = max(height[PARENT[s]], height[s] + 1)
    for found in children:
        found.sort(key=lambda s: -height[s])
    return children


CHILDREN = passed_on()
INNER = sum(1 for found in CHILDREN if found)
GROUP = [s if s < INNER else max(INNER, s // CHUNK * CHUNK) for s in range(SLOTS)]


def exact_dot(a, b, dims=(((1,), (0,)), ((), ()))):
    return lax.dot_general(a, b, dims, precision=HIGHEST, preferred_element_type=jnp.float32)


def reciprocal(x):
    r = pl.reciprocal(x, approx=True)
    r = r * (2.0 - x * r)
    return r * (2.0 - x * r)


def eliminate(m, inverse, scale, panel):
    base = WIDTH * panel
    end = base + WIDTH
    wide = (8, BLOCK)
    lane = lax.broadcasted_iota(jnp.int32, wide, 1)
    within = (lane >= base) & (lane < end)
    raw = [jnp.broadcast_to(m[base + k : base + k + 1, :], wide) for k in range(WIDTH)]
    a = {
        (k, i): jnp.broadcast_to(raw[k][:, base + i : base + i + 1], wide)
        for k in range(WIDTH)
        for i in range(k, WIDTH)
    }
    rows = [jnp.where(within, jnp.where(lane == base + k, 1.0, 0.0), raw[k]) for k in range(WIDTH)]
    over, factor = {}, {}
    for k in range(0, WIDTH, 2):
        p, q, r = a[k, k], a[k, k + 1], a[k + 1, k + 1]
        over[k] = reciprocal(p * r - q * q)
        for i in range(k + 2, WIDTH):
            factor[k, i] = (r * a[k, i] - q * a[k + 1, i]) * over[k]
            factor[k + 1, i] = (p * a[k + 1, i] - q * a[k, i]) * over[k]
            for j in range(i, WIDTH):
                a[i, j] = a[i, j] - (factor[k, i] * a[k, j] + factor[k + 1, i] * a[k + 1, j])
            rows[i] = rows[i] - (factor[k, i] * rows[k] + factor[k + 1, i] * rows[k + 1])
    if end < BLOCK:
        solved = [None] * WIDTH
        for k in range(0, WIDTH, 2):
            p, q, r = a[k, k] * over[k], a[k, k + 1] * over[k], a[k + 1, k + 1] * over[k]
            solved[k] = r * rows[k] - q * rows[k + 1]
            solved[k + 1] = p * rows[k + 1] - q * rows[k]
        for k in range(WIDTH - 2, 0, -2):
            for i in range(k):
                solved[i] = solved[i] - (factor[i, k] * solved[k] + factor[i, k + 1] * solved[k + 1])
        for r in range(end, BLOCK, 8):
            rest = m[r : r + 8, :]
            terms = [jnp.broadcast_to(rest[:, base + k : base + k + 1], wide) * solved[k] for k in range(WIDTH)]
            while len(terms) > 1:
                terms = [x + y for x, y in zip(terms[::2], terms[1::2])]
            m[r : r + 8, :] = jnp.where(within, 0.0, rest) - terms[0]
    for k in range(0, WIDTH, 2):
        p, q = a[k, k], a[k, k + 1]
        first = rows[k] * (scale[...] / jnp.sqrt(p))
        second = (rows[k + 1] - rows[k] * (q / p)) * (scale[...] * jnp.sqrt(p * over[k]))
        for j, done in ((base + k, first), (base + k + 1, second)):
            inverse[j : j + 1, :] = jnp.where(lane < end, done, 0.0)[0:1, :]


def load_scaled(value, m, scale):
    rows = lax.broadcasted_iota(jnp.int32, value.shape, 0)
    lanes = lax.broadcasted_iota(jnp.int32, value.shape, 1)
    diagonal = jnp.sum(jnp.where(rows == lanes, value, 0.0), axis=0, keepdims=True)
    over = 1.0 / jnp.broadcast_to(jnp.sum(diagonal, axis=1, keepdims=True), (8, BLOCK))
    m[...] = value * over[0:1, :]
    scale[...] = jnp.sqrt(over)


def kernel(
    kernel_hbm, start, test, cutoff, image_out, inverse, kept_out,
    buf, kf, khl, acc, m, scale, loc, pieces, lines, full, cloc, cpieces, clines, cfull, psend, precv,
    ag_recv, ag_send, k_local, k_recv, k_send, ar_recv, ar_send, cr_recv, cr_send, p_recv, p_send,
):
    row, col = lax.axis_index("row"), lax.axis_index("col")
    core = lax.rem(col, 2)
    here = (
        lax.rem(lax.div(col, 2), 2) * 2 + lax.rem(row, 2),
        lax.div(col, 4),
        lax.div(row, 2),
    )

    def device(x, y, z, c):
        return (z * 2 + lax.rem(x, 2), (y * 2 + lax.div(x, 2)) * 2 + c)

    def moved(by, core=core):
        return device(*[lax.rem(p + b, RING) for p, b in zip(here, by)], core)

    def hop(s):
        return tuple((a - b) % RING for a, b in zip(ORDER[s], ORDER[PARENT[s]]))

    sibling = device(*here, 1 - core)
    near = {hop(s) for s in range(1, SLOTS)}
    near |= {tuple(-b % RING for b in by) for by in near}
    near |= {(x, y, 0) for x in range(RING) for y in range(RING)} | {(0, 0, z) for z in range(RING)}
    greet = [moved(by) for by in sorted(near - {(0, 0, 0)})]
    greet += [moved((0, 0, z), 1 - core) for z in range(RING)]

    barrier = pltpu.get_barrier_semaphore()
    for other in greet:
        pl.semaphore_signal(barrier, inc=1, device_id=other, device_id_type=MESH)
    pl.semaphore_wait(barrier, len(greet))

    def remote(src, dst, send, recv, to):
        return pltpu.make_async_remote_copy(
            src_ref=src, dst_ref=dst, send_sem=send, recv_sem=recv, device_id=to, device_id_type=MESH
        )

    def block(par, s, count=1):
        return buf.at[par, pl.ds(s * BLOCK, count * BLOCK)]

    def forward(par, s):
        for child in CHILDREN[s]:
            remote(
                block(par, s), block(par, child), ag_send, ag_recv.at[par, GROUP[child]], moved(hop(child))
            ).start()

    def arrived(par, group):
        whole = block(par, group, GROUP.count(group))
        pltpu.make_async_copy(whole, whole, ag_recv.at[par, group]).wait()

    def columns(s, c):
        x, y, z = [lax.rem(p + RING - d, RING) for p, d in zip(here, ORDER[s])]
        r, q = device(x, y, z, c)
        return pl.ds(pl.multiple_of((r * 16 + q) * BLOCK, BLOCK), BLOCK)

    def lanes(c):
        return pl.ds(c * CHUNK * BLOCK, CHUNK * BLOCK)

    def start_kernel_copies(s):
        c, there = s // CHUNK, pl.ds(s * BLOCK, BLOCK)
        remote(
            kernel_hbm.at[:, columns(s, 1 - core)], kf.at[pl.ds(BLOCK, BLOCK), there],
            k_send.at[c], k_recv.at[c], sibling,
        ).start()
        pltpu.make_async_copy(
            kernel_hbm.at[:, columns(s, core)], kf.at[pl.ds(0, BLOCK), there], k_local.at[c]
        ).start()

    def split_kernel(c):
        own, other = kf.at[pl.ds(0, BLOCK), lanes(c)], kf.at[pl.ds(BLOCK, BLOCK), lanes(c)]
        pltpu.make_async_copy(own, own, k_local.at[c]).wait()
        pltpu.make_async_copy(other, other, k_recv.at[c]).wait()
        value = kf[:, lanes(c)]
        high = value.astype(jnp.bfloat16)
        khl[0 : 2 * BLOCK, lanes(c)] = high
        khl[2 * BLOCK : 4 * BLOCK, lanes(c)] = (value - high.astype(jnp.float32)).astype(jnp.bfloat16)

    def leaves(par, c):
        for group in sorted(set(GROUP[c * CHUNK : (c + 1) * CHUNK])):
            if group >= INNER:
                arrived(par, group)

    def multiply(par, c):
        x = buf[par, pl.ds(c * CHUNK * BLOCK, CHUNK * BLOCK), :]
        high = x.astype(jnp.bfloat16)
        low = (x - high.astype(jnp.float32)).astype(jnp.bfloat16)
        term = jnp.dot(
            khl[:, lanes(c)], jnp.concatenate([high, low], axis=1), preferred_element_type=jnp.float32
        )
        if c == 0:
            acc[...] = term
        else:
            acc[...] += term

    def sum_stages(loc, pieces, line, full, recv, send):
        me = here[0] * RING + here[1]
        spot = here[2] * 2 + core

        def part(e):
            return pl.ds(pl.multiple_of(e * PIECE, PIECE), PIECE)

        def to_team(source, target, stage):
            for by in range(1, TEAM):
                e = lax.rem(me + by, TEAM)
                to = device(lax.div(e, RING), lax.rem(e, RING), here[2], core)
                remote(source(e), target.at[by - 1], send.at[stage], recv.at[stage], to).start()

        def await_all(target, count, semaphore):
            whole = target.at[pl.ds(0, count)]
            pltpu.make_async_copy(whole, whole, semaphore).wait()

        def tree_sum(got):
            while len(got) > 1:
                got = [x + y for x, y in zip(got[::2], got[1::2])]
            return got[0]

        def scatter():
            to_team(lambda e: loc.at[part(e)], pieces, 0)

        def exchange():
            await_all(pieces, TEAM - 1, recv.at[0])
            line[LINE - 1] = tree_sum([pieces[k] for k in range(TEAM - 1)] + [loc[part(me), :]])
            for by in range(1, LINE):
                f = lax.rem(spot + by, LINE)
                to = device(here[0], here[1], lax.div(f, 2), lax.rem(f, 2))
                remote(line.at[LINE - 1], line.at[by - 1], send.at[1], recv.at[1], to).start()

        def gather():
            await_all(line, LINE - 1, recv.at[1])
            full[TEAM - 1] = tree_sum([line[lax.rem(spot - f + 2 * LINE - 1, LINE)] for f in range(LINE)])
            to_team(lambda e: full.at[TEAM - 1], full, 2)

        def finish():
            await_all(full, TEAM - 1, recv.at[2])
            await_all(pieces, TEAM - 1, send.at[0])
            await_all(line, LINE - 1, send.at[1])
            await_all(full, TEAM - 1, send.at[2])

        return [scatter, exchange, gather, finish]

    def whole_sum(full):
        me = here[0] * RING + here[1]
        return jnp.concatenate([full[lax.rem(me - e + 2 * TEAM - 1, TEAM)] for e in range(TEAM)], axis=0)

    def factor_panel(p):
        if p == 0:
            load_scaled(whole_sum(full_now[0]), m, scale)
        eliminate(m, inverse, scale, p)

    full_now = [None]

    def gather_and_multiply(par, tasks, work, beside):
        forward(par, 0)
        for s in range(INNER):
            if s:
                arrived(par, s)
                forward(par, s)
            for task in tasks.get(s, ()):
                task()
        for task in work:
            task()
        value = acc[...]
        value = value[:, :BLOCK] + value[:, BLOCK:]
        value = value[: 2 * BLOCK] + value[2 * BLOCK :]
        psend[...] = value[BLOCK:]
        copy = remote(psend, precv.at[par], p_send, p_recv.at[par], sibling)
        copy.start()
        for task in beside:
            task()
        whole = block(par, 1, SLOTS - 1)
        pltpu.make_async_copy(whole, whole, ag_send).wait()
        copy.wait()
        return value[:BLOCK] + precv[par]

    def local_gram(par):
        y = buf[par, pl.ds(0, BLOCK), :]
        loc[...] = exact_dot(y.T, y)

    buf[0, pl.ds(0, BLOCK), :] = start[...]
    tasks = {}
    for s in range(SLOTS):
        tasks.setdefault((s * 2) // 5, []).append(lambda s=s: start_kernel_copies(s))
    work = []
    for c in range(SLOTS // CHUNK):
        into = tasks.setdefault((25, 29)[c], []) if c < 2 else work
        into += [lambda c=c: split_kernel(c), lambda c=c: leaves(0, c), lambda c=c: multiply(0, c)]
    image = gather_and_multiply(0, tasks, work, [])
    buf[1, pl.ds(0, BLOCK), :] = image
    for c in range(SLOTS // CHUNK):
        given = kf.at[pl.ds(0, BLOCK), lanes(c)]
        pltpu.make_async_copy(given, given, k_send.at[c]).wait()

    def step(t, carry):
        par = lax.rem(t, 2)
        stages = sum_stages(loc, pieces.at[par], lines.at[par], full.at[par], ar_recv.at[par], ar_send)
        full_now[0] = full.at[par]
        tasks = {0: [lambda: local_gram(par), stages[0]]}
        for at, stage in zip((5, 13), stages[1:3]):
            tasks.setdefault(at, []).append(stage)
        product = [lambda c=c: multiply(par, c) for c in range(SLOTS // CHUNK)]
        panel = [lambda p=p: factor_panel(p) for p in range(PANELS)]
        for at, c in ((20, 0), (25, 1), (29, 2)):
            tasks.setdefault(at, []).append(product[c])
        work = [product[3], stages[3]] + panel[0:2]
        work += [lambda: leaves(par, 4), lambda: leaves(par, 5), product[4], product[5]] + panel[2:4]
        work += [lambda: leaves(par, 6), product[6]] + panel[4:6] + [lambda: leaves(par, 7), product[7]]
        image = gather_and_multiply(par, tasks, work, panel[6:])
        buf[1 - par, pl.ds(0, BLOCK), :] = exact_dot(image, inverse[...], (((1,), (1,)), ((), ())))
        return carry

    lax.fori_loop(1, ITERATIONS, step, 0)

    par = ITERATIONS % 2
    stages = sum_stages(loc, pieces.at[par], lines.at[par], full.at[par], ar_recv.at[par], ar_send)
    late = sum_stages(cloc, cpieces, clines, cfull, cr_recv, cr_send)
    full_now[0] = full.at[par]
    local_gram(par)
    stages[0]()
    last = buf[par, pl.ds(0, BLOCK), :]
    cloc[...] = exact_dot(last.T, test[...])
    late[0]()
    stages[1]()
    late[1]()
    stages[2]()
    late[2]()
    stages[3]()
    for p in range(PANELS):
        if p == PANELS // 2:
            late[3]()
        factor_panel(p)
    image_out[...] = buf[par, pl.ds(0, BLOCK), :]
    keep = lax.broadcasted_iota(jnp.int32, (BLOCK, TEST), 0) < cutoff[0]
    kept_out[...] = exact_dot(inverse[...], whole_sum(cfull)) * jnp.where(keep, 1.0, 0.0)


def project(image, inverse, kept, subspace, projection):
    block = exact_dot(image[...], inverse[...], (((1,), (1,)), ((), ())))
    subspace[...] = block
    projection[...] = exact_dot(block, kept[...])


def per_device(kernel_rows, start_block, test_kernel, cutoff):
    f32 = jnp.float32
    vmem = pl.BlockSpec(memory_space=pltpu.VMEM)
    dma = pltpu.SemaphoreType.DMA
    chunks = SLOTS // CHUNK
    narrow = jax.ShapeDtypeStruct((BLOCK, BLOCK), f32)
    broad = jax.ShapeDtypeStruct((BLOCK, TEST), f32)
    image, inverse, kept = pl.pallas_call(
        kernel,
        out_shape=(narrow, narrow, broad),
        in_specs=[pl.BlockSpec(memory_space=pl.ANY), vmem, vmem, pl.BlockSpec(memory_space=pltpu.SMEM)],
        out_specs=(vmem, vmem, vmem),
        scratch_shapes=[
            pltpu.VMEM((2, SLOTS * BLOCK, BLOCK), f32),
            pltpu.VMEM((2 * BLOCK, SLOTS * BLOCK), f32),
            pltpu.VMEM((4 * BLOCK, SLOTS * BLOCK), jnp.bfloat16),
            pltpu.VMEM((4 * BLOCK, 2 * BLOCK), f32),
            pltpu.VMEM((BLOCK, BLOCK), f32),
            pltpu.VMEM((8, BLOCK), f32),
            pltpu.VMEM((BLOCK, BLOCK), f32),
            pltpu.VMEM((2, TEAM, PIECE, BLOCK), f32),
            pltpu.VMEM((2, LINE, PIECE, BLOCK), f32),
            pltpu.VMEM((2, TEAM, PIECE, BLOCK), f32),
            pltpu.VMEM((BLOCK, TEST), f32),
            pltpu.VMEM((TEAM, PIECE, TEST), f32),
            pltpu.VMEM((LINE, PIECE, TEST), f32),
            pltpu.VMEM((TEAM, PIECE, TEST), f32),
            pltpu.VMEM((BLOCK, BLOCK), f32),
            pltpu.VMEM((2, BLOCK, BLOCK), f32),
            dma((2, SLOTS)),
            dma,
            dma((chunks,)),
            dma((chunks,)),
            dma((chunks,)),
            dma((2, 3)),
            dma((3,)),
            dma((3,)),
            dma((3,)),
            dma((2,)),
            dma,
        ],
        compiler_params=pltpu.CompilerParams(
            collective_id=0, has_side_effects=True, vmem_limit_bytes=56 * 1024 * 1024
        ),
        cost_estimate=pl.CostEstimate(
            flops=4 * 2 * 512 * 8192 * 256, bytes_accessed=16 * 2**20, transcendentals=0
        ),
        name="iterate",
    )(kernel_rows, start_block, test_kernel, cutoff)
    return pl.pallas_call(project, out_shape=(narrow, broad), name="project")(image, inverse, kept)


def solution(mesh):
    in_specs = (P(("row", "col"), None), P(("row", "col"), None), P(("row", "col"), None), P())
    out_specs = (P(("row", "col"), None), P(("row", "col"), None))
    return jax.shard_map(
        per_device, mesh=mesh, in_specs=in_specs, out_specs=out_specs, check_vma=False
    )
```

```python
import functools

import jax
import jax.numpy as jnp
from jax import lax
from jax.experimental import pallas as pl
from jax.experimental.pallas import tpu as pltpu
from jax.sharding import PartitionSpec as P

BLOCK = 128
TEST = 256
ITERATIONS = 4
RING = 4
SLOTS = RING**3
CHUNK = 8
TEAM = RING * RING
LINE = 2 * RING
PIECE = BLOCK // TEAM
GROUPED = BLOCK
MESH = pl.DeviceIdType.MESH
HIGHEST = lax.Precision.HIGHEST

TREE = (
    0, 49152, 196608, 65536, 28672, 16384, 12288, 69632, 4096, 114753, 131202, 53313,
    61506, 32836, 78019, 110852, 213317, 201224, 148106, 24840, 139719, 258828, 37579, 58059,
    127756, 250575, 119245, 45901, 177104, 208896, 20480, 245890, 82119, 98889, 8713, 74121,
    180878, 95118, 107472, 205905, 86479, 160914, 136273, 218193, 144276, 152722, 243029, 189717,
    103831, 169108, 222419, 230227, 226330, 194072, 255447, 91355, 124570, 42715, 165018, 156954,
    235100, 173852, 239193, 185948,
)
ORDER = [(code // 65536, code // 16384 % 4, code // 4096 % 4) for code in TREE]
PARENT = [code // 64 % 64 for code in TREE]
AFTER = [code % 64 for code in TREE]


def passed_on():
    height = [0] * SLOTS
    for s in reversed(range(1, SLOTS)):
        height[PARENT[s]] = max(height[PARENT[s]], height[s] + 1)
    sent = [[] for _ in TREE]
    for s in range(1, SLOTS):
        sent[AFTER[s]].append(s)
    for at, found in enumerate(sent):
        found.sort(key=lambda s: (PARENT[s] != at, -height[s]))
    return sent


SENT = passed_on()
INNER = len(set(PARENT))
GROUP = [s if s < INNER else max(INNER, s // CHUNK * CHUNK) for s in range(SLOTS)]


def exact_dot(a, b, dims=(((1,), (0,)), ((), ()))):
    return lax.dot_general(a, b, dims, precision=HIGHEST, preferred_element_type=jnp.float32)


def reciprocal(x):
    r = pl.reciprocal(x, approx=True)
    r = r * (2.0 - x * r)
    return r * (2.0 - x * r)


def inverse_root(x):
    r = lax.rsqrt(x)
    return r * (1.5 - 0.5 * x * r * r)


def eliminate(m, inverse, scale, scaled, panel):
    base = 8 * panel
    end = base // GROUPED * GROUPED + GROUPED
    wide = (8, BLOCK)
    lane = lax.broadcasted_iota(jnp.int32, wide, 1)
    within = (lane >= base) & (lane < base + 8)
    top = m[base : base + 8, :]
    raw = [jnp.broadcast_to(top[k : k + 1, :], wide) for k in range(8)]
    a = {
        (k, i): jnp.broadcast_to(raw[k][:, base + i : base + i + 1], wide) for k in range(8) for i in range(k, 8)
    }
    rows = [jnp.where(within, jnp.where(lane == base + k, 1.0, 0.0), raw[k]) for k in range(8)]
    over, factor = {}, {}
    for k in range(0, 8, 2):
        p, q, r = a[k, k], a[k, k + 1], a[k + 1, k + 1]
        over[k] = reciprocal(p * r - q * q)
        for i in range(k + 2, 8):
            factor[k, i] = (r * a[k, i] - q * a[k + 1, i]) * over[k]
            factor[k + 1, i] = (p * a[k + 1, i] - q * a[k, i]) * over[k]
            for j in range(i, 8):
                a[i, j] = a[i, j] - (factor[k, i] * a[k, j] + factor[k + 1, i] * a[k + 1, j])
            rows[i] = rows[i] - (factor[k, i] * rows[k] + factor[k + 1, i] * rows[k + 1])
    if base + 8 < end:
        solved = [None] * 8
        for k in range(0, 8, 2):
            p, q, r = a[k, k] * over[k], a[k, k + 1] * over[k], a[k + 1, k + 1] * over[k]
            solved[k] = r * rows[k] - q * rows[k + 1]
            solved[k + 1] = p * rows[k + 1] - q * rows[k]
        for k in (6, 4, 2):
            for i in range(k):
                solved[i] = solved[i] - (factor[i, k] * solved[k] + factor[i, k + 1] * solved[k + 1])
        for r in range(base + 8, end, 8):
            rest = m[r : r + 8, :]
            terms = [jnp.broadcast_to(rest[:, base + k : base + k + 1], wide) * solved[k] for k in range(8)]
            while len(terms) > 1:
                terms = [x + y for x, y in zip(terms[::2], terms[1::2])]
            m[r : r + 8, :] = jnp.where(within, 0.0, rest) - terms[0]
    for k in range(0, 8, 2):
        p, q = a[k, k], a[k, k + 1]
        r = inverse_root(p)
        ratio = p * over[k]
        first = rows[k] * r
        second = (rows[k + 1] - rows[k] * (q * r * r)) * (ratio * inverse_root(ratio))
        for j, done in ((base + k, first), (base + k + 1, second)):
            inverse[j : j + 1, :] = jnp.where(lane < base + 8, done * scale[...], 0.0)[0:1, :]
            if end < BLOCK:
                kept = (lane < base + 8) | (lane >= end)
                scaled[j % GROUPED : j % GROUPED + 1, :] = jnp.where(kept, done, 0.0)[0:1, :]
    if base + 8 == end and end < BLOCK:
        done = scaled[...]
        lanes = lax.broadcasted_iota(jnp.int32, (BLOCK - end, BLOCK), 1)
        rest = jnp.where((lanes >= end - GROUPED) & (lanes < end), 0.0, m[end:, :])
        m[end:, :] = rest - exact_dot(done.T[end:, :], done)


def load_scaled(value, m, scale):
    rows = lax.broadcasted_iota(jnp.int32, value.shape, 0)
    lanes = lax.broadcasted_iota(jnp.int32, value.shape, 1)
    diagonal = jnp.sum(jnp.where(rows == lanes, value, 0.0), axis=0, keepdims=True)
    over = 1.0 / jnp.broadcast_to(jnp.sum(diagonal, axis=1, keepdims=True), (8, BLOCK))
    m[...] = value * over[0:1, :]
    scale[...] = jnp.sqrt(over)


def kernel(
    kernel_hbm, start, test, cutoff, image_out, inverse, kept_out,
    buf, kf, khl, acc, m, scale, scaled, loc, pieces, lines, full, cloc, cpieces, clines, cfull, psend, precv,
    ag_recv, ag_send, k_local, k_recv, k_send, ar_recv, ar_send, cr_recv, cr_send, p_recv, p_send,
):
    row, col = lax.axis_index("row"), lax.axis_index("col")
    core = lax.rem(col, 2)
    here = (
        lax.rem(lax.div(col, 2), 2) * 2 + lax.rem(row, 2),
        lax.div(col, 4),
        lax.div(row, 2),
    )

    def device(x, y, z, c):
        return (z * 2 + lax.rem(x, 2), (y * 2 + lax.div(x, 2)) * 2 + c)

    def moved(by, core=core):
        return device(*[lax.rem(p + b, RING) for p, b in zip(here, by)], core)

    def hop(s):
        return tuple((a - b) % RING for a, b in zip(ORDER[s], ORDER[PARENT[s]]))

    sibling = device(*here, 1 - core)
    near = {hop(s) for s in range(1, SLOTS)}
    near |= {tuple(-b % RING for b in by) for by in near}
    near |= {(x, y, 0) for x in range(RING) for y in range(RING)} | {(0, 0, z) for z in range(RING)}
    greet = [moved(by) for by in sorted(near - {(0, 0, 0)})]
    greet += [moved((0, 0, z), 1 - core) for z in range(RING)]

    barrier = pltpu.get_barrier_semaphore()
    for other in greet:
        pl.semaphore_signal(barrier, inc=1, device_id=other, device_id_type=MESH)
    pl.semaphore_wait(barrier, len(greet))

    def remote(src, dst, send, recv, to):
        return pltpu.make_async_remote_copy(
            src_ref=src, dst_ref=dst, send_sem=send, recv_sem=recv, device_id=to, device_id_type=MESH
        )

    def block(par, s, count=1):
        return buf.at[par, pl.ds(s * BLOCK, count * BLOCK)]

    def forward(par, s):
        for child in SENT[s]:
            remote(
                block(par, PARENT[child]), block(par, child), ag_send, ag_recv.at[par, GROUP[child]], moved(hop(child))
            ).start()

    def arrived(par, group):
        whole = block(par, group, GROUP.count(group))
        pltpu.make_async_copy(whole, whole, ag_recv.at[par, group]).wait()

    def columns(s, c):
        x, y, z = [lax.rem(p + RING - d, RING) for p, d in zip(here, ORDER[s])]
        r, q = device(x, y, z, c)
        return pl.ds(pl.multiple_of((r * 16 + q) * BLOCK, BLOCK), BLOCK)

    def lanes(c):
        return pl.ds(c * CHUNK * BLOCK, CHUNK * BLOCK)

    def start_kernel_copies(s):
        c, there = s // CHUNK, pl.ds(s * BLOCK, BLOCK)
        remote(
            kernel_hbm.at[:, columns(s, 1 - core)], kf.at[pl.ds(BLOCK, BLOCK), there],
            k_send.at[c], k_recv.at[c], sibling,
        ).start()
        pltpu.make_async_copy(
            kernel_hbm.at[:, columns(s, core)], kf.at[pl.ds(0, BLOCK), there], k_local.at[c]
        ).start()

    def split_kernel(c):
        own, other = kf.at[pl.ds(0, BLOCK), lanes(c)], kf.at[pl.ds(BLOCK, BLOCK), lanes(c)]
        pltpu.make_async_copy(own, own, k_local.at[c]).wait()
        pltpu.make_async_copy(other, other, k_recv.at[c]).wait()
        value = kf[:, lanes(c)]
        high = value.astype(jnp.bfloat16)
        khl[0 : 2 * BLOCK, lanes(c)] = high
        khl[2 * BLOCK : 4 * BLOCK, lanes(c)] = (value - high.astype(jnp.float32)).astype(jnp.bfloat16)

    def leaves(par, c):
        for group in sorted(set(GROUP[c * CHUNK : (c + 1) * CHUNK])):
            if group >= INNER:
                arrived(par, group)

    def multiply(par, c):
        x = buf[par, pl.ds(c * CHUNK * BLOCK, CHUNK * BLOCK), :]
        high = x.astype(jnp.bfloat16)
        low = (x - high.astype(jnp.float32)).astype(jnp.bfloat16)
        term = jnp.dot(
            khl[:, lanes(c)], jnp.concatenate([high, low], axis=1), preferred_element_type=jnp.float32
        )
        if c == 0:
            acc[...] = term
        else:
            acc[...] += term

    def sum_stages(loc, pieces, line, full, recv, send):
        me = here[0] * RING + here[1]
        spot = here[2] * 2 + core

        def part(e):
            return pl.ds(pl.multiple_of(e * PIECE, PIECE), PIECE)

        def to_team(source, target, stage):
            for by in range(1, TEAM):
                e = lax.rem(me + by, TEAM)
                to = device(lax.div(e, RING), lax.rem(e, RING), here[2], core)
                remote(source(e), target.at[by - 1], send.at[stage], recv.at[stage], to).start()

        def await_all(target, count, semaphore):
            whole = target.at[pl.ds(0, count)]
            pltpu.make_async_copy(whole, whole, semaphore).wait()

        def tree_sum(got):
            while len(got) > 1:
                got = [x + y for x, y in zip(got[::2], got[1::2])]
            return got[0]

        def scatter():
            to_team(lambda e: loc.at[part(e)], pieces, 0)

        def exchange():
            await_all(pieces, TEAM - 1, recv.at[0])
            line[LINE - 1] = tree_sum([pieces[k] for k in range(TEAM - 1)] + [loc[part(me), :]])
            for by in range(1, LINE):
                f = lax.rem(spot + by, LINE)
                to = device(here[0], here[1], lax.div(f, 2), lax.rem(f, 2))
                remote(line.at[LINE - 1], line.at[by - 1], send.at[1], recv.at[1], to).start()

        def gather():
            await_all(line, LINE - 1, recv.at[1])
            full[TEAM - 1] = tree_sum([line[lax.rem(spot - f + 2 * LINE - 1, LINE)] for f in range(LINE)])
            to_team(lambda e: full.at[TEAM - 1], full, 2)

        def finish():
            await_all(full, TEAM - 1, recv.at[2])
            await_all(pieces, TEAM - 1, send.at[0])
            await_all(line, LINE - 1, send.at[1])
            await_all(full, TEAM - 1, send.at[2])

        return [scatter, exchange, gather, finish]

    def whole_sum(full):
        me = here[0] * RING + here[1]
        return jnp.concatenate([full[lax.rem(me - e + 2 * TEAM - 1, TEAM)] for e in range(TEAM)], axis=0)

    def factor_panel(p):
        if p == 0:
            load_scaled(whole_sum(full_now[0]), m, scale)
        eliminate(m, inverse, scale, scaled, p)

    full_now = [None]

    def gather_and_multiply(par, tasks, work, beside):
        forward(par, 0)
        for s in range(INNER):
            if s:
                arrived(par, s)
                forward(par, s)
            for task in tasks.get(s, ()):
                task()
        for task in work:
            task()
        value = acc[...]
        value = value[:, :BLOCK] + value[:, BLOCK:]
        value = value[: 2 * BLOCK] + value[2 * BLOCK :]
        psend[...] = value[BLOCK:]
        copy = remote(psend, precv.at[par], p_send, p_recv.at[par], sibling)
        copy.start()
        for task in beside:
            task()
        whole = block(par, 1, SLOTS - 1)
        pltpu.make_async_copy(whole, whole, ag_send).wait()
        copy.wait()
        return value[:BLOCK] + precv[par]

    def local_gram(par):
        y = buf[par, pl.ds(0, BLOCK), :]
        loc[...] = exact_dot(y.T, y)

    buf[0, pl.ds(0, BLOCK), :] = start[...]
    tasks = {}
    for s in range(SLOTS):
        tasks.setdefault((s * 2) // 5, []).append(lambda s=s: start_kernel_copies(s))
    work = []
    for c in range(SLOTS // CHUNK):
        into = tasks.setdefault((17, 23)[c], []) if c < 2 else work
        into += [lambda c=c: split_kernel(c), lambda c=c: leaves(0, c), lambda c=c: multiply(0, c)]
    image = gather_and_multiply(0, tasks, work, [])
    buf[1, pl.ds(0, BLOCK), :] = image
    for c in range(SLOTS // CHUNK):
        given = kf.at[pl.ds(0, BLOCK), lanes(c)]
        pltpu.make_async_copy(given, given, k_send.at[c]).wait()

    def step(t, carry):
        par = lax.rem(t, 2)
        stages = sum_stages(loc, pieces.at[par], lines.at[par], full.at[par], ar_recv.at[par], ar_send)
        full_now[0] = full.at[par]
        tasks = {0: [lambda: local_gram(par), stages[0]]}
        for at, stage in zip((3, 12), stages[1:3]):
            tasks.setdefault(at, []).append(stage)
        product = [lambda c=c: multiply(par, c) for c in range(SLOTS // CHUNK)]
        panel = [lambda p=p: factor_panel(p) for p in range(16)]
        for at, c in ((13, 0), (17, 1), (23, 2)):
            tasks.setdefault(at, []).append(product[c])
        work = [stages[3]] + panel[0:4] + [lambda: leaves(par, 3), product[3]] + panel[4:8]
        work += [lambda: leaves(par, 4), product[4]] + panel[8:12] + [lambda: leaves(par, 5), product[5]]
        work += [lambda: leaves(par, 6), product[6], lambda: leaves(par, 7), product[7]]
        image = gather_and_multiply(par, tasks, work, panel[12:])
        buf[1 - par, pl.ds(0, BLOCK), :] = exact_dot(image, inverse[...], (((1,), (1,)), ((), ())))
        return carry

    lax.fori_loop(1, ITERATIONS, step, 0)

    par = ITERATIONS % 2
    stages = sum_stages(loc, pieces.at[par], lines.at[par], full.at[par], ar_recv.at[par], ar_send)
    late = sum_stages(cloc, cpieces, clines, cfull, cr_recv, cr_send)
    full_now[0] = full.at[par]
    local_gram(par)
    stages[0]()
    last = buf[par, pl.ds(0, BLOCK), :]
    cloc[...] = exact_dot(last.T, test[...])
    late[0]()
    stages[1]()
    late[1]()
    stages[2]()
    late[2]()
    stages[3]()
    for p in range(16):
        if p == 8:
            late[3]()
        factor_panel(p)
    image_out[...] = buf[par, pl.ds(0, BLOCK), :]
    keep = lax.broadcasted_iota(jnp.int32, (BLOCK, TEST), 0) < cutoff[0]
    kept_out[...] = exact_dot(inverse[...], whole_sum(cfull)) * jnp.where(keep, 1.0, 0.0)


def project(image, inverse, kept, subspace, projection):
    block = exact_dot(image[...], inverse[...], (((1,), (1,)), ((), ())))
    subspace[...] = block
    projection[...] = exact_dot(block, kept[...])


def per_device(kernel_rows, start_block, test_kernel, cutoff):
    f32 = jnp.float32
    vmem = pl.BlockSpec(memory_space=pltpu.VMEM)
    dma = pltpu.SemaphoreType.DMA
    chunks = SLOTS // CHUNK
    narrow = jax.ShapeDtypeStruct((BLOCK, BLOCK), f32)
    broad = jax.ShapeDtypeStruct((BLOCK, TEST), f32)
    image, inverse, kept = pl.pallas_call(
        kernel,
        out_shape=(narrow, narrow, broad),
        in_specs=[pl.BlockSpec(memory_space=pl.ANY), vmem, vmem, pl.BlockSpec(memory_space=pltpu.SMEM)],
        out_specs=(vmem, vmem, vmem),
        scratch_shapes=[
            pltpu.VMEM((2, SLOTS * BLOCK, BLOCK), f32),
            pltpu.VMEM((2 * BLOCK, SLOTS * BLOCK), f32),
            pltpu.VMEM((4 * BLOCK, SLOTS * BLOCK), jnp.bfloat16),
            pltpu.VMEM((4 * BLOCK, 2 * BLOCK), f32),
            pltpu.VMEM((BLOCK, BLOCK), f32),
            pltpu.VMEM((8, BLOCK), f32),
            pltpu.VMEM((GROUPED, BLOCK), f32),
            pltpu.VMEM((BLOCK, BLOCK), f32),
            pltpu.VMEM((2, TEAM, PIECE, BLOCK), f32),
            pltpu.VMEM((2, LINE, PIECE, BLOCK), f32),
            pltpu.VMEM((2, TEAM, PIECE, BLOCK), f32),
            pltpu.VMEM((BLOCK, TEST), f32),
            pltpu.VMEM((TEAM, PIECE, TEST), f32),
            pltpu.VMEM((LINE, PIECE, TEST), f32),
            pltpu.VMEM((TEAM, PIECE, TEST), f32),
            pltpu.VMEM((BLOCK, BLOCK), f32),
            pltpu.VMEM((2, BLOCK, BLOCK), f32),
            dma((2, SLOTS)),
            dma,
            dma((chunks,)),
            dma((chunks,)),
            dma((chunks,)),
            dma((2, 3)),
            dma((3,)),
            dma((3,)),
            dma((3,)),
            dma((2,)),
            dma,
        ],
        compiler_params=pltpu.CompilerParams(
            collective_id=0, has_side_effects=True, vmem_limit_bytes=56 * 1024 * 1024
        ),
        cost_estimate=pl.CostEstimate(
            flops=4 * 2 * 512 * 8192 * 256, bytes_accessed=16 * 2**20, transcendentals=0
        ),
        name="iterate",
    )(kernel_rows, start_block, test_kernel, cutoff)
    return pl.pallas_call(project, out_shape=(narrow, broad), name="project")(image, inverse, kept)


def solution(mesh):
    in_specs = (P(("row", "col"), None), P(("row", "col"), None), P(("row", "col"), None), P())
    out_specs = (P(("row", "col"), None), P(("row", "col"), None))
    return jax.shard_map(
        per_device, mesh=mesh, in_specs=in_specs, out_specs=out_specs, check_vma=False
    )
```

```python
import functools

import jax
import jax.numpy as jnp
from jax import lax
from jax.experimental import pallas as pl
from jax.experimental.pallas import tpu as pltpu
from jax.sharding import PartitionSpec as P

BLOCK = 128
TEST = 256
ITERATIONS = 4
RING = 4
SLOTS = RING**3
CHUNK = 8
PARTS = 4
TEAM = RING * RING
LINE = 2 * RING
PIECE = BLOCK // TEAM
GROUPED = BLOCK
MESH = pl.DeviceIdType.MESH
HIGHEST = lax.Precision.HIGHEST

TREE = (
    0, 49152, 196608, 65536, 28672, 16384, 12288, 69632, 4096, 114753, 131202, 53313,
    61506, 32836, 78019, 110852, 213317, 201224, 148106, 24840, 139719, 258828, 37579, 58059,
    127756, 250575, 119245, 45901, 177104, 208896, 20480, 245890, 82119, 98889, 8713, 74121,
    180878, 95118, 107472, 205905, 86479, 160914, 136273, 218193, 144276, 152722, 243029, 189717,
    103831, 169108, 222419, 230227, 226330, 194072, 255447, 91355, 124570, 42715, 165018, 156954,
    235100, 173852, 239193, 185948,
)
ORDER = [(code // 65536, code // 16384 % 4, code // 4096 % 4) for code in TREE]
PARENT = [code // 64 % 64 for code in TREE]
AFTER = [code % 64 for code in TREE]


def passed_on():
    height = [0] * SLOTS
    for s in reversed(range(1, SLOTS)):
        height[PARENT[s]] = max(height[PARENT[s]], height[s] + 1)
    sent = [[] for _ in TREE]
    for s in range(1, SLOTS):
        sent[AFTER[s]].append(s)
    for at, found in enumerate(sent):
        found.sort(key=lambda s: (PARENT[s] != at, -height[s]))
    return sent


SENT = passed_on()
INNER = len(set(PARENT))
GROUP = [s if s < INNER else max(INNER, s // CHUNK * CHUNK) for s in range(SLOTS)]


def exact_dot(a, b, dims=(((1,), (0,)), ((), ()))):
    return lax.dot_general(a, b, dims, precision=HIGHEST, preferred_element_type=jnp.float32)


def reciprocal(x):
    r = pl.reciprocal(x, approx=True)
    r = r * (2.0 - x * r)
    return r * (2.0 - x * r)


def inverse_root(x):
    r = lax.rsqrt(x)
    return r * (1.5 - 0.5 * x * r * r)


def eliminate(m, inverse, scale, scaled, panel):
    base = 8 * panel
    end = base // GROUPED * GROUPED + GROUPED
    wide = (8, BLOCK)
    lane = lax.broadcasted_iota(jnp.int32, wide, 1)
    within = (lane >= base) & (lane < base + 8)
    top = m[base : base + 8, :]
    raw = [jnp.broadcast_to(top[k : k + 1, :], wide) for k in range(8)]
    a = {
        (k, i): jnp.broadcast_to(raw[k][:, base + i : base + i + 1], wide) for k in range(8) for i in range(k, 8)
    }
    rows = [jnp.where(within, jnp.where(lane == base + k, 1.0, 0.0), raw[k]) for k in range(8)]
    over, factor = {}, {}
    for k in range(0, 8, 2):
        p, q, r = a[k, k], a[k, k + 1], a[k + 1, k + 1]
        over[k] = reciprocal(p * r - q * q)
        for i in range(k + 2, 8):
            factor[k, i] = (r * a[k, i] - q * a[k + 1, i]) * over[k]
            factor[k + 1, i] = (p * a[k + 1, i] - q * a[k, i]) * over[k]
            for j in range(i, 8):
                a[i, j] = a[i, j] - (factor[k, i] * a[k, j] + factor[k + 1, i] * a[k + 1, j])
            rows[i] = rows[i] - (factor[k, i] * rows[k] + factor[k + 1, i] * rows[k + 1])
    if base + 8 < end:
        solved = [None] * 8
        for k in range(0, 8, 2):
            p, q, r = a[k, k] * over[k], a[k, k + 1] * over[k], a[k + 1, k + 1] * over[k]
            solved[k] = r * rows[k] - q * rows[k + 1]
            solved[k + 1] = p * rows[k + 1] - q * rows[k]
        for k in (6, 4, 2):
            for i in range(k):
                solved[i] = solved[i] - (factor[i, k] * solved[k] + factor[i, k + 1] * solved[k + 1])
        for r in range(base + 8, end, 8):
            rest = m[r : r + 8, :]
            terms = [jnp.broadcast_to(rest[:, base + k : base + k + 1], wide) * solved[k] for k in range(8)]
            while len(terms) > 1:
                terms = [x + y for x, y in zip(terms[::2], terms[1::2])]
            m[r : r + 8, :] = jnp.where(within, 0.0, rest) - terms[0]
    for k in range(0, 8, 2):
        p, q = a[k, k], a[k, k + 1]
        r = inverse_root(p)
        ratio = p * over[k]
        first = rows[k] * r
        second = (rows[k + 1] - rows[k] * (q * r * r)) * (ratio * inverse_root(ratio))
        for j, done in ((base + k, first), (base + k + 1, second)):
            inverse[j : j + 1, :] = jnp.where(lane < base + 8, done * scale[...], 0.0)[0:1, :]
            if end < BLOCK:
                kept = (lane < base + 8) | (lane >= end)
                scaled[j % GROUPED : j % GROUPED + 1, :] = jnp.where(kept, done, 0.0)[0:1, :]
    if base + 8 == end and end < BLOCK:
        done = scaled[...]
        lanes = lax.broadcasted_iota(jnp.int32, (BLOCK - end, BLOCK), 1)
        rest = jnp.where((lanes >= end - GROUPED) & (lanes < end), 0.0, m[end:, :])
        m[end:, :] = rest - exact_dot(done.T[end:, :], done)


def load_scaled(value, m, scale):
    rows = lax.broadcasted_iota(jnp.int32, value.shape, 0)
    lanes = lax.broadcasted_iota(jnp.int32, value.shape, 1)
    diagonal = jnp.sum(jnp.where(rows == lanes, value, 0.0), axis=0, keepdims=True)
    over = 1.0 / jnp.broadcast_to(jnp.sum(diagonal, axis=1, keepdims=True), (8, BLOCK))
    m[...] = value * over[0:1, :]
    scale[...] = jnp.sqrt(over)


def kernel(
    kernel_hbm, start, test, cutoff, image_out, inverse, kept_out,
    buf, kall, kgive, kget, khl, acc, m, scale, scaled, loc, pieces, lines, full, cloc, cpieces, clines, cfull, psend, precv,
    ag_recv, ag_send, k_local, k_recv, k_send, ar_recv, ar_send, cr_recv, cr_send, p_recv, p_send,
):
    row, col = lax.axis_index("row"), lax.axis_index("col")
    core = lax.rem(col, 2)
    here = (
        lax.rem(lax.div(col, 2), 2) * 2 + lax.rem(row, 2),
        lax.div(col, 4),
        lax.div(row, 2),
    )

    def device(x, y, z, c):
        return (z * 2 + lax.rem(x, 2), (y * 2 + lax.div(x, 2)) * 2 + c)

    def moved(by, core=core):
        return device(*[lax.rem(p + b, RING) for p, b in zip(here, by)], core)

    def hop(s):
        return tuple((a - b) % RING for a, b in zip(ORDER[s], ORDER[PARENT[s]]))

    sibling = device(*here, 1 - core)
    near = {hop(s) for s in range(1, SLOTS)}
    near |= {tuple(-b % RING for b in by) for by in near}
    near |= {(x, y, 0) for x in range(RING) for y in range(RING)} | {(0, 0, z) for z in range(RING)}
    greet = [moved(by) for by in sorted(near - {(0, 0, 0)})]
    greet += [moved((0, 0, z), 1 - core) for z in range(RING)]

    pltpu.make_async_copy(kernel_hbm, kall, k_local).start()
    barrier = pltpu.get_barrier_semaphore()
    for other in greet:
        pl.semaphore_signal(barrier, inc=1, device_id=other, device_id_type=MESH)
    pl.semaphore_wait(barrier, len(greet))

    def remote(src, dst, send, recv, to):
        return pltpu.make_async_remote_copy(
            src_ref=src, dst_ref=dst, send_sem=send, recv_sem=recv, device_id=to, device_id_type=MESH
        )

    def block(par, s, count=1):
        return buf.at[par, pl.ds(s * BLOCK, count * BLOCK)]

    def forward(par, s):
        for child in SENT[s]:
            remote(
                block(par, PARENT[child]), block(par, child), ag_send, ag_recv.at[par, GROUP[child]], moved(hop(child))
            ).start()

    def arrived(par, group):
        whole = block(par, group, GROUP.count(group))
        pltpu.make_async_copy(whole, whole, ag_recv.at[par, group]).wait()

    def rank(s):
        x, y, z = [lax.rem(p + RING - d, RING) for p, d in zip(here, ORDER[s])]
        return (z * 2 + lax.rem(x, 2)) * 8 + y * 2 + lax.div(x, 2)

    def columns(j):
        return pl.ds(pl.multiple_of(j * BLOCK, BLOCK), BLOCK)

    def lanes(c):
        return pl.ds(c * CHUNK * BLOCK, CHUNK * BLOCK)

    def part_of_given(c):
        return pl.ds(c * (SLOTS // PARTS) * BLOCK, (SLOTS // PARTS) * BLOCK)

    def give_kernel():
        pltpu.make_async_copy(kernel_hbm, kall, k_local).wait()
        for c in range(PARTS):
            for j in range(c * (SLOTS // PARTS), (c + 1) * (SLOTS // PARTS)):
                kgive[:, j * BLOCK : (j + 1) * BLOCK] = kall[:, columns(2 * j + 1 - core)]
            there = part_of_given(c)
            remote(kgive.at[:, there], kget.at[:, there], k_send.at[c], k_recv.at[c], sibling).start()

    def given_kernel(c):
        there = part_of_given(c)
        remote(kgive.at[:, there], kget.at[:, there], k_send.at[c], k_recv.at[c], sibling).wait()

    def split_kernel(c, own):
        for s in range(c * CHUNK, (c + 1) * CHUNK):
            j = rank(s)
            value = kall[:, columns(2 * j + core)] if own else kget[:, columns(j)]
            high = value.astype(jnp.bfloat16)
            low = (value - high.astype(jnp.float32)).astype(jnp.bfloat16)
            first, there = 0 if own else BLOCK, slice(s * BLOCK, (s + 1) * BLOCK)
            khl[first : first + BLOCK, there] = high
            khl[2 * BLOCK + first : 3 * BLOCK + first, there] = low

    def leaves(par, c):
        for group in sorted(set(GROUP[c * CHUNK : (c + 1) * CHUNK])):
            if group >= INNER:
                arrived(par, group)

    def multiply(par, c):
        x = buf[par, pl.ds(c * CHUNK * BLOCK, CHUNK * BLOCK), :]
        high = x.astype(jnp.bfloat16)
        low = (x - high.astype(jnp.float32)).astype(jnp.bfloat16)
        term = jnp.dot(
            khl[:, lanes(c)], jnp.concatenate([high, low], axis=1), preferred_element_type=jnp.float32
        )
        if c == 0:
            acc[...] = term
        else:
            acc[...] += term

    def sum_stages(loc, pieces, line, full, recv, send):
        me = here[0] * RING + here[1]
        spot = here[2] * 2 + core

        def part(e):
            return pl.ds(pl.multiple_of(e * PIECE, PIECE), PIECE)

        def to_team(source, target, stage):
            for by in range(1, TEAM):
                e = lax.rem(me + by, TEAM)
                to = device(lax.div(e, RING), lax.rem(e, RING), here[2], core)
                remote(source(e), target.at[by - 1], send.at[stage], recv.at[stage], to).start()

        def await_all(target, count, semaphore):
            whole = target.at[pl.ds(0, count)]
            pltpu.make_async_copy(whole, whole, semaphore).wait()

        def tree_sum(got):
            while len(got) > 1:
                got = [x + y for x, y in zip(got[::2], got[1::2])]
            return got[0]

        def scatter():
            to_team(lambda e: loc.at[part(e)], pieces, 0)

        def exchange():
            await_all(pieces, TEAM - 1, recv.at[0])
            line[LINE - 1] = tree_sum([pieces[k] for k in range(TEAM - 1)] + [loc[part(me), :]])
            for by in range(1, LINE):
                f = lax.rem(spot + by, LINE)
                to = device(here[0], here[1], lax.div(f, 2), lax.rem(f, 2))
                remote(line.at[LINE - 1], line.at[by - 1], send.at[1], recv.at[1], to).start()

        def gather():
            await_all(line, LINE - 1, recv.at[1])
            full[TEAM - 1] = tree_sum([line[lax.rem(spot - f + 2 * LINE - 1, LINE)] for f in range(LINE)])
            to_team(lambda e: full.at[TEAM - 1], full, 2)

        def finish():
            await_all(full, TEAM - 1, recv.at[2])
            await_all(pieces, TEAM - 1, send.at[0])
            await_all(line, LINE - 1, send.at[1])
            await_all(full, TEAM - 1, send.at[2])

        return [scatter, exchange, gather, finish]

    def whole_sum(full):
        me = here[0] * RING + here[1]
        return jnp.concatenate([full[lax.rem(me - e + 2 * TEAM - 1, TEAM)] for e in range(TEAM)], axis=0)

    def factor_panel(p):
        if p == 0:
            load_scaled(whole_sum(full_now[0]), m, scale)
        eliminate(m, inverse, scale, scaled, p)

    full_now = [None]

    def gather_and_multiply(par, tasks, work, beside):
        forward(par, 0)
        for s in range(INNER):
            if s:
                arrived(par, s)
                forward(par, s)
            for task in tasks.get(s, ()):
                task()
        for task in work:
            task()
        value = acc[...]
        value = value[:, :BLOCK] + value[:, BLOCK:]
        value = value[: 2 * BLOCK] + value[2 * BLOCK :]
        psend[...] = value[BLOCK:]
        copy = remote(psend, precv.at[par], p_send, p_recv.at[par], sibling)
        copy.start()
        for task in beside:
            task()
        whole = block(par, 1, SLOTS - 1)
        pltpu.make_async_copy(whole, whole, ag_send).wait()
        copy.wait()
        return value[:BLOCK] + precv[par]

    def local_gram(par):
        y = buf[par, pl.ds(0, BLOCK), :]
        loc[...] = exact_dot(y.T, y)

    buf[0, pl.ds(0, BLOCK), :] = start[...]
    tasks = {0: [give_kernel]}
    work = [lambda c=c: given_kernel(c) for c in range(PARTS)]
    for c in range(SLOTS // CHUNK):
        tasks[10 + 2 * c] = [lambda c=c: split_kernel(c, True)]
        work += [lambda c=c: split_kernel(c, False), lambda c=c: leaves(0, c), lambda c=c: multiply(0, c)]
    image = gather_and_multiply(0, tasks, work, [])
    buf[1, pl.ds(0, BLOCK), :] = image

    def step(t, carry):
        par = lax.rem(t, 2)
        stages = sum_stages(loc, pieces.at[par], lines.at[par], full.at[par], ar_recv.at[par], ar_send)
        full_now[0] = full.at[par]
        tasks = {0: [lambda: local_gram(par), stages[0]]}
        for at, stage in zip((3, 12), stages[1:3]):
            tasks.setdefault(at, []).append(stage)
        product = [lambda c=c: multiply(par, c) for c in range(SLOTS // CHUNK)]
        panel = [lambda p=p: factor_panel(p) for p in range(16)]
        for at, c in ((13, 0), (17, 1), (23, 2)):
            tasks.setdefault(at, []).append(product[c])
        work = [stages[3]] + panel[0:4] + [lambda: leaves(par, 3), product[3]] + panel[4:8]
        work += [lambda: leaves(par, 4), product[4]] + panel[8:12] + [lambda: leaves(par, 5), product[5]]
        work += [lambda: leaves(par, 6), product[6], lambda: leaves(par, 7), product[7]]
        image = gather_and_multiply(par, tasks, work, panel[12:])
        buf[1 - par, pl.ds(0, BLOCK), :] = exact_dot(image, inverse[...], (((1,), (1,)), ((), ())))
        return carry

    lax.fori_loop(1, ITERATIONS, step, 0)

    par = ITERATIONS % 2
    stages = sum_stages(loc, pieces.at[par], lines.at[par], full.at[par], ar_recv.at[par], ar_send)
    late = sum_stages(cloc, cpieces, clines, cfull, cr_recv, cr_send)
    full_now[0] = full.at[par]
    local_gram(par)
    stages[0]()
    last = buf[par, pl.ds(0, BLOCK), :]
    cloc[...] = exact_dot(last.T, test[...])
    late[0]()
    stages[1]()
    late[1]()
    stages[2]()
    late[2]()
    stages[3]()
    for p in range(16):
        if p == 8:
            late[3]()
        factor_panel(p)
    image_out[...] = buf[par, pl.ds(0, BLOCK), :]
    keep = lax.broadcasted_iota(jnp.int32, (BLOCK, TEST), 0) < cutoff[0]
    kept_out[...] = exact_dot(inverse[...], whole_sum(cfull)) * jnp.where(keep, 1.0, 0.0)


def project(image, inverse, kept, subspace, projection):
    block = exact_dot(image[...], inverse[...], (((1,), (1,)), ((), ())))
    subspace[...] = block
    projection[...] = exact_dot(block, kept[...])


def per_device(kernel_rows, start_block, test_kernel, cutoff):
    f32 = jnp.float32
    vmem = pl.BlockSpec(memory_space=pltpu.VMEM)
    dma = pltpu.SemaphoreType.DMA
    narrow = jax.ShapeDtypeStruct((BLOCK, BLOCK), f32)
    broad = jax.ShapeDtypeStruct((BLOCK, TEST), f32)
    image, inverse, kept = pl.pallas_call(
        kernel,
        out_shape=(narrow, narrow, broad),
        in_specs=[pl.BlockSpec(memory_space=pl.ANY), vmem, vmem, pl.BlockSpec(memory_space=pltpu.SMEM)],
        out_specs=(vmem, vmem, vmem),
        scratch_shapes=[
            pltpu.VMEM((2, SLOTS * BLOCK, BLOCK), f32),
            pltpu.VMEM((BLOCK, 2 * SLOTS * BLOCK), f32),
            pltpu.VMEM((BLOCK, SLOTS * BLOCK), f32),
            pltpu.VMEM((BLOCK, SLOTS * BLOCK), f32),
            pltpu.VMEM((4 * BLOCK, SLOTS * BLOCK), jnp.bfloat16),
            pltpu.VMEM((4 * BLOCK, 2 * BLOCK), f32),
            pltpu.VMEM((BLOCK, BLOCK), f32),
            pltpu.VMEM((8, BLOCK), f32),
            pltpu.VMEM((GROUPED, BLOCK), f32),
            pltpu.VMEM((BLOCK, BLOCK), f32),
            pltpu.VMEM((2, TEAM, PIECE, BLOCK), f32),
            pltpu.VMEM((2, LINE, PIECE, BLOCK), f32),
            pltpu.VMEM((2, TEAM, PIECE, BLOCK), f32),
            pltpu.VMEM((BLOCK, TEST), f32),
            pltpu.VMEM((TEAM, PIECE, TEST), f32),
            pltpu.VMEM((LINE, PIECE, TEST), f32),
            pltpu.VMEM((TEAM, PIECE, TEST), f32),
            pltpu.VMEM((BLOCK, BLOCK), f32),
            pltpu.VMEM((2, BLOCK, BLOCK), f32),
            dma((2, SLOTS)),
            dma,
            dma,
            dma((PARTS,)),
            dma((PARTS,)),
            dma((2, 3)),
            dma((3,)),
            dma((3,)),
            dma((3,)),
            dma((2,)),
            dma,
        ],
        compiler_params=pltpu.CompilerParams(
            collective_id=0, has_side_effects=True, vmem_limit_bytes=56 * 1024 * 1024
        ),
        cost_estimate=pl.CostEstimate(
            flops=4 * 2 * 512 * 8192 * 256, bytes_accessed=16 * 2**20, transcendentals=0
        ),
        name="iterate",
    )(kernel_rows, start_block, test_kernel, cutoff)
    return pl.pallas_call(project, out_shape=(narrow, broad), name="project")(image, inverse, kept)


def solution(mesh):
    in_specs = (P(("row", "col"), None), P(("row", "col"), None), P(("row", "col"), None), P())
    out_specs = (P(("row", "col"), None), P(("row", "col"), None))
    return jax.shard_map(
        per_device, mesh=mesh, in_specs=in_specs, out_specs=out_specs, check_vma=False
    )
```

```python
import functools

import jax
import jax.numpy as jnp
from jax import lax
from jax.experimental import pallas as pl
from jax.experimental.pallas import tpu as pltpu
from jax.sharding import PartitionSpec as P

BLOCK = 128
TEST = 256
ITERATIONS = 4
RING = 4
SLOTS = RING**3
CHUNK = 8
PARTS = 4
TEAM = RING * RING
LINE = 2 * RING
PIECE = BLOCK // TEAM
GROUPED = BLOCK
MESH = pl.DeviceIdType.MESH
HIGHEST = lax.Precision.HIGHEST

TREE = (
    0, 49152, 196608, 65536, 28672, 16384, 12288, 69632, 4096, 114753, 131202, 53313,
    61506, 32836, 78019, 110852, 213317, 201224, 148106, 24840, 139719, 258828, 37579, 58059,
    127756, 250575, 119245, 45901, 177104, 208896, 20480, 245890, 82119, 98889, 8713, 74121,
    180878, 95118, 107472, 205905, 86479, 160914, 136273, 218193, 144276, 152722, 243029, 189717,
    103831, 169108, 222419, 230227, 226330, 194072, 255447, 91355, 124570, 42715, 165018, 156954,
    235100, 173852, 239193, 185948,
)
ORDER = [(code // 65536, code // 16384 % 4, code // 4096 % 4) for code in TREE]
PARENT = [code // 64 % 64 for code in TREE]
AFTER = [code % 64 for code in TREE]


def passed_on():
    height = [0] * SLOTS
    for s in reversed(range(1, SLOTS)):
        height[PARENT[s]] = max(height[PARENT[s]], height[s] + 1)
    sent = [[] for _ in TREE]
    for s in range(1, SLOTS):
        sent[AFTER[s]].append(s)
    for at, found in enumerate(sent):
        found.sort(key=lambda s: (PARENT[s] != at, -height[s]))
    return sent


SENT = passed_on()
INNER = len(set(PARENT))
GROUP = [s if s < INNER else max(INNER, s // CHUNK * CHUNK) for s in range(SLOTS)]


def exact_dot(a, b, dims=(((1,), (0,)), ((), ()))):
    return lax.dot_general(a, b, dims, precision=HIGHEST, preferred_element_type=jnp.float32)


def reciprocal(x):
    r = pl.reciprocal(x, approx=True)
    r = r * (2.0 - x * r)
    return r * (2.0 - x * r)


def inverse_root(x):
    r = lax.rsqrt(x)
    return r * (1.5 - 0.5 * x * r * r)


def eliminate(m, inverse, scale, scaled, panel):
    base = 8 * panel
    end = base // GROUPED * GROUPED + GROUPED
    wide = (8, BLOCK)
    lane = lax.broadcasted_iota(jnp.int32, wide, 1)
    within = (lane >= base) & (lane < base + 8)
    top = m[base : base + 8, :]
    raw = [jnp.broadcast_to(top[k : k + 1, :], wide) for k in range(8)]
    a = {
        (k, i): jnp.broadcast_to(raw[k][:, base + i : base + i + 1], wide) for k in range(8) for i in range(k, 8)
    }
    rows = [jnp.where(within, jnp.where(lane == base + k, 1.0, 0.0), raw[k]) for k in range(8)]
    over, factor = {}, {}
    for k in range(0, 8, 2):
        p, q, r = a[k, k], a[k, k + 1], a[k + 1, k + 1]
        over[k] = reciprocal(p * r - q * q)
        for i in range(k + 2, 8):
            factor[k, i] = (r * a[k, i] - q * a[k + 1, i]) * over[k]
            factor[k + 1, i] = (p * a[k + 1, i] - q * a[k, i]) * over[k]
            for j in range(i, 8):
                a[i, j] = a[i, j] - (factor[k, i] * a[k, j] + factor[k + 1, i] * a[k + 1, j])
            rows[i] = rows[i] - (factor[k, i] * rows[k] + factor[k + 1, i] * rows[k + 1])
    if base + 8 < end:
        solved = [None] * 8
        for k in range(0, 8, 2):
            p, q, r = a[k, k] * over[k], a[k, k + 1] * over[k], a[k + 1, k + 1] * over[k]
            solved[k] = r * rows[k] - q * rows[k + 1]
            solved[k + 1] = p * rows[k + 1] - q * rows[k]
        for k in (6, 4, 2):
            for i in range(k):
                solved[i] = solved[i] - (factor[i, k] * solved[k] + factor[i, k + 1] * solved[k + 1])
        for r in range(base + 8, end, 8):
            rest = m[r : r + 8, :]
            terms = [jnp.broadcast_to(rest[:, base + k : base + k + 1], wide) * solved[k] for k in range(8)]
            while len(terms) > 1:
                terms = [x + y for x, y in zip(terms[::2], terms[1::2])]
            m[r : r + 8, :] = jnp.where(within, 0.0, rest) - terms[0]
    for k in range(0, 8, 2):
        p, q = a[k, k], a[k, k + 1]
        r = inverse_root(p)
        ratio = p * over[k]
        first = rows[k] * r
        second = (rows[k + 1] - rows[k] * (q * r * r)) * (ratio * inverse_root(ratio))
        for j, done in ((base + k, first), (base + k + 1, second)):
            inverse[j : j + 1, :] = jnp.where(lane < base + 8, done * scale[...], 0.0)[0:1, :]
            if end < BLOCK:
                kept = (lane < base + 8) | (lane >= end)
                scaled[j % GROUPED : j % GROUPED + 1, :] = jnp.where(kept, done, 0.0)[0:1, :]
    if base + 8 == end and end < BLOCK:
        done = scaled[...]
        lanes = lax.broadcasted_iota(jnp.int32, (BLOCK - end, BLOCK), 1)
        rest = jnp.where((lanes >= end - GROUPED) & (lanes < end), 0.0, m[end:, :])
        m[end:, :] = rest - exact_dot(done.T[end:, :], done)


def load_scaled(value, m, scale):
    rows = lax.broadcasted_iota(jnp.int32, value.shape, 0)
    lanes = lax.broadcasted_iota(jnp.int32, value.shape, 1)
    diagonal = jnp.sum(jnp.where(rows == lanes, value, 0.0), axis=0, keepdims=True)
    over = 1.0 / jnp.broadcast_to(jnp.sum(diagonal, axis=1, keepdims=True), (8, BLOCK))
    m[...] = value * over[0:1, :]
    scale[...] = jnp.sqrt(over)


def kernel(
    kernel_hbm, start, test, cutoff, image_out, inverse, kept_out,
    buf, kall, kgive, kget, khl, acc, m, scale, scaled, loc, pieces, lines, full, cloc, cpieces, clines, cfull, psend, precv,
    ag_recv, ag_send, k_local, k_recv, k_send, ar_recv, ar_send, cr_recv, cr_send, p_recv, p_send,
):
    row, col = lax.axis_index("row"), lax.axis_index("col")
    core = lax.rem(col, 2)
    here = (
        lax.rem(lax.div(col, 2), 2) * 2 + lax.rem(row, 2),
        lax.div(col, 4),
        lax.div(row, 2),
    )

    def device(x, y, z, c):
        return (z * 2 + lax.rem(x, 2), (y * 2 + lax.div(x, 2)) * 2 + c)

    def moved(by, core=core):
        return device(*[lax.rem(p + b, RING) for p, b in zip(here, by)], core)

    def hop(s):
        return tuple((a - b) % RING for a, b in zip(ORDER[s], ORDER[PARENT[s]]))

    sibling = device(*here, 1 - core)
    near = {hop(s) for s in range(1, SLOTS)}
    near |= {tuple(-b % RING for b in by) for by in near}
    near |= {(x, y, 0) for x in range(RING) for y in range(RING)} | {(0, 0, z) for z in range(RING)}
    greet = [moved(by) for by in sorted(near - {(0, 0, 0)})]
    greet += [moved((0, 0, z), 1 - core) for z in range(RING)]

    pltpu.make_async_copy(kernel_hbm, kall, k_local).start()
    barrier = pltpu.get_barrier_semaphore()
    for other in greet:
        pl.semaphore_signal(barrier, inc=1, device_id=other, device_id_type=MESH)
    pl.semaphore_wait(barrier, len(greet))

    def remote(src, dst, send, recv, to):
        return pltpu.make_async_remote_copy(
            src_ref=src, dst_ref=dst, send_sem=send, recv_sem=recv, device_id=to, device_id_type=MESH
        )

    def block(par, s, count=1):
        return buf.at[par, pl.ds(s * BLOCK, count * BLOCK)]

    def forward(par, s):
        for child in SENT[s]:
            remote(
                block(par, PARENT[child]), block(par, child), ag_send, ag_recv.at[par, GROUP[child]], moved(hop(child))
            ).start()

    def arrived(par, group):
        whole = block(par, group, GROUP.count(group))
        pltpu.make_async_copy(whole, whole, ag_recv.at[par, group]).wait()

    def rank(s):
        x, y, z = [lax.rem(p + RING - d, RING) for p, d in zip(here, ORDER[s])]
        return (z * 2 + lax.rem(x, 2)) * 8 + y * 2 + lax.div(x, 2)

    def columns(j):
        return pl.ds(pl.multiple_of(j * BLOCK, BLOCK), BLOCK)

    def lanes(c):
        return pl.ds(c * CHUNK * BLOCK, CHUNK * BLOCK)

    def part_of_given(c):
        return pl.ds(c * (SLOTS // PARTS) * BLOCK, (SLOTS // PARTS) * BLOCK)

    def give_kernel():
        pltpu.make_async_copy(kernel_hbm, kall, k_local).wait()
        for c in range(PARTS):
            for j in range(c * (SLOTS // PARTS), (c + 1) * (SLOTS // PARTS)):
                kgive[:, j * BLOCK : (j + 1) * BLOCK] = kall[:, columns(2 * j + 1 - core)]
            there = part_of_given(c)
            remote(kgive.at[:, there], kget.at[:, there], k_send.at[c], k_recv.at[c], sibling).start()

    def given_kernel(c):
        there = part_of_given(c)
        remote(kgive.at[:, there], kget.at[:, there], k_send.at[c], k_recv.at[c], sibling).wait()

    def split_kernel(c, own):
        for s in range(c * CHUNK, (c + 1) * CHUNK):
            j = rank(s)
            value = kall[:, columns(2 * j + core)] if own else kget[:, columns(j)]
            high = value.astype(jnp.bfloat16)
            low = (value - high.astype(jnp.float32)).astype(jnp.bfloat16)
            first, there = 0 if own else BLOCK, slice(s * BLOCK, (s + 1) * BLOCK)
            khl[first : first + BLOCK, there] = high
            khl[2 * BLOCK + first : 3 * BLOCK + first, there] = low

    def leaves(par, c):
        for group in sorted(set(GROUP[c * CHUNK : (c + 1) * CHUNK])):
            if group >= INNER:
                arrived(par, group)

    def multiply(par, c):
        x = buf[par, pl.ds(c * CHUNK * BLOCK, CHUNK * BLOCK), :]
        high = x.astype(jnp.bfloat16)
        low = (x - high.astype(jnp.float32)).astype(jnp.bfloat16)
        term = jnp.dot(
            khl[:, lanes(c)], jnp.concatenate([high, low], axis=1), preferred_element_type=jnp.float32
        )
        if c == 0:
            acc[...] = term
        else:
            acc[...] += term

    def sum_stages(loc, pieces, line, full, recv, send):
        me = here[0] * RING + here[1]
        spot = here[2] * 2 + core

        def part(e):
            return pl.ds(pl.multiple_of(e * PIECE, PIECE), PIECE)

        def to_team(source, target, stage):
            for by in range(1, TEAM):
                e = lax.rem(me + by, TEAM)
                to = device(lax.div(e, RING), lax.rem(e, RING), here[2], core)
                remote(source(e), target.at[by - 1], send.at[stage], recv.at[stage], to).start()

        def await_all(target, count, semaphore):
            whole = target.at[pl.ds(0, count)]
            pltpu.make_async_copy(whole, whole, semaphore).wait()

        def tree_sum(got):
            while len(got) > 1:
                got = [x + y for x, y in zip(got[::2], got[1::2])]
            return got[0]

        def scatter():
            to_team(lambda e: loc.at[part(e)], pieces, 0)

        def exchange():
            await_all(pieces, TEAM - 1, recv.at[0])
            line[LINE - 1] = tree_sum([pieces[k] for k in range(TEAM - 1)] + [loc[part(me), :]])
            for by in range(1, LINE):
                f = lax.rem(spot + by, LINE)
                to = device(here[0], here[1], lax.div(f, 2), lax.rem(f, 2))
                remote(line.at[LINE - 1], line.at[by - 1], send.at[1], recv.at[1], to).start()

        def gather():
            await_all(line, LINE - 1, recv.at[1])
            full[TEAM - 1] = tree_sum([line[lax.rem(spot - f + 2 * LINE - 1, LINE)] for f in range(LINE)])
            to_team(lambda e: full.at[TEAM - 1], full, 2)

        def finish():
            await_all(full, TEAM - 1, recv.at[2])
            await_all(pieces, TEAM - 1, send.at[0])
            await_all(line, LINE - 1, send.at[1])
            await_all(full, TEAM - 1, send.at[2])

        return [scatter, exchange, gather, finish]

    def whole_sum(full):
        me = here[0] * RING + here[1]
        return jnp.concatenate([full[lax.rem(me - e + 2 * TEAM - 1, TEAM)] for e in range(TEAM)], axis=0)

    def factor_panel(p):
        if p == 0:
            load_scaled(whole_sum(full_now[0]), m, scale)
        eliminate(m, inverse, scale, scaled, p)

    full_now = [None]

    def gather_and_multiply(par, tasks, work, beside):
        forward(par, 0)
        for s in range(INNER):
            if s:
                arrived(par, s)
                forward(par, s)
            for task in tasks.get(s, ()):
                task()
        for task in work:
            task()
        value = acc[...]
        value = value[:, :BLOCK] + value[:, BLOCK:]
        value = value[: 2 * BLOCK] + value[2 * BLOCK :]
        psend[...] = value[BLOCK:]
        copy = remote(psend, precv.at[par], p_send, p_recv.at[par], sibling)
        copy.start()
        for task in beside:
            task()
        whole = block(par, 1, SLOTS - 1)
        pltpu.make_async_copy(whole, whole, ag_send).wait()
        copy.wait()
        return value[:BLOCK] + precv[par]

    def local_gram(par):
        y = buf[par, pl.ds(0, BLOCK), :]
        loc[...] = exact_dot(y.T, y)

    buf[0, pl.ds(0, BLOCK), :] = start[...]
    tasks = {0: [give_kernel]}
    work = [lambda c=c: given_kernel(c) for c in range(PARTS)]
    for c in range(SLOTS // CHUNK):
        tasks[10 + 2 * c] = [lambda c=c: split_kernel(c, True)]
        work += [lambda c=c: split_kernel(c, False), lambda c=c: leaves(0, c), lambda c=c: multiply(0, c)]
    image = gather_and_multiply(0, tasks, work, [])
    buf[1, pl.ds(0, BLOCK), :] = image

    def step(t, carry):
        par = lax.rem(t, 2)
        stages = sum_stages(loc, pieces.at[par], lines.at[par], full.at[par], ar_recv.at[par], ar_send)
        full_now[0] = full.at[par]
        tasks = {0: [lambda: local_gram(par), stages[0]]}
        for at, stage in zip((0, 8, 24), stages[1:]):
            tasks.setdefault(at, []).append(stage)
        product = [lambda c=c: multiply(par, c) for c in range(SLOTS // CHUNK)]
        panel = [lambda p=p: factor_panel(p) for p in range(16)]
        for at, task in [(13, product[0]), (17, product[1])] + [(25 + p // 2, panel[p]) for p in range(8)]:
            tasks.setdefault(at, []).append(task)
        work = [product[2], lambda: leaves(par, 3), product[3]] + panel[8:10]
        work += [lambda: leaves(par, 4), product[4]] + panel[10:12] + [lambda: leaves(par, 5), product[5]]
        work += [lambda: leaves(par, 6), product[6], lambda: leaves(par, 7), product[7]]
        image = gather_and_multiply(par, tasks, work, panel[12:])
        buf[1 - par, pl.ds(0, BLOCK), :] = exact_dot(image, inverse[...], (((1,), (1,)), ((), ())))
        return carry

    lax.fori_loop(1, ITERATIONS, step, 0)

    par = ITERATIONS % 2
    stages = sum_stages(loc, pieces.at[par], lines.at[par], full.at[par], ar_recv.at[par], ar_send)
    late = sum_stages(cloc, cpieces, clines, cfull, cr_recv, cr_send)
    full_now[0] = full.at[par]
    local_gram(par)
    stages[0]()
    last = buf[par, pl.ds(0, BLOCK), :]
    cloc[...] = exact_dot(last.T, test[...])
    late[0]()
    stages[1]()
    late[1]()
    stages[2]()
    late[2]()
    stages[3]()
    for p in range(16):
        if p == 8:
            late[3]()
        factor_panel(p)
    image_out[...] = buf[par, pl.ds(0, BLOCK), :]
    keep = lax.broadcasted_iota(jnp.int32, (BLOCK, TEST), 0) < cutoff[0]
    kept_out[...] = exact_dot(inverse[...], whole_sum(cfull)) * jnp.where(keep, 1.0, 0.0)


def project(image, inverse, kept, subspace, projection):
    block = exact_dot(image[...], inverse[...], (((1,), (1,)), ((), ())))
    subspace[...] = block
    projection[...] = exact_dot(block, kept[...])


def per_device(kernel_rows, start_block, test_kernel, cutoff):
    f32 = jnp.float32
    vmem = pl.BlockSpec(memory_space=pltpu.VMEM)
    dma = pltpu.SemaphoreType.DMA
    narrow = jax.ShapeDtypeStruct((BLOCK, BLOCK), f32)
    broad = jax.ShapeDtypeStruct((BLOCK, TEST), f32)
    image, inverse, kept = pl.pallas_call(
        kernel,
        out_shape=(narrow, narrow, broad),
        in_specs=[pl.BlockSpec(memory_space=pl.ANY), vmem, vmem, pl.BlockSpec(memory_space=pltpu.SMEM)],
        out_specs=(vmem, vmem, vmem),
        scratch_shapes=[
            pltpu.VMEM((2, SLOTS * BLOCK, BLOCK), f32),
            pltpu.VMEM((BLOCK, 2 * SLOTS * BLOCK), f32),
            pltpu.VMEM((BLOCK, SLOTS * BLOCK), f32),
            pltpu.VMEM((BLOCK, SLOTS * BLOCK), f32),
            pltpu.VMEM((4 * BLOCK, SLOTS * BLOCK), jnp.bfloat16),
            pltpu.VMEM((4 * BLOCK, 2 * BLOCK), f32),
            pltpu.VMEM((BLOCK, BLOCK), f32),
            pltpu.VMEM((8, BLOCK), f32),
            pltpu.VMEM((GROUPED, BLOCK), f32),
            pltpu.VMEM((BLOCK, BLOCK), f32),
            pltpu.VMEM((2, TEAM, PIECE, BLOCK), f32),
            pltpu.VMEM((2, LINE, PIECE, BLOCK), f32),
            pltpu.VMEM((2, TEAM, PIECE, BLOCK), f32),
            pltpu.VMEM((BLOCK, TEST), f32),
            pltpu.VMEM((TEAM, PIECE, TEST), f32),
            pltpu.VMEM((LINE, PIECE, TEST), f32),
            pltpu.VMEM((TEAM, PIECE, TEST), f32),
            pltpu.VMEM((BLOCK, BLOCK), f32),
            pltpu.VMEM((2, BLOCK, BLOCK), f32),
            dma((2, SLOTS)),
            dma,
            dma,
            dma((PARTS,)),
            dma((PARTS,)),
            dma((2, 3)),
            dma((3,)),
            dma((3,)),
            dma((3,)),
            dma((2,)),
            dma,
        ],
        compiler_params=pltpu.CompilerParams(
            collective_id=0, has_side_effects=True, vmem_limit_bytes=56 * 1024 * 1024
        ),
        cost_estimate=pl.CostEstimate(
            flops=4 * 2 * 512 * 8192 * 256, bytes_accessed=16 * 2**20, transcendentals=0
        ),
        name="iterate",
    )(kernel_rows, start_block, test_kernel, cutoff)
    return pl.pallas_call(project, out_shape=(narrow, broad), name="project")(image, inverse, kept)


def solution(mesh):
    in_specs = (P(("row", "col"), None), P(("row", "col"), None), P(("row", "col"), None), P())
    out_specs = (P(("row", "col"), None), P(("row", "col"), None))
    return jax.shard_map(
        per_device, mesh=mesh, in_specs=in_specs, out_specs=out_specs, check_vma=False
    )
```

```python
import functools

import jax
import jax.numpy as jnp
from jax import lax
from jax.experimental import pallas as pl
from jax.experimental.pallas import tpu as pltpu
from jax.sharding import PartitionSpec as P

BLOCK = 128
TEST = 256
ITERATIONS = 4
RING = 4
SLOTS = RING**3
CHUNK = 8
PARTS = 4
TEAM = RING * RING
LINE = 2 * RING
PIECE = BLOCK // TEAM
GROUPED = BLOCK
MESH = pl.DeviceIdType.MESH
HIGHEST = lax.Precision.HIGHEST

TREE = (
    0, 49152, 196608, 65536, 28672, 16384, 12288, 69632, 4096, 114753, 131202, 53313,
    61506, 32836, 78019, 110852, 213317, 201224, 148106, 24840, 139719, 258828, 37579, 58059,
    127756, 250575, 119245, 45901, 177104, 208896, 20480, 245890, 82119, 98889, 8713, 74121,
    180878, 95118, 107472, 205905, 86479, 160914, 136273, 218193, 144276, 152722, 243029, 189717,
    103831, 169108, 222419, 230227, 226330, 194072, 255447, 91355, 124570, 42715, 165018, 156954,
    235100, 173852, 239193, 185948,
)
ORDER = [(code // 65536, code // 16384 % 4, code // 4096 % 4) for code in TREE]
PARENT = [code // 64 % 64 for code in TREE]
AFTER = [code % 64 for code in TREE]


def passed_on():
    height = [0] * SLOTS
    for s in reversed(range(1, SLOTS)):
        height[PARENT[s]] = max(height[PARENT[s]], height[s] + 1)
    sent = [[] for _ in TREE]
    for s in range(1, SLOTS):
        sent[AFTER[s]].append(s)
    for at, found in enumerate(sent):
        found.sort(key=lambda s: (PARENT[s] != at, -height[s]))
    return sent


SENT = passed_on()
INNER = len(set(PARENT))
GROUP = [s if s < INNER else max(INNER, s // CHUNK * CHUNK) for s in range(SLOTS)]


def exact_dot(a, b, dims=(((1,), (0,)), ((), ()))):
    return lax.dot_general(a, b, dims, precision=HIGHEST, preferred_element_type=jnp.float32)


def reciprocal(x):
    r = pl.reciprocal(x, approx=True)
    r = r * (2.0 - x * r)
    return r * (2.0 - x * r)


def inverse_root(x):
    r = lax.rsqrt(x)
    return r * (1.5 - 0.5 * x * r * r)


def eliminate(m, inverse, scale, scaled, panel):
    base = 8 * panel
    end = base // GROUPED * GROUPED + GROUPED
    wide = (8, BLOCK)
    lane = lax.broadcasted_iota(jnp.int32, wide, 1)
    within = (lane >= base) & (lane < base + 8)
    top = m[base : base + 8, :]
    raw = [jnp.broadcast_to(top[k : k + 1, :], wide) for k in range(8)]
    a = {
        (k, i): jnp.broadcast_to(raw[k][:, base + i : base + i + 1], wide) for k in range(8) for i in range(k, 8)
    }
    rows = [jnp.where(within, jnp.where(lane == base + k, 1.0, 0.0), raw[k]) for k in range(8)]
    over, factor = {}, {}
    for k in range(0, 8, 2):
        p, q, r = a[k, k], a[k, k + 1], a[k + 1, k + 1]
        over[k] = reciprocal(p * r - q * q)
        for i in range(k + 2, 8):
            factor[k, i] = (r * a[k, i] - q * a[k + 1, i]) * over[k]
            factor[k + 1, i] = (p * a[k + 1, i] - q * a[k, i]) * over[k]
            for j in range(i, 8):
                a[i, j] = a[i, j] - (factor[k, i] * a[k, j] + factor[k + 1, i] * a[k + 1, j])
            rows[i] = rows[i] - (factor[k, i] * rows[k] + factor[k + 1, i] * rows[k + 1])
    if base + 8 < end:
        solved = [None] * 8
        for k in range(0, 8, 2):
            p, q, r = a[k, k] * over[k], a[k, k + 1] * over[k], a[k + 1, k + 1] * over[k]
            solved[k] = r * rows[k] - q * rows[k + 1]
            solved[k + 1] = p * rows[k + 1] - q * rows[k]
        for k in (6, 4, 2):
            for i in range(k):
                solved[i] = solved[i] - (factor[i, k] * solved[k] + factor[i, k + 1] * solved[k + 1])
        for r in range(base + 8, end, 8):
            rest = m[r : r + 8, :]
            terms = [jnp.broadcast_to(rest[:, base + k : base + k + 1], wide) * solved[k] for k in range(8)]
            while len(terms) > 1:
                terms = [x + y for x, y in zip(terms[::2], terms[1::2])]
            m[r : r + 8, :] = jnp.where(within, 0.0, rest) - terms[0]
    for k in range(0, 8, 2):
        p, q = a[k, k], a[k, k + 1]
        r = inverse_root(p)
        ratio = p * over[k]
        first = rows[k] * r
        second = (rows[k + 1] - rows[k] * (q * r * r)) * (ratio * inverse_root(ratio))
        for j, done in ((base + k, first), (base + k + 1, second)):
            inverse[j : j + 1, :] = jnp.where(lane < base + 8, done * scale[...], 0.0)[0:1, :]
            if end < BLOCK:
                kept = (lane < base + 8) | (lane >= end)
                scaled[j % GROUPED : j % GROUPED + 1, :] = jnp.where(kept, done, 0.0)[0:1, :]
    if base + 8 == end and end < BLOCK:
        done = scaled[...]
        lanes = lax.broadcasted_iota(jnp.int32, (BLOCK - end, BLOCK), 1)
        rest = jnp.where((lanes >= end - GROUPED) & (lanes < end), 0.0, m[end:, :])
        m[end:, :] = rest - exact_dot(done.T[end:, :], done)


def load_scaled(value, m, scale):
    rows = lax.broadcasted_iota(jnp.int32, value.shape, 0)
    lanes = lax.broadcasted_iota(jnp.int32, value.shape, 1)
    diagonal = jnp.sum(jnp.where(rows == lanes, value, 0.0), axis=0, keepdims=True)
    over = 1.0 / jnp.broadcast_to(jnp.sum(diagonal, axis=1, keepdims=True), (8, BLOCK))
    m[...] = value * over[0:1, :]
    scale[...] = jnp.sqrt(over)


def kernel(
    kernel_hbm, start, test, cutoff, image_out, inverse, kept_out,
    buf, kall, kgive, kget, khl, acc, m, scale, scaled, loc, pieces, lines, full, cloc, cpieces, clines, cfull, psend, precv,
    ag_recv, ag_send, k_local, k_recv, k_send, ar_recv, ar_send, cr_recv, cr_send, p_recv, p_send,
):
    row, col = lax.axis_index("row"), lax.axis_index("col")
    core = lax.rem(col, 2)
    here = (
        lax.rem(lax.div(col, 2), 2) * 2 + lax.rem(row, 2),
        lax.div(col, 4),
        lax.div(row, 2),
    )

    def device(x, y, z, c):
        return (z * 2 + lax.rem(x, 2), (y * 2 + lax.div(x, 2)) * 2 + c)

    def moved(by, core=core):
        return device(*[lax.rem(p + b, RING) for p, b in zip(here, by)], core)

    def hop(s):
        return tuple((a - b) % RING for a, b in zip(ORDER[s], ORDER[PARENT[s]]))

    sibling = device(*here, 1 - core)
    near = {hop(s) for s in range(1, SLOTS)}
    near |= {tuple(-b % RING for b in by) for by in near}
    near |= {(x, y, 0) for x in range(RING) for y in range(RING)} | {(0, 0, z) for z in range(RING)}
    greet = [moved(by) for by in sorted(near - {(0, 0, 0)})]
    greet += [moved((0, 0, z), 1 - core) for z in range(RING)]

    pltpu.make_async_copy(kernel_hbm, kall, k_local).start()
    barrier = pltpu.get_barrier_semaphore()
    for other in greet:
        pl.semaphore_signal(barrier, inc=1, device_id=other, device_id_type=MESH)
    pl.semaphore_wait(barrier, len(greet))

    def remote(src, dst, send, recv, to):
        return pltpu.make_async_remote_copy(
            src_ref=src, dst_ref=dst, send_sem=send, recv_sem=recv, device_id=to, device_id_type=MESH
        )

    def block(par, s, count=1):
        return buf.at[par, pl.ds(s * BLOCK, count * BLOCK)]

    def forward(par, s):
        for child in SENT[s]:
            remote(
                block(par, PARENT[child]), block(par, child), ag_send, ag_recv.at[par, GROUP[child]], moved(hop(child))
            ).start()

    def arrived(par, group):
        whole = block(par, group, GROUP.count(group))
        pltpu.make_async_copy(whole, whole, ag_recv.at[par, group]).wait()

    def rank(s):
        x, y, z = [lax.rem(p + RING - d, RING) for p, d in zip(here, ORDER[s])]
        return (z * 2 + lax.rem(x, 2)) * 8 + y * 2 + lax.div(x, 2)

    def columns(j):
        return pl.ds(pl.multiple_of(j * BLOCK, BLOCK), BLOCK)

    def lanes(c):
        return pl.ds(c * CHUNK * BLOCK, CHUNK * BLOCK)

    def part_of_given(c):
        return pl.ds(c * (SLOTS // PARTS) * BLOCK, (SLOTS // PARTS) * BLOCK)

    def give_kernel():
        pltpu.make_async_copy(kernel_hbm, kall, k_local).wait()
        for c in range(PARTS):
            for j in range(c * (SLOTS // PARTS), (c + 1) * (SLOTS // PARTS)):
                kgive[:, j * BLOCK : (j + 1) * BLOCK] = kall[:, columns(2 * j + 1 - core)]
            there = part_of_given(c)
            remote(kgive.at[:, there], kget.at[:, there], k_send.at[c], k_recv.at[c], sibling).start()

    def given_kernel(c):
        there = part_of_given(c)
        remote(kgive.at[:, there], kget.at[:, there], k_send.at[c], k_recv.at[c], sibling).wait()

    def split_kernel(c, own):
        for s in range(c * CHUNK, (c + 1) * CHUNK):
            j = rank(s)
            value = kall[:, columns(2 * j + core)] if own else kget[:, columns(j)]
            high = value.astype(jnp.bfloat16)
            low = (value - high.astype(jnp.float32)).astype(jnp.bfloat16)
            first, there = 0 if own else BLOCK, slice(s * BLOCK, (s + 1) * BLOCK)
            khl[first : first + BLOCK, there] = high
            khl[2 * BLOCK + first : 3 * BLOCK + first, there] = low

    def leaves(par, c):
        for group in sorted(set(GROUP[c * CHUNK : (c + 1) * CHUNK])):
            if group >= INNER:
                arrived(par, group)

    def multiply(par, c):
        x = buf[par, pl.ds(c * CHUNK * BLOCK, CHUNK * BLOCK), :]
        high = x.astype(jnp.bfloat16)
        low = (x - high.astype(jnp.float32)).astype(jnp.bfloat16)
        term = jnp.dot(
            khl[:, lanes(c)], jnp.concatenate([high, low], axis=1), preferred_element_type=jnp.float32
        )
        if c == 0:
            acc[...] = term
        else:
            acc[...] += term

    def sum_stages(loc, pieces, line, full, recv, send):
        me = here[0] * RING + here[1]
        spot = here[2] * 2 + core

        def part(e):
            return pl.ds(pl.multiple_of(e * PIECE, PIECE), PIECE)

        def to_team(source, target, stage):
            for by in range(1, TEAM):
                e = lax.rem(me + by, TEAM)
                to = device(lax.div(e, RING), lax.rem(e, RING), here[2], core)
                remote(source(e), target.at[by - 1], send.at[stage], recv.at[stage], to).start()

        def await_all(target, count, semaphore):
            whole = target.at[pl.ds(0, count)]
            pltpu.make_async_copy(whole, whole, semaphore).wait()

        def tree_sum(got):
            while len(got) > 1:
                got = [x + y for x, y in zip(got[::2], got[1::2])]
            return got[0]

        def scatter():
            to_team(lambda e: loc.at[part(e)], pieces, 0)

        def exchange():
            await_all(pieces, TEAM - 1, recv.at[0])
            line[LINE - 1] = tree_sum([pieces[k] for k in range(TEAM - 1)] + [loc[part(me), :]])
            for by in range(1, LINE):
                f = lax.rem(spot + by, LINE)
                to = device(here[0], here[1], lax.div(f, 2), lax.rem(f, 2))
                remote(line.at[LINE - 1], line.at[by - 1], send.at[1], recv.at[1], to).start()

        def gather():
            await_all(line, LINE - 1, recv.at[1])
            full[TEAM - 1] = tree_sum([line[lax.rem(spot - f + 2 * LINE - 1, LINE)] for f in range(LINE)])
            to_team(lambda e: full.at[TEAM - 1], full, 2)

        def finish():
            await_all(full, TEAM - 1, recv.at[2])
            await_all(pieces, TEAM - 1, send.at[0])
            await_all(line, LINE - 1, send.at[1])
            await_all(full, TEAM - 1, send.at[2])

        return [scatter, exchange, gather, finish]

    def whole_sum(full):
        me = here[0] * RING + here[1]
        return jnp.concatenate([full[lax.rem(me - e + 2 * TEAM - 1, TEAM)] for e in range(TEAM)], axis=0)

    def factor_panel(p):
        if p == 0:
            load_scaled(whole_sum(full_now[0]), m, scale)
        eliminate(m, inverse, scale, scaled, p)

    full_now = [None]

    def gather_and_multiply(par, tasks, work, beside):
        forward(par, 0)
        for s in range(INNER):
            if s:
                arrived(par, s)
                forward(par, s)
            for task in tasks.get(s, ()):
                task()
        for task in work:
            task()
        value = acc[...]
        value = value[:, :BLOCK] + value[:, BLOCK:]
        value = value[: 2 * BLOCK] + value[2 * BLOCK :]
        psend[...] = value[BLOCK:]
        copy = remote(psend, precv.at[par], p_send, p_recv.at[par], sibling)
        copy.start()
        for task in beside:
            task()
        whole = block(par, 1, SLOTS - 1)
        pltpu.make_async_copy(whole, whole, ag_send).wait()
        copy.wait()
        return value[:BLOCK] + precv[par]

    def local_gram(par):
        y = buf[par, pl.ds(0, BLOCK), :]
        loc[...] = exact_dot(y.T, y)

    buf[0, pl.ds(0, BLOCK), :] = start[...]
    tasks = {0: [give_kernel]}
    work = [lambda c=c: given_kernel(c) for c in range(PARTS)]
    for c in range(SLOTS // CHUNK):
        tasks[10 + 2 * c] = [lambda c=c: split_kernel(c, True)]
        work += [lambda c=c: split_kernel(c, False), lambda c=c: leaves(0, c), lambda c=c: multiply(0, c)]
    image = gather_and_multiply(0, tasks, work, [])
    buf[1, pl.ds(0, BLOCK), :] = image

    def step(t, carry):
        par = lax.rem(t, 2)
        stages = sum_stages(loc, pieces.at[par], lines.at[par], full.at[par], ar_recv.at[par], ar_send)
        full_now[0] = full.at[par]
        tasks = {0: [lambda: local_gram(par), stages[0]]}
        for at, stage in zip((6, 18), stages[1:3]):
            tasks.setdefault(at, []).append(stage)
        product = [lambda c=c: multiply(par, c) for c in range(SLOTS // CHUNK)]
        panel = [lambda p=p: factor_panel(p) for p in range(16)]
        for at, c in ((13, 0), (17, 1)):
            tasks.setdefault(at, []).append(product[c])
        work = [product[2], lambda: leaves(par, 3), product[3], lambda: leaves(par, 4), product[4], stages[3]]
        work += panel[0:6] + [lambda: leaves(par, 5), product[5]] + panel[6:10]
        work += [lambda: leaves(par, 6), product[6], lambda: leaves(par, 7), product[7]]
        image = gather_and_multiply(par, tasks, work, panel[10:])
        buf[1 - par, pl.ds(0, BLOCK), :] = exact_dot(image, inverse[...], (((1,), (1,)), ((), ())))
        return carry

    lax.fori_loop(1, ITERATIONS, step, 0)

    par = ITERATIONS % 2
    stages = sum_stages(loc, pieces.at[par], lines.at[par], full.at[par], ar_recv.at[par], ar_send)
    late = sum_stages(cloc, cpieces, clines, cfull, cr_recv, cr_send)
    full_now[0] = full.at[par]
    local_gram(par)
    stages[0]()
    last = buf[par, pl.ds(0, BLOCK), :]
    cloc[...] = exact_dot(last.T, test[...])
    late[0]()
    stages[1]()
    late[1]()
    stages[2]()
    late[2]()
    stages[3]()
    for p in range(16):
        if p == 8:
            late[3]()
        factor_panel(p)
    image_out[...] = buf[par, pl.ds(0, BLOCK), :]
    keep = lax.broadcasted_iota(jnp.int32, (BLOCK, TEST), 0) < cutoff[0]
    kept_out[...] = exact_dot(inverse[...], whole_sum(cfull)) * jnp.where(keep, 1.0, 0.0)


def project(image, inverse, kept, subspace, projection):
    block = exact_dot(image[...], inverse[...], (((1,), (1,)), ((), ())))
    subspace[...] = block
    projection[...] = exact_dot(block, kept[...])


def per_device(kernel_rows, start_block, test_kernel, cutoff):
    f32 = jnp.float32
    vmem = pl.BlockSpec(memory_space=pltpu.VMEM)
    dma = pltpu.SemaphoreType.DMA
    narrow = jax.ShapeDtypeStruct((BLOCK, BLOCK), f32)
    broad = jax.ShapeDtypeStruct((BLOCK, TEST), f32)
    image, inverse, kept = pl.pallas_call(
        kernel,
        out_shape=(narrow, narrow, broad),
        in_specs=[pl.BlockSpec(memory_space=pl.ANY), vmem, vmem, pl.BlockSpec(memory_space=pltpu.SMEM)],
        out_specs=(vmem, vmem, vmem),
        scratch_shapes=[
            pltpu.VMEM((2, SLOTS * BLOCK, BLOCK), f32),
            pltpu.VMEM((BLOCK, 2 * SLOTS * BLOCK), f32),
            pltpu.VMEM((BLOCK, SLOTS * BLOCK), f32),
            pltpu.VMEM((BLOCK, SLOTS * BLOCK), f32),
            pltpu.VMEM((4 * BLOCK, SLOTS * BLOCK), jnp.bfloat16),
            pltpu.VMEM((4 * BLOCK, 2 * BLOCK), f32),
            pltpu.VMEM((BLOCK, BLOCK), f32),
            pltpu.VMEM((8, BLOCK), f32),
            pltpu.VMEM((GROUPED, BLOCK), f32),
            pltpu.VMEM((BLOCK, BLOCK), f32),
            pltpu.VMEM((2, TEAM, PIECE, BLOCK), f32),
            pltpu.VMEM((2, LINE, PIECE, BLOCK), f32),
            pltpu.VMEM((2, TEAM, PIECE, BLOCK), f32),
            pltpu.VMEM((BLOCK, TEST), f32),
            pltpu.VMEM((TEAM, PIECE, TEST), f32),
            pltpu.VMEM((LINE, PIECE, TEST), f32),
            pltpu.VMEM((TEAM, PIECE, TEST), f32),
            pltpu.VMEM((BLOCK, BLOCK), f32),
            pltpu.VMEM((2, BLOCK, BLOCK), f32),
            dma((2, SLOTS)),
            dma,
            dma,
            dma((PARTS,)),
            dma((PARTS,)),
            dma((2, 3)),
            dma((3,)),
            dma((3,)),
            dma((3,)),
            dma((2,)),
            dma,
        ],
        compiler_params=pltpu.CompilerParams(
            collective_id=0, has_side_effects=True, vmem_limit_bytes=56 * 1024 * 1024
        ),
        cost_estimate=pl.CostEstimate(
            flops=4 * 2 * 512 * 8192 * 256, bytes_accessed=16 * 2**20, transcendentals=0
        ),
        name="iterate",
    )(kernel_rows, start_block, test_kernel, cutoff)
    return pl.pallas_call(project, out_shape=(narrow, broad), name="project")(image, inverse, kept)


def solution(mesh):
    in_specs = (P(("row", "col"), None), P(("row", "col"), None), P(("row", "col"), None), P())
    out_specs = (P(("row", "col"), None), P(("row", "col"), None))
    return jax.shard_map(
        per_device, mesh=mesh, in_specs=in_specs, out_specs=out_specs, check_vma=False
    )
```

```python
import functools

import jax
import jax.numpy as jnp
from jax import lax
from jax.experimental import pallas as pl
from jax.experimental.pallas import tpu as pltpu
from jax.sharding import PartitionSpec as P

BLOCK = 128
TEST = 256
ITERATIONS = 4
RING = 4
SLOTS = RING**3
CHUNK = 8
PARTS = 4
TEAM = RING * RING
LINE = 2 * RING
PIECE = BLOCK // TEAM
GROUPED = BLOCK
MESH = pl.DeviceIdType.MESH
HIGHEST = lax.Precision.HIGHEST

TREE = (
    0, 49152, 196608, 65536, 28672, 16384, 12288, 69632, 4096, 114753, 131202, 53313,
    61506, 32836, 78019, 110852, 213317, 201224, 148106, 24840, 139719, 258828, 37579, 58059,
    127756, 250575, 119245, 45901, 177104, 208896, 20480, 245890, 82119, 98889, 8713, 74121,
    180878, 95118, 107472, 205905, 86479, 160914, 136273, 218193, 144276, 152722, 243029, 189717,
    103831, 169108, 222419, 230227, 226330, 194072, 255447, 91355, 124570, 42715, 165018, 156954,
    235100, 173852, 239193, 185948,
)
ORDER = [(code // 65536, code // 16384 % 4, code // 4096 % 4) for code in TREE]
PARENT = [code // 64 % 64 for code in TREE]
AFTER = [code % 64 for code in TREE]


def passed_on():
    height = [0] * SLOTS
    for s in reversed(range(1, SLOTS)):
        height[PARENT[s]] = max(height[PARENT[s]], height[s] + 1)
    sent = [[] for _ in TREE]
    for s in range(1, SLOTS):
        sent[AFTER[s]].append(s)
    for at, found in enumerate(sent):
        found.sort(key=lambda s: (PARENT[s] != at, -height[s]))
    return sent


SENT = passed_on()
INNER = len(set(PARENT))
GROUP = [s if s < INNER else max(INNER, s // CHUNK * CHUNK) for s in range(SLOTS)]


def exact_dot(a, b, dims=(((1,), (0,)), ((), ()))):
    return lax.dot_general(a, b, dims, precision=HIGHEST, preferred_element_type=jnp.float32)


def reciprocal(x):
    r = pl.reciprocal(x, approx=True)
    r = r * (2.0 - x * r)
    return r * (2.0 - x * r)


def inverse_root(x):
    r = lax.rsqrt(x)
    return r * (1.5 - 0.5 * x * r * r)


def eliminate(m, inverse, scale, scaled, panel):
    base = 8 * panel
    end = base // GROUPED * GROUPED + GROUPED
    wide = (8, BLOCK)
    lane = lax.broadcasted_iota(jnp.int32, wide, 1)
    within = (lane >= base) & (lane < base + 8)
    top = m[base : base + 8, :]
    raw = [jnp.broadcast_to(top[k : k + 1, :], wide) for k in range(8)]
    a = {
        (k, i): jnp.broadcast_to(raw[k][:, base + i : base + i + 1], wide) for k in range(8) for i in range(k, 8)
    }
    rows = [jnp.where(within, jnp.where(lane == base + k, 1.0, 0.0), raw[k]) for k in range(8)]
    over, factor = {}, {}
    for k in range(0, 8, 2):
        p, q, r = a[k, k], a[k, k + 1], a[k + 1, k + 1]
        over[k] = reciprocal(p * r - q * q)
        for i in range(k + 2, 8):
            factor[k, i] = (r * a[k, i] - q * a[k + 1, i]) * over[k]
            factor[k + 1, i] = (p * a[k + 1, i] - q * a[k, i]) * over[k]
            for j in range(i, 8):
                a[i, j] = a[i, j] - (factor[k, i] * a[k, j] + factor[k + 1, i] * a[k + 1, j])
            rows[i] = rows[i] - (factor[k, i] * rows[k] + factor[k + 1, i] * rows[k + 1])
    if base + 8 < end:
        solved = [None] * 8
        for k in range(0, 8, 2):
            p, q, r = a[k, k] * over[k], a[k, k + 1] * over[k], a[k + 1, k + 1] * over[k]
            solved[k] = r * rows[k] - q * rows[k + 1]
            solved[k + 1] = p * rows[k + 1] - q * rows[k]
        for k in (6, 4, 2):
            for i in range(k):
                solved[i] = solved[i] - (factor[i, k] * solved[k] + factor[i, k + 1] * solved[k + 1])
        for r in range(base + 8, end, 8):
            rest = m[r : r + 8, :]
            terms = [jnp.broadcast_to(rest[:, base + k : base + k + 1], wide) * solved[k] for k in range(8)]
            while len(terms) > 1:
                terms = [x + y for x, y in zip(terms[::2], terms[1::2])]
            m[r : r + 8, :] = jnp.where(within, 0.0, rest) - terms[0]
    for k in range(0, 8, 2):
        p, q = a[k, k], a[k, k + 1]
        r = inverse_root(p)
        ratio = p * over[k]
        first = rows[k] * r
        second = (rows[k + 1] - rows[k] * (q * r * r)) * (ratio * inverse_root(ratio))
        for j, done in ((base + k, first), (base + k + 1, second)):
            inverse[j : j + 1, :] = jnp.where(lane < base + 8, done * scale[...], 0.0)[0:1, :]
            if end < BLOCK:
                kept = (lane < base + 8) | (lane >= end)
                scaled[j % GROUPED : j % GROUPED + 1, :] = jnp.where(kept, done, 0.0)[0:1, :]
    if base + 8 == end and end < BLOCK:
        done = scaled[...]
        lanes = lax.broadcasted_iota(jnp.int32, (BLOCK - end, BLOCK), 1)
        rest = jnp.where((lanes >= end - GROUPED) & (lanes < end), 0.0, m[end:, :])
        m[end:, :] = rest - exact_dot(done.T[end:, :], done)


def load_scaled(value, m, scale):
    rows = lax.broadcasted_iota(jnp.int32, value.shape, 0)
    lanes = lax.broadcasted_iota(jnp.int32, value.shape, 1)
    diagonal = jnp.sum(jnp.where(rows == lanes, value, 0.0), axis=0, keepdims=True)
    over = 1.0 / jnp.broadcast_to(jnp.sum(diagonal, axis=1, keepdims=True), (8, BLOCK))
    m[...] = value * over[0:1, :]
    scale[...] = jnp.sqrt(over)


def kernel(
    kernel_hbm, start, test, cutoff, image_out, inverse, kept_out,
    buf, kall, kgive, kget, khl, acc, m, scale, scaled, loc, pieces, lines, full, cloc, cpieces, clines, cfull, psend, precv,
    ag_recv, ag_send, k_local, k_recv, k_send, ar_recv, ar_send, cr_recv, cr_send, p_recv, p_send,
):
    row, col = lax.axis_index("row"), lax.axis_index("col")
    core = lax.rem(col, 2)
    here = (
        lax.rem(lax.div(col, 2), 2) * 2 + lax.rem(row, 2),
        lax.div(col, 4),
        lax.div(row, 2),
    )

    def device(x, y, z, c):
        return (z * 2 + lax.rem(x, 2), (y * 2 + lax.div(x, 2)) * 2 + c)

    def moved(by, core=core):
        return device(*[lax.rem(p + b, RING) for p, b in zip(here, by)], core)

    def hop(s):
        return tuple((a - b) % RING for a, b in zip(ORDER[s], ORDER[PARENT[s]]))

    sibling = device(*here, 1 - core)
    near = {hop(s) for s in range(1, SLOTS)}
    near |= {tuple(-b % RING for b in by) for by in near}
    near |= {(x, y, 0) for x in range(RING) for y in range(RING)} | {(0, 0, z) for z in range(RING)}
    greet = [moved(by) for by in sorted(near - {(0, 0, 0)})]
    greet += [moved((0, 0, z), 1 - core) for z in range(RING)]

    pltpu.make_async_copy(kernel_hbm, kall, k_local).start()
    barrier = pltpu.get_barrier_semaphore()
    for other in greet:
        pl.semaphore_signal(barrier, inc=1, device_id=other, device_id_type=MESH)
    pl.semaphore_wait(barrier, len(greet))

    def remote(src, dst, send, recv, to):
        return pltpu.make_async_remote_copy(
            src_ref=src, dst_ref=dst, send_sem=send, recv_sem=recv, device_id=to, device_id_type=MESH
        )

    def block(par, s, count=1):
        return buf.at[par, pl.ds(s * BLOCK, count * BLOCK)]

    def forward(par, s):
        for child in SENT[s]:
            remote(
                block(par, PARENT[child]), block(par, child), ag_send, ag_recv.at[par, GROUP[child]], moved(hop(child))
            ).start()

    def arrived(par, group):
        whole = block(par, group, GROUP.count(group))
        pltpu.make_async_copy(whole, whole, ag_recv.at[par, group]).wait()

    def rank(s):
        x, y, z = [lax.rem(p + RING - d, RING) for p, d in zip(here, ORDER[s])]
        return (z * 2 + lax.rem(x, 2)) * 8 + y * 2 + lax.div(x, 2)

    def columns(j):
        return pl.ds(pl.multiple_of(j * BLOCK, BLOCK), BLOCK)

    def lanes(c):
        return pl.ds(c * CHUNK * BLOCK, CHUNK * BLOCK)

    def part_of_given(c):
        return pl.ds(c * (SLOTS // PARTS) * BLOCK, (SLOTS // PARTS) * BLOCK)

    def give_kernel():
        pltpu.make_async_copy(kernel_hbm, kall, k_local).wait()
        for c in range(PARTS):
            for j in range(c * (SLOTS // PARTS), (c + 1) * (SLOTS // PARTS)):
                kgive[:, j * BLOCK : (j + 1) * BLOCK] = kall[:, columns(2 * j + 1 - core)]
            there = part_of_given(c)
            remote(kgive.at[:, there], kget.at[:, there], k_send.at[c], k_recv.at[c], sibling).start()

    def given_kernel(c):
        there = part_of_given(c)
        remote(kgive.at[:, there], kget.at[:, there], k_send.at[c], k_recv.at[c], sibling).wait()

    def split_kernel(c, own):
        for s in range(c * CHUNK, (c + 1) * CHUNK):
            j = rank(s)
            value = kall[:, columns(2 * j + core)] if own else kget[:, columns(j)]
            high = value.astype(jnp.bfloat16)
            low = (value - high.astype(jnp.float32)).astype(jnp.bfloat16)
            first, there = 0 if own else BLOCK, slice(s * BLOCK, (s + 1) * BLOCK)
            khl[first : first + BLOCK, there] = high
            khl[2 * BLOCK + first : 3 * BLOCK + first, there] = low

    def leaves(par, c):
        for group in sorted(set(GROUP[c * CHUNK : (c + 1) * CHUNK])):
            if group >= INNER:
                arrived(par, group)

    def multiply(par, c):
        x = buf[par, pl.ds(c * CHUNK * BLOCK, CHUNK * BLOCK), :]
        high = x.astype(jnp.bfloat16)
        low = (x - high.astype(jnp.float32)).astype(jnp.bfloat16)
        term = jnp.dot(
            khl[:, lanes(c)], jnp.concatenate([high, low], axis=1), preferred_element_type=jnp.float32
        )
        if c == 0:
            acc[...] = term
        else:
            acc[...] += term

    def sum_stages(loc, pieces, line, full, recv, send):
        me = here[0] * RING + here[1]
        spot = here[2] * 2 + core

        def part(e):
            return pl.ds(pl.multiple_of(e * PIECE, PIECE), PIECE)

        def to_team(source, target, stage):
            for by in range(1, TEAM):
                e = lax.rem(me + by, TEAM)
                to = device(lax.div(e, RING), lax.rem(e, RING), here[2], core)
                remote(source(e), target.at[by - 1], send.at[stage], recv.at[stage], to).start()

        def await_all(target, count, semaphore):
            whole = target.at[pl.ds(0, count)]
            pltpu.make_async_copy(whole, whole, semaphore).wait()

        def tree_sum(got):
            while len(got) > 1:
                got = [x + y for x, y in zip(got[::2], got[1::2])]
            return got[0]

        def scatter():
            to_team(lambda e: loc.at[part(e)], pieces, 0)

        def exchange():
            await_all(pieces, TEAM - 1, recv.at[0])
            line[LINE - 1] = tree_sum([pieces[k] for k in range(TEAM - 1)] + [loc[part(me), :]])
            for by in range(1, LINE):
                f = lax.rem(spot + by, LINE)
                to = device(here[0], here[1], lax.div(f, 2), lax.rem(f, 2))
                remote(line.at[LINE - 1], line.at[by - 1], send.at[1], recv.at[1], to).start()

        def gather():
            await_all(line, LINE - 1, recv.at[1])
            full[TEAM - 1] = tree_sum([line[lax.rem(spot - f + 2 * LINE - 1, LINE)] for f in range(LINE)])
            to_team(lambda e: full.at[TEAM - 1], full, 2)

        def finish():
            await_all(full, TEAM - 1, recv.at[2])
            await_all(pieces, TEAM - 1, send.at[0])
            await_all(line, LINE - 1, send.at[1])
            await_all(full, TEAM - 1, send.at[2])

        return [scatter, exchange, gather, finish]

    def whole_sum(full):
        me = here[0] * RING + here[1]
        return jnp.concatenate([full[lax.rem(me - e + 2 * TEAM - 1, TEAM)] for e in range(TEAM)], axis=0)

    def factor_panel(p):
        if p == 0:
            load_scaled(whole_sum(full_now[0]), m, scale)
        eliminate(m, inverse, scale, scaled, p)

    full_now = [None]

    def gather_and_multiply(par, tasks, work, beside):
        forward(par, 0)
        for s in range(INNER):
            if s:
                arrived(par, s)
                forward(par, s)
            for task in tasks.get(s, ()):
                task()
        for task in work:
            task()
        value = acc[...]
        value = value[:, :BLOCK] + value[:, BLOCK:]
        value = value[: 2 * BLOCK] + value[2 * BLOCK :]
        psend[...] = value[BLOCK:]
        copy = remote(psend, precv.at[par], p_send, p_recv.at[par], sibling)
        copy.start()
        for task in beside:
            task()
        whole = block(par, 1, SLOTS - 1)
        pltpu.make_async_copy(whole, whole, ag_send).wait()
        copy.wait()
        return value[:BLOCK] + precv[par]

    def local_gram(par):
        y = buf[par, pl.ds(0, BLOCK), :]
        loc[...] = exact_dot(y.T, y)

    buf[0, pl.ds(0, BLOCK), :] = start[...]
    tasks = {0: [give_kernel]}
    work = [lambda c=c: given_kernel(c) for c in range(PARTS)]
    for c in range(SLOTS // CHUNK):
        tasks[10 + 2 * c] = [lambda c=c: split_kernel(c, True)]
        work += [lambda c=c: split_kernel(c, False), lambda c=c: leaves(0, c), lambda c=c: multiply(0, c)]
    image = gather_and_multiply(0, tasks, work, [])
    buf[1, pl.ds(0, BLOCK), :] = image

    def step(t, carry):
        par = lax.rem(t, 2)
        stages = sum_stages(loc, pieces.at[par], lines.at[par], full.at[par], ar_recv.at[par], ar_send)
        full_now[0] = full.at[par]
        tasks = {0: [lambda: local_gram(par), stages[0]]}
        for at, stage in zip((9, 22), stages[1:3]):
            tasks.setdefault(at, []).append(stage)
        product = [lambda c=c: multiply(par, c) for c in range(SLOTS // CHUNK)]
        panel = [lambda p=p: factor_panel(p) for p in range(16)]
        work = product[0:3] + [lambda: leaves(par, 3), product[3], lambda: leaves(par, 4), product[4], stages[3]]
        work += panel[0:6] + [lambda: leaves(par, 5), product[5]] + panel[6:10]
        work += [lambda: leaves(par, 6), product[6], lambda: leaves(par, 7), product[7]]
        image = gather_and_multiply(par, tasks, work, panel[10:])
        buf[1 - par, pl.ds(0, BLOCK), :] = exact_dot(image, inverse[...], (((1,), (1,)), ((), ())))
        return carry

    lax.fori_loop(1, ITERATIONS, step, 0)

    par = ITERATIONS % 2
    stages = sum_stages(loc, pieces.at[par], lines.at[par], full.at[par], ar_recv.at[par], ar_send)
    late = sum_stages(cloc, cpieces, clines, cfull, cr_recv, cr_send)
    full_now[0] = full.at[par]
    local_gram(par)
    stages[0]()
    last = buf[par, pl.ds(0, BLOCK), :]
    cloc[...] = exact_dot(last.T, test[...])
    late[0]()
    stages[1]()
    late[1]()
    stages[2]()
    late[2]()
    stages[3]()
    for p in range(16):
        if p == 8:
            late[3]()
        factor_panel(p)
    image_out[...] = buf[par, pl.ds(0, BLOCK), :]
    keep = lax.broadcasted_iota(jnp.int32, (BLOCK, TEST), 0) < cutoff[0]
    kept_out[...] = exact_dot(inverse[...], whole_sum(cfull)) * jnp.where(keep, 1.0, 0.0)


def project(image, inverse, kept, subspace, projection):
    block = exact_dot(image[...], inverse[...], (((1,), (1,)), ((), ())))
    subspace[...] = block
    projection[...] = exact_dot(block, kept[...])


def per_device(kernel_rows, start_block, test_kernel, cutoff):
    f32 = jnp.float32
    vmem = pl.BlockSpec(memory_space=pltpu.VMEM)
    dma = pltpu.SemaphoreType.DMA
    narrow = jax.ShapeDtypeStruct((BLOCK, BLOCK), f32)
    broad = jax.ShapeDtypeStruct((BLOCK, TEST), f32)
    image, inverse, kept = pl.pallas_call(
        kernel,
        out_shape=(narrow, narrow, broad),
        in_specs=[pl.BlockSpec(memory_space=pl.ANY), vmem, vmem, pl.BlockSpec(memory_space=pltpu.SMEM)],
        out_specs=(vmem, vmem, vmem),
        scratch_shapes=[
            pltpu.VMEM((2, SLOTS * BLOCK, BLOCK), f32),
            pltpu.VMEM((BLOCK, 2 * SLOTS * BLOCK), f32),
            pltpu.VMEM((BLOCK, SLOTS * BLOCK), f32),
            pltpu.VMEM((BLOCK, SLOTS * BLOCK), f32),
            pltpu.VMEM((4 * BLOCK, SLOTS * BLOCK), jnp.bfloat16),
            pltpu.VMEM((4 * BLOCK, 2 * BLOCK), f32),
            pltpu.VMEM((BLOCK, BLOCK), f32),
            pltpu.VMEM((8, BLOCK), f32),
            pltpu.VMEM((GROUPED, BLOCK), f32),
            pltpu.VMEM((BLOCK, BLOCK), f32),
            pltpu.VMEM((2, TEAM, PIECE, BLOCK), f32),
            pltpu.VMEM((2, LINE, PIECE, BLOCK), f32),
            pltpu.VMEM((2, TEAM, PIECE, BLOCK), f32),
            pltpu.VMEM((BLOCK, TEST), f32),
            pltpu.VMEM((TEAM, PIECE, TEST), f32),
            pltpu.VMEM((LINE, PIECE, TEST), f32),
            pltpu.VMEM((TEAM, PIECE, TEST), f32),
            pltpu.VMEM((BLOCK, BLOCK), f32),
            pltpu.VMEM((2, BLOCK, BLOCK), f32),
            dma((2, SLOTS)),
            dma,
            dma,
            dma((PARTS,)),
            dma((PARTS,)),
            dma((2, 3)),
            dma((3,)),
            dma((3,)),
            dma((3,)),
            dma((2,)),
            dma,
        ],
        compiler_params=pltpu.CompilerParams(
            collective_id=0, has_side_effects=True, vmem_limit_bytes=56 * 1024 * 1024
        ),
        cost_estimate=pl.CostEstimate(
            flops=4 * 2 * 512 * 8192 * 256, bytes_accessed=16 * 2**20, transcendentals=0
        ),
        name="iterate",
    )(kernel_rows, start_block, test_kernel, cutoff)
    return pl.pallas_call(project, out_shape=(narrow, broad), name="project")(image, inverse, kept)


def solution(mesh):
    in_specs = (P(("row", "col"), None), P(("row", "col"), None), P(("row", "col"), None), P())
    out_specs = (P(("row", "col"), None), P(("row", "col"), None))
    return jax.shard_map(
        per_device, mesh=mesh, in_specs=in_specs, out_specs=out_specs, check_vma=False
    )
```

```python
import functools

import jax
import jax.numpy as jnp
from jax import lax
from jax.experimental import pallas as pl
from jax.experimental.pallas import tpu as pltpu
from jax.sharding import PartitionSpec as P

BLOCK = 128
TEST = 256
ITERATIONS = 4
RING = 4
SLOTS = RING**3
CHUNK = 8
PARTS = 4
TEAM = RING * RING
LINE = 2 * RING
PIECE = BLOCK // TEAM
GROUPED = BLOCK
MESH = pl.DeviceIdType.MESH
HIGHEST = lax.Precision.HIGHEST

TREE = (
    0, 49152, 196608, 65536, 28672, 16384, 12288, 69632, 4096, 114753, 131202, 53313,
    61506, 32836, 78019, 110852, 213317, 201224, 148106, 24840, 139719, 258828, 37579, 58059,
    127756, 250575, 119245, 45901, 177104, 208896, 20480, 245890, 82119, 98889, 8713, 74121,
    180878, 95118, 107472, 205905, 86479, 160914, 136273, 218193, 144276, 152722, 243029, 189717,
    103831, 169108, 222419, 230227, 226330, 194072, 255447, 91355, 124570, 42715, 165018, 156954,
    235100, 173852, 239193, 185948,
)
ORDER = [(code // 65536, code // 16384 % 4, code // 4096 % 4) for code in TREE]
PARENT = [code // 64 % 64 for code in TREE]
AFTER = [code % 64 for code in TREE]


def passed_on():
    height = [0] * SLOTS
    for s in reversed(range(1, SLOTS)):
        height[PARENT[s]] = max(height[PARENT[s]], height[s] + 1)
    sent = [[] for _ in TREE]
    for s in range(1, SLOTS):
        sent[AFTER[s]].append(s)
    for at, found in enumerate(sent):
        found.sort(key=lambda s: (PARENT[s] != at, -height[s]))
    return sent


SENT = passed_on()
INNER = len(set(PARENT))
GROUP = [s if s < INNER else max(INNER, s // CHUNK * CHUNK) for s in range(SLOTS)]


def exact_dot(a, b, dims=(((1,), (0,)), ((), ()))):
    return lax.dot_general(a, b, dims, precision=HIGHEST, preferred_element_type=jnp.float32)


def reciprocal(x):
    r = pl.reciprocal(x, approx=True)
    r = r * (2.0 - x * r)
    return r * (2.0 - x * r)


def inverse_root(x):
    r = lax.rsqrt(x)
    return r * (1.5 - 0.5 * x * r * r)


def eliminate(m, inverse, scale, scaled, panel):
    base = 8 * panel
    end = base // GROUPED * GROUPED + GROUPED
    wide = (8, BLOCK)
    lane = lax.broadcasted_iota(jnp.int32, wide, 1)
    within = (lane >= base) & (lane < base + 8)
    top = m[base : base + 8, :]
    raw = [jnp.broadcast_to(top[k : k + 1, :], wide) for k in range(8)]
    a = {
        (k, i): jnp.broadcast_to(raw[k][:, base + i : base + i + 1], wide) for k in range(8) for i in range(k, 8)
    }
    rows = [jnp.where(within, jnp.where(lane == base + k, 1.0, 0.0), raw[k]) for k in range(8)]
    over, factor = {}, {}
    for k in range(0, 8, 2):
        p, q, r = a[k, k], a[k, k + 1], a[k + 1, k + 1]
        over[k] = reciprocal(p * r - q * q)
        for i in range(k + 2, 8):
            factor[k, i] = (r * a[k, i] - q * a[k + 1, i]) * over[k]
            factor[k + 1, i] = (p * a[k + 1, i] - q * a[k, i]) * over[k]
            for j in range(i, 8):
                a[i, j] = a[i, j] - (factor[k, i] * a[k, j] + factor[k + 1, i] * a[k + 1, j])
            rows[i] = rows[i] - (factor[k, i] * rows[k] + factor[k + 1, i] * rows[k + 1])
    if base + 8 < end:
        solved = [None] * 8
        for k in range(0, 8, 2):
            p, q, r = a[k, k] * over[k], a[k, k + 1] * over[k], a[k + 1, k + 1] * over[k]
            solved[k] = r * rows[k] - q * rows[k + 1]
            solved[k + 1] = p * rows[k + 1] - q * rows[k]
        for k in (6, 4, 2):
            for i in range(k):
                solved[i] = solved[i] - (factor[i, k] * solved[k] + factor[i, k + 1] * solved[k + 1])
        for r in range(base + 8, end, 8):
            rest = m[r : r + 8, :]
            terms = [jnp.broadcast_to(rest[:, base + k : base + k + 1], wide) * solved[k] for k in range(8)]
            while len(terms) > 1:
                terms = [x + y for x, y in zip(terms[::2], terms[1::2])]
            m[r : r + 8, :] = jnp.where(within, 0.0, rest) - terms[0]
    for k in range(0, 8, 2):
        p, q = a[k, k], a[k, k + 1]
        r = inverse_root(p)
        ratio = p * over[k]
        first = rows[k] * r
        second = (rows[k + 1] - rows[k] * (q * r * r)) * (ratio * inverse_root(ratio))
        for j, done in ((base + k, first), (base + k + 1, second)):
            inverse[j : j + 1, :] = jnp.where(lane < base + 8, done * scale[...], 0.0)[0:1, :]
            if end < BLOCK:
                kept = (lane < base + 8) | (lane >= end)
                scaled[j % GROUPED : j % GROUPED + 1, :] = jnp.where(kept, done, 0.0)[0:1, :]
    if base + 8 == end and end < BLOCK:
        done = scaled[...]
        lanes = lax.broadcasted_iota(jnp.int32, (BLOCK - end, BLOCK), 1)
        rest = jnp.where((lanes >= end - GROUPED) & (lanes < end), 0.0, m[end:, :])
        m[end:, :] = rest - exact_dot(done.T[end:, :], done)


def load_scaled(value, m, scale):
    rows = lax.broadcasted_iota(jnp.int32, value.shape, 0)
    lanes = lax.broadcasted_iota(jnp.int32, value.shape, 1)
    diagonal = jnp.sum(jnp.where(rows == lanes, value, 0.0), axis=0, keepdims=True)
    over = 1.0 / jnp.broadcast_to(jnp.sum(diagonal, axis=1, keepdims=True), (8, BLOCK))
    m[...] = value * over[0:1, :]
    scale[...] = jnp.sqrt(over)


def kernel(
    kernel_hbm, start, test, cutoff, image_out, inverse, kept_out,
    buf, kall, kgive, kget, khl, acc, m, scale, scaled, loc, pieces, lines, full, cloc, cpieces, clines, cfull, psend, precv,
    ag_recv, ag_send, k_local, k_recv, k_send, ar_recv, ar_send, cr_recv, cr_send, p_recv, p_send,
):
    row, col = lax.axis_index("row"), lax.axis_index("col")
    core = lax.rem(col, 2)
    here = (
        lax.rem(lax.div(col, 2), 2) * 2 + lax.rem(row, 2),
        lax.div(col, 4),
        lax.div(row, 2),
    )

    def device(x, y, z, c):
        return (z * 2 + lax.rem(x, 2), (y * 2 + lax.div(x, 2)) * 2 + c)

    def moved(by, core=core):
        return device(*[lax.rem(p + b, RING) for p, b in zip(here, by)], core)

    def hop(s):
        return tuple((a - b) % RING for a, b in zip(ORDER[s], ORDER[PARENT[s]]))

    sibling = device(*here, 1 - core)
    near = {hop(s) for s in range(1, SLOTS)}
    near |= {tuple(-b % RING for b in by) for by in near}
    near |= {(x, y, 0) for x in range(RING) for y in range(RING)} | {(0, 0, z) for z in range(RING)}
    greet = [moved(by) for by in sorted(near - {(0, 0, 0)})]
    greet += [moved((0, 0, z), 1 - core) for z in range(RING)]

    pltpu.make_async_copy(kernel_hbm, kall, k_local).start()
    barrier = pltpu.get_barrier_semaphore()
    for other in greet:
        pl.semaphore_signal(barrier, inc=1, device_id=other, device_id_type=MESH)
    pl.semaphore_wait(barrier, len(greet))

    def remote(src, dst, send, recv, to):
        return pltpu.make_async_remote_copy(
            src_ref=src, dst_ref=dst, send_sem=send, recv_sem=recv, device_id=to, device_id_type=MESH
        )

    def block(par, s, count=1):
        return buf.at[par, pl.ds(s * BLOCK, count * BLOCK)]

    def forward(par, s):
        for child in SENT[s]:
            remote(
                block(par, PARENT[child]), block(par, child), ag_send, ag_recv.at[par, GROUP[child]], moved(hop(child))
            ).start()

    def arrived(par, group):
        whole = block(par, group, GROUP.count(group))
        pltpu.make_async_copy(whole, whole, ag_recv.at[par, group]).wait()

    def rank(s):
        x, y, z = [lax.rem(p + RING - d, RING) for p, d in zip(here, ORDER[s])]
        return (z * 2 + lax.rem(x, 2)) * 8 + y * 2 + lax.div(x, 2)

    def columns(j):
        return pl.ds(pl.multiple_of(j * BLOCK, BLOCK), BLOCK)

    def lanes(c):
        return pl.ds(c * CHUNK * BLOCK, CHUNK * BLOCK)

    def part_of_given(c):
        return pl.ds(c * (SLOTS // PARTS) * BLOCK, (SLOTS // PARTS) * BLOCK)

    def give_kernel():
        pltpu.make_async_copy(kernel_hbm, kall, k_local).wait()
        for c in range(PARTS):
            for j in range(c * (SLOTS // PARTS), (c + 1) * (SLOTS // PARTS)):
                kgive[:, j * BLOCK : (j + 1) * BLOCK] = kall[:, columns(2 * j + 1 - core)]
            there = part_of_given(c)
            remote(kgive.at[:, there], kget.at[:, there], k_send.at[c], k_recv.at[c], sibling).start()

    def given_kernel(c):
        there = part_of_given(c)
        remote(kgive.at[:, there], kget.at[:, there], k_send.at[c], k_recv.at[c], sibling).wait()

    def split_kernel(c, own):
        for s in range(c * CHUNK, (c + 1) * CHUNK):
            j = rank(s)
            value = kall[:, columns(2 * j + core)] if own else kget[:, columns(j)]
            high = value.astype(jnp.bfloat16)
            low = (value - high.astype(jnp.float32)).astype(jnp.bfloat16)
            first, there = 0 if own else BLOCK, slice(s * BLOCK, (s + 1) * BLOCK)
            khl[first : first + BLOCK, there] = high
            khl[2 * BLOCK + first : 3 * BLOCK + first, there] = low

    def leaves(par, c):
        for group in sorted(set(GROUP[c * CHUNK : (c + 1) * CHUNK])):
            if group >= INNER:
                arrived(par, group)

    def multiply(par, c):
        x = buf[par, pl.ds(c * CHUNK * BLOCK, CHUNK * BLOCK), :]
        high = x.astype(jnp.bfloat16)
        low = (x - high.astype(jnp.float32)).astype(jnp.bfloat16)
        term = jnp.dot(
            khl[:, lanes(c)], jnp.concatenate([high, low], axis=1), preferred_element_type=jnp.float32
        )
        if c == 0:
            acc[...] = term
        else:
            acc[...] += term

    def sum_stages(loc, pieces, line, full, recv, send):
        me = here[0] * RING + here[1]
        spot = here[2] * 2 + core

        def part(e):
            return pl.ds(pl.multiple_of(e * PIECE, PIECE), PIECE)

        def to_team(source, target, stage):
            for by in range(1, TEAM):
                e = lax.rem(me + by, TEAM)
                to = device(lax.div(e, RING), lax.rem(e, RING), here[2], core)
                remote(source(e), target.at[by - 1], send.at[stage], recv.at[stage], to).start()

        def await_all(target, count, semaphore):
            whole = target.at[pl.ds(0, count)]
            pltpu.make_async_copy(whole, whole, semaphore).wait()

        def tree_sum(got):
            while len(got) > 1:
                got = [x + y for x, y in zip(got[::2], got[1::2])]
            return got[0]

        def scatter():
            to_team(lambda e: loc.at[part(e)], pieces, 0)

        def exchange():
            await_all(pieces, TEAM - 1, recv.at[0])
            line[LINE - 1] = tree_sum([pieces[k] for k in range(TEAM - 1)] + [loc[part(me), :]])
            for by in range(1, LINE):
                f = lax.rem(spot + by, LINE)
                to = device(here[0], here[1], lax.div(f, 2), lax.rem(f, 2))
                remote(line.at[LINE - 1], line.at[by - 1], send.at[1], recv.at[1], to).start()

        def gather():
            await_all(line, LINE - 1, recv.at[1])
            full[TEAM - 1] = tree_sum([line[lax.rem(spot - f + 2 * LINE - 1, LINE)] for f in range(LINE)])
            to_team(lambda e: full.at[TEAM - 1], full, 2)

        def finish():
            await_all(full, TEAM - 1, recv.at[2])
            await_all(pieces, TEAM - 1, send.at[0])
            await_all(line, LINE - 1, send.at[1])
            await_all(full, TEAM - 1, send.at[2])

        return [scatter, exchange, gather, finish]

    def whole_sum(full):
        me = here[0] * RING + here[1]
        return jnp.concatenate([full[lax.rem(me - e + 2 * TEAM - 1, TEAM)] for e in range(TEAM)], axis=0)

    def factor_panel(p):
        if p == 0:
            load_scaled(whole_sum(full_now[0]), m, scale)
        eliminate(m, inverse, scale, scaled, p)

    full_now = [None]

    def gather_and_multiply(par, tasks, work, beside):
        forward(par, 0)
        for s in range(INNER):
            if s:
                arrived(par, s)
                forward(par, s)
            for task in tasks.get(s, ()):
                task()
        for task in work:
            task()
        value = acc[...]
        value = value[:, :BLOCK] + value[:, BLOCK:]
        value = value[: 2 * BLOCK] + value[2 * BLOCK :]
        psend[...] = value[BLOCK:]
        copy = remote(psend, precv.at[par], p_send, p_recv.at[par], sibling)
        copy.start()
        for task in beside:
            task()
        whole = block(par, 1, SLOTS - 1)
        pltpu.make_async_copy(whole, whole, ag_send).wait()
        copy.wait()
        return value[:BLOCK] + precv[par]

    def local_gram(par):
        y = buf[par, pl.ds(0, BLOCK), :]
        loc[...] = exact_dot(y.T, y)

    buf[0, pl.ds(0, BLOCK), :] = start[...]
    tasks = {0: [give_kernel]}
    work = [lambda c=c: given_kernel(c) for c in range(PARTS)]
    for c in range(SLOTS // CHUNK):
        tasks[10 + 2 * c] = [lambda c=c: split_kernel(c, True)]
        work += [lambda c=c: split_kernel(c, False), lambda c=c: leaves(0, c), lambda c=c: multiply(0, c)]
    image = gather_and_multiply(0, tasks, work, [])
    buf[1, pl.ds(0, BLOCK), :] = image

    def step(t, carry):
        par = lax.rem(t, 2)
        stages = sum_stages(loc, pieces.at[par], lines.at[par], full.at[par], ar_recv.at[par], ar_send)
        full_now[0] = full.at[par]
        tasks = {0: [lambda: local_gram(par), stages[0]]}
        for at, stage in zip((5, 16), stages[1:3]):
            tasks.setdefault(at, []).append(stage)
        product = [lambda c=c: multiply(par, c) for c in range(SLOTS // CHUNK)]
        panel = [lambda p=p: factor_panel(p) for p in range(16)]
        for at, c in ((11, 0), (17, 1), (23, 2)):
            tasks.setdefault(at, []).append(product[c])
        work = [lambda: leaves(par, 3), product[3], lambda: leaves(par, 4), product[4], stages[3]]
        work += panel[0:6] + [lambda: leaves(par, 5), product[5]] + panel[6:10]
        work += [lambda: leaves(par, 6), product[6], lambda: leaves(par, 7), product[7]]
        image = gather_and_multiply(par, tasks, work, panel[10:])
        buf[1 - par, pl.ds(0, BLOCK), :] = exact_dot(image, inverse[...], (((1,), (1,)), ((), ())))
        return carry

    lax.fori_loop(1, ITERATIONS, step, 0)

    par = ITERATIONS % 2
    stages = sum_stages(loc, pieces.at[par], lines.at[par], full.at[par], ar_recv.at[par], ar_send)
    late = sum_stages(cloc, cpieces, clines, cfull, cr_recv, cr_send)
    full_now[0] = full.at[par]
    local_gram(par)
    stages[0]()
    last = buf[par, pl.ds(0, BLOCK), :]
    cloc[...] = exact_dot(last.T, test[...])
    late[0]()
    stages[1]()
    late[1]()
    stages[2]()
    late[2]()
    stages[3]()
    for p in range(16):
        if p == 8:
            late[3]()
        factor_panel(p)
    image_out[...] = buf[par, pl.ds(0, BLOCK), :]
    keep = lax.broadcasted_iota(jnp.int32, (BLOCK, TEST), 0) < cutoff[0]
    kept_out[...] = exact_dot(inverse[...], whole_sum(cfull)) * jnp.where(keep, 1.0, 0.0)


def project(image, inverse, kept, subspace, projection):
    block = exact_dot(image[...], inverse[...], (((1,), (1,)), ((), ())))
    subspace[...] = block
    projection[...] = exact_dot(block, kept[...])


def per_device(kernel_rows, start_block, test_kernel, cutoff):
    f32 = jnp.float32
    vmem = pl.BlockSpec(memory_space=pltpu.VMEM)
    dma = pltpu.SemaphoreType.DMA
    narrow = jax.ShapeDtypeStruct((BLOCK, BLOCK), f32)
    broad = jax.ShapeDtypeStruct((BLOCK, TEST), f32)
    image, inverse, kept = pl.pallas_call(
        kernel,
        out_shape=(narrow, narrow, broad),
        in_specs=[pl.BlockSpec(memory_space=pl.ANY), vmem, vmem, pl.BlockSpec(memory_space=pltpu.SMEM)],
        out_specs=(vmem, vmem, vmem),
        scratch_shapes=[
            pltpu.VMEM((2, SLOTS * BLOCK, BLOCK), f32),
            pltpu.VMEM((BLOCK, 2 * SLOTS * BLOCK), f32),
            pltpu.VMEM((BLOCK, SLOTS * BLOCK), f32),
            pltpu.VMEM((BLOCK, SLOTS * BLOCK), f32),
            pltpu.VMEM((4 * BLOCK, SLOTS * BLOCK), jnp.bfloat16),
            pltpu.VMEM((4 * BLOCK, 2 * BLOCK), f32),
            pltpu.VMEM((BLOCK, BLOCK), f32),
            pltpu.VMEM((8, BLOCK), f32),
            pltpu.VMEM((GROUPED, BLOCK), f32),
            pltpu.VMEM((BLOCK, BLOCK), f32),
            pltpu.VMEM((2, TEAM, PIECE, BLOCK), f32),
            pltpu.VMEM((2, LINE, PIECE, BLOCK), f32),
            pltpu.VMEM((2, TEAM, PIECE, BLOCK), f32),
            pltpu.VMEM((BLOCK, TEST), f32),
            pltpu.VMEM((TEAM, PIECE, TEST), f32),
            pltpu.VMEM((LINE, PIECE, TEST), f32),
            pltpu.VMEM((TEAM, PIECE, TEST), f32),
            pltpu.VMEM((BLOCK, BLOCK), f32),
            pltpu.VMEM((2, BLOCK, BLOCK), f32),
            dma((2, SLOTS)),
            dma,
            dma,
            dma((PARTS,)),
            dma((PARTS,)),
            dma((2, 3)),
            dma((3,)),
            dma((3,)),
            dma((3,)),
            dma((2,)),
            dma,
        ],
        compiler_params=pltpu.CompilerParams(
            collective_id=0, has_side_effects=True, vmem_limit_bytes=56 * 1024 * 1024
        ),
        cost_estimate=pl.CostEstimate(
            flops=4 * 2 * 512 * 8192 * 256, bytes_accessed=16 * 2**20, transcendentals=0
        ),
        name="iterate",
    )(kernel_rows, start_block, test_kernel, cutoff)
    return pl.pallas_call(project, out_shape=(narrow, broad), name="project")(image, inverse, kept)


def solution(mesh):
    in_specs = (P(("row", "col"), None), P(("row", "col"), None), P(("row", "col"), None), P())
    out_specs = (P(("row", "col"), None), P(("row", "col"), None))
    return jax.shard_map(
        per_device, mesh=mesh, in_specs=in_specs, out_specs=out_specs, check_vma=False
    )
```

```python
import functools

import jax
import jax.numpy as jnp
from jax import lax
from jax.experimental import pallas as pl
from jax.experimental.pallas import tpu as pltpu
from jax.sharding import PartitionSpec as P

BLOCK = 128
TEST = 256
ITERATIONS = 4
RING = 4
SLOTS = RING**3
CHUNK = 8
PARTS = 4
TEAM = RING * RING
LINE = 2 * RING
PIECE = BLOCK // TEAM
GROUPED = BLOCK
MESH = pl.DeviceIdType.MESH
HIGHEST = lax.Precision.HIGHEST

TREE = (
    0, 49152, 196608, 65536, 28672, 16384, 12288, 69632, 4096, 114753, 131202, 53313,
    61506, 32836, 78019, 110852, 213317, 201224, 148106, 24840, 139719, 258828, 37579, 58059,
    127756, 250575, 119245, 45901, 177104, 208896, 20480, 245890, 82119, 98889, 8713, 74121,
    180878, 95118, 107472, 205905, 86479, 160914, 136273, 218193, 144276, 152722, 243029, 189717,
    103831, 169108, 222419, 230227, 226330, 194072, 255447, 91355, 124570, 42715, 165018, 156954,
    235100, 173852, 239193, 185948,
)
ORDER = [(code // 65536, code // 16384 % 4, code // 4096 % 4) for code in TREE]
PARENT = [code // 64 % 64 for code in TREE]
AFTER = [code % 64 for code in TREE]


def passed_on():
    height = [0] * SLOTS
    for s in reversed(range(1, SLOTS)):
        height[PARENT[s]] = max(height[PARENT[s]], height[s] + 1)
    sent = [[] for _ in TREE]
    for s in range(1, SLOTS):
        sent[AFTER[s]].append(s)
    for at, found in enumerate(sent):
        found.sort(key=lambda s: (PARENT[s] != at, -height[s]))
    return sent


SENT = passed_on()
INNER = len(set(PARENT))
GROUP = [s if s < INNER else max(INNER, s // CHUNK * CHUNK) for s in range(SLOTS)]


def exact_dot(a, b, dims=(((1,), (0,)), ((), ()))):
    return lax.dot_general(a, b, dims, precision=HIGHEST, preferred_element_type=jnp.float32)


def reciprocal(x):
    r = pl.reciprocal(x, approx=True)
    r = r * (2.0 - x * r)
    return r * (2.0 - x * r)


def inverse_root(x):
    r = lax.rsqrt(x)
    return r * (1.5 - 0.5 * x * r * r)


def eliminate(m, inverse, scale, scaled, panel):
    base = 8 * panel
    end = base // GROUPED * GROUPED + GROUPED
    wide = (8, BLOCK)
    lane = lax.broadcasted_iota(jnp.int32, wide, 1)
    within = (lane >= base) & (lane < base + 8)
    top = m[base : base + 8, :]
    raw = [jnp.broadcast_to(top[k : k + 1, :], wide) for k in range(8)]
    a = {
        (k, i): jnp.broadcast_to(raw[k][:, base + i : base + i + 1], wide) for k in range(8) for i in range(k, 8)
    }
    rows = [jnp.where(within, jnp.where(lane == base + k, 1.0, 0.0), raw[k]) for k in range(8)]
    over, factor = {}, {}
    for k in range(0, 8, 2):
        p, q, r = a[k, k], a[k, k + 1], a[k + 1, k + 1]
        over[k] = reciprocal(p * r - q * q)
        for i in range(k + 2, 8):
            factor[k, i] = (r * a[k, i] - q * a[k + 1, i]) * over[k]
            factor[k + 1, i] = (p * a[k + 1, i] - q * a[k, i]) * over[k]
            for j in range(i, 8):
                a[i, j] = a[i, j] - (factor[k, i] * a[k, j] + factor[k + 1, i] * a[k + 1, j])
            rows[i] = rows[i] - (factor[k, i] * rows[k] + factor[k + 1, i] * rows[k + 1])
    if base + 8 < end:
        solved = [None] * 8
        for k in range(0, 8, 2):
            p, q, r = a[k, k] * over[k], a[k, k + 1] * over[k], a[k + 1, k + 1] * over[k]
            solved[k] = r * rows[k] - q * rows[k + 1]
            solved[k + 1] = p * rows[k + 1] - q * rows[k]
        for k in (6, 4, 2):
            for i in range(k):
                solved[i] = solved[i] - (factor[i, k] * solved[k] + factor[i, k + 1] * solved[k + 1])
        for r in range(base + 8, end, 8):
            rest = m[r : r + 8, :]
            terms = [jnp.broadcast_to(rest[:, base + k : base + k + 1], wide) * solved[k] for k in range(8)]
            while len(terms) > 1:
                terms = [x + y for x, y in zip(terms[::2], terms[1::2])]
            m[r : r + 8, :] = jnp.where(within, 0.0, rest) - terms[0]
    for k in range(0, 8, 2):
        p, q = a[k, k], a[k, k + 1]
        r = inverse_root(p)
        ratio = p * over[k]
        first = rows[k] * r
        second = (rows[k + 1] - rows[k] * (q * r * r)) * (ratio * inverse_root(ratio))
        for j, done in ((base + k, first), (base + k + 1, second)):
            inverse[j : j + 1, :] = jnp.where(lane < base + 8, done * scale[...], 0.0)[0:1, :]
            if end < BLOCK:
                kept = (lane < base + 8) | (lane >= end)
                scaled[j % GROUPED : j % GROUPED + 1, :] = jnp.where(kept, done, 0.0)[0:1, :]
    if base + 8 == end and end < BLOCK:
        done = scaled[...]
        lanes = lax.broadcasted_iota(jnp.int32, (BLOCK - end, BLOCK), 1)
        rest = jnp.where((lanes >= end - GROUPED) & (lanes < end), 0.0, m[end:, :])
        m[end:, :] = rest - exact_dot(done.T[end:, :], done)


def load_scaled(value, m, scale):
    rows = lax.broadcasted_iota(jnp.int32, value.shape, 0)
    lanes = lax.broadcasted_iota(jnp.int32, value.shape, 1)
    diagonal = jnp.sum(jnp.where(rows == lanes, value, 0.0), axis=0, keepdims=True)
    over = 1.0 / jnp.broadcast_to(jnp.sum(diagonal, axis=1, keepdims=True), (8, BLOCK))
    m[...] = value * over[0:1, :]
    scale[...] = jnp.sqrt(over)


def kernel(
    kernel_hbm, start, test, cutoff, image_out, inverse, kept_out,
    buf, kall, kgive, kget, khl, acc, m, scale, scaled, loc, pieces, lines, full, cloc, cpieces, clines, cfull, psend, precv,
    ag_recv, ag_send, k_local, k_recv, k_send, ar_recv, ar_send, cr_recv, cr_send, p_recv, p_send,
):
    row, col = lax.axis_index("row"), lax.axis_index("col")
    core = lax.rem(col, 2)
    here = (
        lax.rem(lax.div(col, 2), 2) * 2 + lax.rem(row, 2),
        lax.div(col, 4),
        lax.div(row, 2),
    )

    def device(x, y, z, c):
        return (z * 2 + lax.rem(x, 2), (y * 2 + lax.div(x, 2)) * 2 + c)

    def moved(by, core=core):
        return device(*[lax.rem(p + b, RING) for p, b in zip(here, by)], core)

    def hop(s):
        return tuple((a - b) % RING for a, b in zip(ORDER[s], ORDER[PARENT[s]]))

    sibling = device(*here, 1 - core)
    near = {hop(s) for s in range(1, SLOTS)}
    near |= {tuple(-b % RING for b in by) for by in near}
    near |= {(x, y, 0) for x in range(RING) for y in range(RING)} | {(0, 0, z) for z in range(RING)}
    greet = [moved(by) for by in sorted(near - {(0, 0, 0)})]
    greet += [moved((0, 0, z), 1 - core) for z in range(RING)]

    pltpu.make_async_copy(kernel_hbm, kall, k_local).start()
    barrier = pltpu.get_barrier_semaphore()
    for other in greet:
        pl.semaphore_signal(barrier, inc=1, device_id=other, device_id_type=MESH)
    pl.semaphore_wait(barrier, len(greet))

    def remote(src, dst, send, recv, to):
        return pltpu.make_async_remote_copy(
            src_ref=src, dst_ref=dst, send_sem=send, recv_sem=recv, device_id=to, device_id_type=MESH
        )

    def block(par, s, count=1):
        return buf.at[par, pl.ds(s * BLOCK, count * BLOCK)]

    def forward(par, s):
        for child in SENT[s]:
            remote(
                block(par, PARENT[child]), block(par, child), ag_send, ag_recv.at[par, GROUP[child]], moved(hop(child))
            ).start()

    def arrived(par, group):
        whole = block(par, group, GROUP.count(group))
        pltpu.make_async_copy(whole, whole, ag_recv.at[par, group]).wait()

    def rank(s):
        x, y, z = [lax.rem(p + RING - d, RING) for p, d in zip(here, ORDER[s])]
        return (z * 2 + lax.rem(x, 2)) * 8 + y * 2 + lax.div(x, 2)

    def columns(j):
        return pl.ds(pl.multiple_of(j * BLOCK, BLOCK), BLOCK)

    def lanes(c):
        return pl.ds(c * CHUNK * BLOCK, CHUNK * BLOCK)

    def part_of_given(c):
        return pl.ds(c * (SLOTS // PARTS) * BLOCK, (SLOTS // PARTS) * BLOCK)

    def give_kernel():
        pltpu.make_async_copy(kernel_hbm, kall, k_local).wait()
        for c in range(PARTS):
            for j in range(c * (SLOTS // PARTS), (c + 1) * (SLOTS // PARTS)):
                kgive[:, j * BLOCK : (j + 1) * BLOCK] = kall[:, columns(2 * j + 1 - core)]
            there = part_of_given(c)
            remote(kgive.at[:, there], kget.at[:, there], k_send.at[c], k_recv.at[c], sibling).start()

    def given_kernel(c):
        there = part_of_given(c)
        remote(kgive.at[:, there], kget.at[:, there], k_send.at[c], k_recv.at[c], sibling).wait()

    def split_kernel(c, own):
        for s in range(c * CHUNK, (c + 1) * CHUNK):
            j = rank(s)
            value = kall[:, columns(2 * j + core)] if own else kget[:, columns(j)]
            high = value.astype(jnp.bfloat16)
            low = (value - high.astype(jnp.float32)).astype(jnp.bfloat16)
            first, there = 0 if own else BLOCK, slice(s * BLOCK, (s + 1) * BLOCK)
            khl[first : first + BLOCK, there] = high
            khl[2 * BLOCK + first : 3 * BLOCK + first, there] = low

    def leaves(par, c):
        for group in sorted(set(GROUP[c * CHUNK : (c + 1) * CHUNK])):
            if group >= INNER:
                arrived(par, group)

    def multiply(par, c):
        x = buf[par, pl.ds(c * CHUNK * BLOCK, CHUNK * BLOCK), :]
        high = x.astype(jnp.bfloat16)
        low = (x - high.astype(jnp.float32)).astype(jnp.bfloat16)
        term = jnp.dot(
            khl[:, lanes(c)], jnp.concatenate([high, low], axis=1), preferred_element_type=jnp.float32
        )
        if c == 0:
            acc[...] = term
        else:
            acc[...] += term

    def sum_stages(loc, pieces, line, full, recv, send):
        me = here[0] * RING + here[1]
        spot = here[2] * 2 + core

        def part(e):
            return pl.ds(pl.multiple_of(e * PIECE, PIECE), PIECE)

        def to_team(source, target, stage):
            for by in range(1, TEAM):
                e = lax.rem(me + by, TEAM)
                to = device(lax.div(e, RING), lax.rem(e, RING), here[2], core)
                remote(source(e), target.at[by - 1], send.at[stage], recv.at[stage], to).start()

        def await_all(target, count, semaphore):
            whole = target.at[pl.ds(0, count)]
            pltpu.make_async_copy(whole, whole, semaphore).wait()

        def tree_sum(got):
            while len(got) > 1:
                got = [x + y for x, y in zip(got[::2], got[1::2])]
            return got[0]

        def scatter():
            to_team(lambda e: loc.at[part(e)], pieces, 0)

        def exchange():
            await_all(pieces, TEAM - 1, recv.at[0])
            line[LINE - 1] = tree_sum([pieces[k] for k in range(TEAM - 1)] + [loc[part(me), :]])
            for by in range(1, LINE):
                f = lax.rem(spot + by, LINE)
                to = device(here[0], here[1], lax.div(f, 2), lax.rem(f, 2))
                remote(line.at[LINE - 1], line.at[by - 1], send.at[1], recv.at[1], to).start()

        def gather():
            await_all(line, LINE - 1, recv.at[1])
            full[TEAM - 1] = tree_sum([line[lax.rem(spot - f + 2 * LINE - 1, LINE)] for f in range(LINE)])
            to_team(lambda e: full.at[TEAM - 1], full, 2)

        def finish():
            await_all(full, TEAM - 1, recv.at[2])
            await_all(pieces, TEAM - 1, send.at[0])
            await_all(line, LINE - 1, send.at[1])
            await_all(full, TEAM - 1, send.at[2])

        return [scatter, exchange, gather, finish]

    def whole_sum(full):
        me = here[0] * RING + here[1]
        return jnp.concatenate([full[lax.rem(me - e + 2 * TEAM - 1, TEAM)] for e in range(TEAM)], axis=0)

    def factor_panel(p):
        if p == 0:
            load_scaled(whole_sum(full_now[0]), m, scale)
        eliminate(m, inverse, scale, scaled, p)

    full_now = [None]

    def gather_and_multiply(par, tasks, work, beside):
        forward(par, 0)
        for s in range(INNER):
            if s:
                arrived(par, s)
                forward(par, s)
            for task in tasks.get(s, ()):
                task()
        for task in work:
            task()
        value = acc[...]
        value = value[:, :BLOCK] + value[:, BLOCK:]
        value = value[: 2 * BLOCK] + value[2 * BLOCK :]
        psend[...] = value[BLOCK:]
        copy = remote(psend, precv.at[par], p_send, p_recv.at[par], sibling)
        copy.start()
        for task in beside:
            task()
        whole = block(par, 1, SLOTS - 1)
        pltpu.make_async_copy(whole, whole, ag_send).wait()
        copy.wait()
        return value[:BLOCK] + precv[par]

    def local_gram(par):
        y = buf[par, pl.ds(0, BLOCK), :]
        loc[...] = exact_dot(y.T, y)

    buf[0, pl.ds(0, BLOCK), :] = start[...]
    tasks = {0: [give_kernel]}
    work = [lambda c=c: given_kernel(c) for c in range(PARTS)]
    for c in range(SLOTS // CHUNK):
        tasks[10 + 2 * c] = [lambda c=c: split_kernel(c, True)]
        work += [lambda c=c: split_kernel(c, False), lambda c=c: leaves(0, c), lambda c=c: multiply(0, c)]
    image = gather_and_multiply(0, tasks, work, [])
    buf[1, pl.ds(0, BLOCK), :] = image

    def step(t, carry):
        par = lax.rem(t, 2)
        stages = sum_stages(loc, pieces.at[par], lines.at[par], full.at[par], ar_recv.at[par], ar_send)
        full_now[0] = full.at[par]
        tasks = {0: [lambda: local_gram(par), stages[0]]}
        for at, stage in zip((6, 18), stages[1:3]):
            tasks.setdefault(at, []).append(stage)
        product = [lambda c=c: multiply(par, c) for c in range(SLOTS // CHUNK)]
        panel = [lambda p=p: factor_panel(p) for p in range(16)]
        for at, c in ((13, 0), (17, 1)):
            tasks.setdefault(at, []).append(product[c])
        work = [product[2], lambda: leaves(par, 3), product[3], lambda: leaves(par, 4), product[4], stages[3]]
        work += panel[0:6] + [lambda: leaves(par, 5), product[5]] + panel[6:10]
        work += [lambda: leaves(par, 6), product[6], lambda: leaves(par, 7), product[7]]
        image = gather_and_multiply(par, tasks, work, panel[10:])
        buf[1 - par, pl.ds(0, BLOCK), :] = exact_dot(image, inverse[...], (((1,), (1,)), ((), ())))
        return carry

    lax.fori_loop(1, ITERATIONS, step, 0)

    par = ITERATIONS % 2
    stages = sum_stages(loc, pieces.at[par], lines.at[par], full.at[par], ar_recv.at[par], ar_send)
    late = sum_stages(cloc, cpieces, clines, cfull, cr_recv, cr_send)
    full_now[0] = full.at[par]
    local_gram(par)
    stages[0]()
    last = buf[par, pl.ds(0, BLOCK), :]
    cloc[...] = exact_dot(last.T, test[...])
    late[0]()
    stages[1]()
    stages[2]()
    late[1]()
    stages[3]()
    for p in range(16):
        if p == 4:
            late[2]()
        if p == 12:
            late[3]()
        factor_panel(p)
    image_out[...] = buf[par, pl.ds(0, BLOCK), :]
    keep = lax.broadcasted_iota(jnp.int32, (BLOCK, TEST), 0) < cutoff[0]
    kept_out[...] = exact_dot(inverse[...], whole_sum(cfull)) * jnp.where(keep, 1.0, 0.0)


def project(image, inverse, kept, subspace, projection):
    block = exact_dot(image[...], inverse[...], (((1,), (1,)), ((), ())))
    subspace[...] = block
    projection[...] = exact_dot(block, kept[...])


def per_device(kernel_rows, start_block, test_kernel, cutoff):
    f32 = jnp.float32
    vmem = pl.BlockSpec(memory_space=pltpu.VMEM)
    dma = pltpu.SemaphoreType.DMA
    narrow = jax.ShapeDtypeStruct((BLOCK, BLOCK), f32)
    broad = jax.ShapeDtypeStruct((BLOCK, TEST), f32)
    image, inverse, kept = pl.pallas_call(
        kernel,
        out_shape=(narrow, narrow, broad),
        in_specs=[pl.BlockSpec(memory_space=pl.ANY), vmem, vmem, pl.BlockSpec(memory_space=pltpu.SMEM)],
        out_specs=(vmem, vmem, vmem),
        scratch_shapes=[
            pltpu.VMEM((2, SLOTS * BLOCK, BLOCK), f32),
            pltpu.VMEM((BLOCK, 2 * SLOTS * BLOCK), f32),
            pltpu.VMEM((BLOCK, SLOTS * BLOCK), f32),
            pltpu.VMEM((BLOCK, SLOTS * BLOCK), f32),
            pltpu.VMEM((4 * BLOCK, SLOTS * BLOCK), jnp.bfloat16),
            pltpu.VMEM((4 * BLOCK, 2 * BLOCK), f32),
            pltpu.VMEM((BLOCK, BLOCK), f32),
            pltpu.VMEM((8, BLOCK), f32),
            pltpu.VMEM((GROUPED, BLOCK), f32),
            pltpu.VMEM((BLOCK, BLOCK), f32),
            pltpu.VMEM((2, TEAM, PIECE, BLOCK), f32),
            pltpu.VMEM((2, LINE, PIECE, BLOCK), f32),
            pltpu.VMEM((2, TEAM, PIECE, BLOCK), f32),
            pltpu.VMEM((BLOCK, TEST), f32),
            pltpu.VMEM((TEAM, PIECE, TEST), f32),
            pltpu.VMEM((LINE, PIECE, TEST), f32),
            pltpu.VMEM((TEAM, PIECE, TEST), f32),
            pltpu.VMEM((BLOCK, BLOCK), f32),
            pltpu.VMEM((2, BLOCK, BLOCK), f32),
            dma((2, SLOTS)),
            dma,
            dma,
            dma((PARTS,)),
            dma((PARTS,)),
            dma((2, 3)),
            dma((3,)),
            dma((3,)),
            dma((3,)),
            dma((2,)),
            dma,
        ],
        compiler_params=pltpu.CompilerParams(
            collective_id=0, has_side_effects=True, vmem_limit_bytes=56 * 1024 * 1024
        ),
        cost_estimate=pl.CostEstimate(
            flops=4 * 2 * 512 * 8192 * 256, bytes_accessed=16 * 2**20, transcendentals=0
        ),
        name="iterate",
    )(kernel_rows, start_block, test_kernel, cutoff)
    return pl.pallas_call(project, out_shape=(narrow, broad), name="project")(image, inverse, kept)


def solution(mesh):
    in_specs = (P(("row", "col"), None), P(("row", "col"), None), P(("row", "col"), None), P())
    out_specs = (P(("row", "col"), None), P(("row", "col"), None))
    return jax.shard_map(
        per_device, mesh=mesh, in_specs=in_specs, out_specs=out_specs, check_vma=False
    )
```

```python
import functools

import jax
import jax.numpy as jnp
from jax import lax
from jax.experimental import pallas as pl
from jax.experimental.pallas import tpu as pltpu
from jax.sharding import PartitionSpec as P

BLOCK = 128
TEST = 256
ITERATIONS = 4
RING = 4
SLOTS = RING**3
CHUNK = 8
PARTS = 4
TEAM = RING * RING
LINE = 2 * RING
PIECE = BLOCK // TEAM
GROUPED = BLOCK
MESH = pl.DeviceIdType.MESH
HIGHEST = lax.Precision.HIGHEST

TREE = (
    0, 49152, 196608, 65536, 28672, 16384, 12288, 69632, 4096, 114753, 131202, 53313,
    61506, 32836, 78019, 110852, 213317, 201224, 148106, 24840, 139719, 258828, 37579, 58059,
    127756, 250575, 119245, 45901, 177104, 208896, 20480, 245890, 82119, 98889, 8713, 74121,
    180878, 95118, 107472, 205905, 86479, 160914, 136273, 218193, 144276, 152722, 243029, 189717,
    103831, 169108, 222419, 230227, 226330, 194072, 255447, 91355, 124570, 42715, 165018, 156954,
    235100, 173852, 239193, 185948,
)
ORDER = [(code // 65536, code // 16384 % 4, code // 4096 % 4) for code in TREE]
PARENT = [code // 64 % 64 for code in TREE]
AFTER = [code % 64 for code in TREE]


def passed_on():
    height = [0] * SLOTS
    for s in reversed(range(1, SLOTS)):
        height[PARENT[s]] = max(height[PARENT[s]], height[s] + 1)
    sent = [[] for _ in TREE]
    for s in range(1, SLOTS):
        sent[AFTER[s]].append(s)
    for at, found in enumerate(sent):
        found.sort(key=lambda s: (PARENT[s] != at, -height[s]))
    return sent


SENT = passed_on()
INNER = len(set(PARENT))
GROUP = [s if s < INNER else max(INNER, s // CHUNK * CHUNK) for s in range(SLOTS)]


def exact_dot(a, b, dims=(((1,), (0,)), ((), ()))):
    return lax.dot_general(a, b, dims, precision=HIGHEST, preferred_element_type=jnp.float32)


def reciprocal(x):
    r = pl.reciprocal(x, approx=True)
    r = r * (2.0 - x * r)
    return r * (2.0 - x * r)


def inverse_root(x):
    r = lax.rsqrt(x)
    return r * (1.5 - 0.5 * x * r * r)


def eliminate(m, inverse, scale, scaled, panel):
    base = 8 * panel
    end = base // GROUPED * GROUPED + GROUPED
    wide = (8, BLOCK)
    lane = lax.broadcasted_iota(jnp.int32, wide, 1)
    within = (lane >= base) & (lane < base + 8)
    top = m[base : base + 8, :]
    raw = [jnp.broadcast_to(top[k : k + 1, :], wide) for k in range(8)]
    a = {
        (k, i): jnp.broadcast_to(raw[k][:, base + i : base + i + 1], wide) for k in range(8) for i in range(k, 8)
    }
    rows = [jnp.where(within, jnp.where(lane == base + k, 1.0, 0.0), raw[k]) for k in range(8)]
    over, factor = {}, {}
    for k in range(0, 8, 2):
        p, q, r = a[k, k], a[k, k + 1], a[k + 1, k + 1]
        over[k] = reciprocal(p * r - q * q)
        for i in range(k + 2, 8):
            factor[k, i] = (r * a[k, i] - q * a[k + 1, i]) * over[k]
            factor[k + 1, i] = (p * a[k + 1, i] - q * a[k, i]) * over[k]
            for j in range(i, 8):
                a[i, j] = a[i, j] - (factor[k, i] * a[k, j] + factor[k + 1, i] * a[k + 1, j])
            rows[i] = rows[i] - (factor[k, i] * rows[k] + factor[k + 1, i] * rows[k + 1])
    if base + 8 < end:
        solved = [None] * 8
        for k in range(0, 8, 2):
            p, q, r = a[k, k] * over[k], a[k, k + 1] * over[k], a[k + 1, k + 1] * over[k]
            solved[k] = r * rows[k] - q * rows[k + 1]
            solved[k + 1] = p * rows[k + 1] - q * rows[k]
        for k in (6, 4, 2):
            for i in range(k):
                solved[i] = solved[i] - (factor[i, k] * solved[k] + factor[i, k + 1] * solved[k + 1])
        for r in range(base + 8, end, 8):
            rest = m[r : r + 8, :]
            terms = [jnp.broadcast_to(rest[:, base + k : base + k + 1], wide) * solved[k] for k in range(8)]
            while len(terms) > 1:
                terms = [x + y for x, y in zip(terms[::2], terms[1::2])]
            m[r : r + 8, :] = jnp.where(within, 0.0, rest) - terms[0]
    for k in range(0, 8, 2):
        p, q = a[k, k], a[k, k + 1]
        r = inverse_root(p)
        ratio = p * over[k]
        first = rows[k] * r
        second = (rows[k + 1] - rows[k] * (q * r * r)) * (ratio * inverse_root(ratio))
        for j, done in ((base + k, first), (base + k + 1, second)):
            inverse[j : j + 1, :] = jnp.where(lane < base + 8, done * scale[...], 0.0)[0:1, :]
            if end < BLOCK:
                kept = (lane < base + 8) | (lane >= end)
                scaled[j % GROUPED : j % GROUPED + 1, :] = jnp.where(kept, done, 0.0)[0:1, :]
    if base + 8 == end and end < BLOCK:
        done = scaled[...]
        lanes = lax.broadcasted_iota(jnp.int32, (BLOCK - end, BLOCK), 1)
        rest = jnp.where((lanes >= end - GROUPED) & (lanes < end), 0.0, m[end:, :])
        m[end:, :] = rest - exact_dot(done.T[end:, :], done)


def load_scaled(value, m, scale):
    rows = lax.broadcasted_iota(jnp.int32, value.shape, 0)
    lanes = lax.broadcasted_iota(jnp.int32, value.shape, 1)
    diagonal = jnp.sum(jnp.where(rows == lanes, value, 0.0), axis=0, keepdims=True)
    over = 1.0 / jnp.broadcast_to(jnp.sum(diagonal, axis=1, keepdims=True), (8, BLOCK))
    m[...] = value * over[0:1, :]
    scale[...] = jnp.sqrt(over)


def kernel(
    kernel_hbm, start, test, cutoff, image_out, inverse, kept_out,
    buf, kall, kgive, kget, khl, acc, m, scale, scaled, loc, pieces, lines, full, cloc, cpieces, clines, cfull, psend, precv,
    ag_recv, ag_send, k_local, k_recv, k_send, ar_recv, ar_send, cr_recv, cr_send, p_recv, p_send,
):
    row, col = lax.axis_index("row"), lax.axis_index("col")
    core = lax.rem(col, 2)
    here = (
        lax.rem(lax.div(col, 2), 2) * 2 + lax.rem(row, 2),
        lax.div(col, 4),
        lax.div(row, 2),
    )

    def device(x, y, z, c):
        return (z * 2 + lax.rem(x, 2), (y * 2 + lax.div(x, 2)) * 2 + c)

    def moved(by, core=core):
        return device(*[lax.rem(p + b, RING) for p, b in zip(here, by)], core)

    def hop(s):
        return tuple((a - b) % RING for a, b in zip(ORDER[s], ORDER[PARENT[s]]))

    sibling = device(*here, 1 - core)
    near = {hop(s) for s in range(1, SLOTS)}
    near |= {tuple(-b % RING for b in by) for by in near}
    near |= {(x, y, 0) for x in range(RING) for y in range(RING)} | {(0, 0, z) for z in range(RING)}
    greet = [moved(by) for by in sorted(near - {(0, 0, 0)})]
    greet += [moved((0, 0, z), 1 - core) for z in range(RING)]

    pltpu.make_async_copy(kernel_hbm, kall, k_local).start()
    barrier = pltpu.get_barrier_semaphore()
    for other in greet:
        pl.semaphore_signal(barrier, inc=1, device_id=other, device_id_type=MESH)
    pl.semaphore_wait(barrier, len(greet))

    def remote(src, dst, send, recv, to):
        return pltpu.make_async_remote_copy(
            src_ref=src, dst_ref=dst, send_sem=send, recv_sem=recv, device_id=to, device_id_type=MESH
        )

    def block(par, s, count=1):
        return buf.at[par, pl.ds(s * BLOCK, count * BLOCK)]

    def forward(par, s):
        for child in SENT[s]:
            remote(
                block(par, PARENT[child]), block(par, child), ag_send, ag_recv.at[par, GROUP[child]], moved(hop(child))
            ).start()

    def arrived(par, group):
        whole = block(par, group, GROUP.count(group))
        pltpu.make_async_copy(whole, whole, ag_recv.at[par, group]).wait()

    def rank(s):
        x, y, z = [lax.rem(p + RING - d, RING) for p, d in zip(here, ORDER[s])]
        return (z * 2 + lax.rem(x, 2)) * 8 + y * 2 + lax.div(x, 2)

    def columns(j):
        return pl.ds(pl.multiple_of(j * BLOCK, BLOCK), BLOCK)

    def lanes(c):
        return pl.ds(c * CHUNK * BLOCK, CHUNK * BLOCK)

    def part_of_given(c):
        return pl.ds(c * (SLOTS // PARTS) * BLOCK, (SLOTS // PARTS) * BLOCK)

    def give_kernel():
        pltpu.make_async_copy(kernel_hbm, kall, k_local).wait()
        for c in range(PARTS):
            for j in range(c * (SLOTS // PARTS), (c + 1) * (SLOTS // PARTS)):
                kgive[:, j * BLOCK : (j + 1) * BLOCK] = kall[:, columns(2 * j + 1 - core)]
            there = part_of_given(c)
            remote(kgive.at[:, there], kget.at[:, there], k_send.at[c], k_recv.at[c], sibling).start()

    def given_kernel(c):
        there = part_of_given(c)
        remote(kgive.at[:, there], kget.at[:, there], k_send.at[c], k_recv.at[c], sibling).wait()

    def split_kernel(c, own):
        for s in range(c * CHUNK, (c + 1) * CHUNK):
            j = rank(s)
            value = kall[:, columns(2 * j + core)] if own else kget[:, columns(j)]
            high = value.astype(jnp.bfloat16)
            low = (value - high.astype(jnp.float32)).astype(jnp.bfloat16)
            first, there = 0 if own else BLOCK, slice(s * BLOCK, (s + 1) * BLOCK)
            khl[first : first + BLOCK, there] = high
            khl[2 * BLOCK + first : 3 * BLOCK + first, there] = low

    def leaves(par, c):
        for group in sorted(set(GROUP[c * CHUNK : (c + 1) * CHUNK])):
            if group >= INNER:
                arrived(par, group)

    def multiply(par, c):
        x = buf[par, pl.ds(c * CHUNK * BLOCK, CHUNK * BLOCK), :]
        high = x.astype(jnp.bfloat16)
        low = (x - high.astype(jnp.float32)).astype(jnp.bfloat16)
        term = jnp.dot(
            khl[:, lanes(c)], jnp.concatenate([high, low], axis=1), preferred_element_type=jnp.float32
        )
        if c == 0:
            acc[...] = term
        else:
            acc[...] += term

    def sum_stages(loc, pieces, line, full, recv, send):
        me = here[0] * RING + here[1]
        spot = here[2] * 2 + core

        def part(e):
            return pl.ds(pl.multiple_of(e * PIECE, PIECE), PIECE)

        def to_team(source, target, stage):
            for by in range(1, TEAM):
                e = lax.rem(me + by, TEAM)
                to = device(lax.div(e, RING), lax.rem(e, RING), here[2], core)
                remote(source(e), target.at[by - 1], send.at[stage], recv.at[stage], to).start()

        def await_all(target, count, semaphore):
            whole = target.at[pl.ds(0, count)]
            pltpu.make_async_copy(whole, whole, semaphore).wait()

        def tree_sum(got):
            while len(got) > 1:
                got = [x + y for x, y in zip(got[::2], got[1::2])]
            return got[0]

        def scatter():
            to_team(lambda e: loc.at[part(e)], pieces, 0)

        def exchange():
            await_all(pieces, TEAM - 1, recv.at[0])
            line[LINE - 1] = tree_sum([pieces[k] for k in range(TEAM - 1)] + [loc[part(me), :]])
            for by in range(1, LINE):
                f = lax.rem(spot + by, LINE)
                to = device(here[0], here[1], lax.div(f, 2), lax.rem(f, 2))
                remote(line.at[LINE - 1], line.at[by - 1], send.at[1], recv.at[1], to).start()

        def gather():
            await_all(line, LINE - 1, recv.at[1])
            full[TEAM - 1] = tree_sum([line[lax.rem(spot - f + 2 * LINE - 1, LINE)] for f in range(LINE)])
            to_team(lambda e: full.at[TEAM - 1], full, 2)

        def finish():
            await_all(full, TEAM - 1, recv.at[2])
            await_all(pieces, TEAM - 1, send.at[0])
            await_all(line, LINE - 1, send.at[1])
            await_all(full, TEAM - 1, send.at[2])

        return [scatter, exchange, gather, finish]

    def whole_sum(full):
        me = here[0] * RING + here[1]
        return jnp.concatenate([full[lax.rem(me - e + 2 * TEAM - 1, TEAM)] for e in range(TEAM)], axis=0)

    def factor_panel(p):
        if p == 0:
            load_scaled(whole_sum(full_now[0]), m, scale)
        eliminate(m, inverse, scale, scaled, p)

    full_now = [None]

    def gather_and_multiply(par, tasks, work, beside):
        forward(par, 0)
        for s in range(INNER):
            if s:
                arrived(par, s)
                forward(par, s)
            for task in tasks.get(s, ()):
                task()
        for task in work:
            task()
        value = acc[...]
        value = value[:, :BLOCK] + value[:, BLOCK:]
        value = value[: 2 * BLOCK] + value[2 * BLOCK :]
        psend[...] = value[BLOCK:]
        copy = remote(psend, precv.at[par], p_send, p_recv.at[par], sibling)
        copy.start()
        for task in beside:
            task()
        whole = block(par, 1, SLOTS - 1)
        pltpu.make_async_copy(whole, whole, ag_send).wait()
        copy.wait()
        return value[:BLOCK] + precv[par]

    def local_gram(par):
        y = buf[par, pl.ds(0, BLOCK), :]
        loc[...] = exact_dot(y.T, y)

    buf[0, pl.ds(0, BLOCK), :] = start[...]
    tasks = {0: [give_kernel]}
    work = [lambda c=c: given_kernel(c) for c in range(PARTS)]
    for c in range(SLOTS // CHUNK):
        tasks[10 + 2 * c] = [lambda c=c: split_kernel(c, True)]
        work += [lambda c=c: split_kernel(c, False), lambda c=c: leaves(0, c), lambda c=c: multiply(0, c)]
    image = gather_and_multiply(0, tasks, work, [])
    buf[1, pl.ds(0, BLOCK), :] = image

    def step(t, carry):
        par = lax.rem(t, 2)
        stages = sum_stages(loc, pieces.at[par], lines.at[par], full.at[par], ar_recv.at[par], ar_send)
        full_now[0] = full.at[par]
        tasks = {0: [lambda: local_gram(par), stages[0]]}
        for at, stage in zip((6, 18), stages[1:3]):
            tasks.setdefault(at, []).append(stage)
        product = [lambda c=c: multiply(par, c) for c in range(SLOTS // CHUNK)]
        panel = [lambda p=p: factor_panel(p) for p in range(16)]
        for at, c in ((13, 0), (17, 1)):
            tasks.setdefault(at, []).append(product[c])
        work = [product[2], lambda: leaves(par, 3), product[3], lambda: leaves(par, 4), product[4], stages[3]]
        work += panel[0:6] + [lambda: leaves(par, 5), product[5]] + panel[6:8]
        work += [lambda: leaves(par, 6), product[6], lambda: leaves(par, 7), product[7]]
        image = gather_and_multiply(par, tasks, work, panel[8:])
        buf[1 - par, pl.ds(0, BLOCK), :] = exact_dot(image, inverse[...], (((1,), (1,)), ((), ())))
        return carry

    lax.fori_loop(1, ITERATIONS, step, 0)

    par = ITERATIONS % 2
    stages = sum_stages(loc, pieces.at[par], lines.at[par], full.at[par], ar_recv.at[par], ar_send)
    late = sum_stages(cloc, cpieces, clines, cfull, cr_recv, cr_send)
    full_now[0] = full.at[par]
    local_gram(par)
    stages[0]()
    last = buf[par, pl.ds(0, BLOCK), :]
    cloc[...] = exact_dot(last.T, test[...])
    late[0]()
    stages[1]()
    late[1]()
    stages[2]()
    late[2]()
    stages[3]()
    for p in range(16):
        if p == 8:
            late[3]()
        factor_panel(p)
    image_out[...] = buf[par, pl.ds(0, BLOCK), :]
    keep = lax.broadcasted_iota(jnp.int32, (BLOCK, TEST), 0) < cutoff[0]
    kept_out[...] = exact_dot(inverse[...], whole_sum(cfull)) * jnp.where(keep, 1.0, 0.0)


def project(image, inverse, kept, subspace, projection):
    block = exact_dot(image[...], inverse[...], (((1,), (1,)), ((), ())))
    subspace[...] = block
    projection[...] = exact_dot(block, kept[...])


def per_device(kernel_rows, start_block, test_kernel, cutoff):
    f32 = jnp.float32
    vmem = pl.BlockSpec(memory_space=pltpu.VMEM)
    dma = pltpu.SemaphoreType.DMA
    narrow = jax.ShapeDtypeStruct((BLOCK, BLOCK), f32)
    broad = jax.ShapeDtypeStruct((BLOCK, TEST), f32)
    image, inverse, kept = pl.pallas_call(
        kernel,
        out_shape=(narrow, narrow, broad),
        in_specs=[pl.BlockSpec(memory_space=pl.ANY), vmem, vmem, pl.BlockSpec(memory_space=pltpu.SMEM)],
        out_specs=(vmem, vmem, vmem),
        scratch_shapes=[
            pltpu.VMEM((2, SLOTS * BLOCK, BLOCK), f32),
            pltpu.VMEM((BLOCK, 2 * SLOTS * BLOCK), f32),
            pltpu.VMEM((BLOCK, SLOTS * BLOCK), f32),
            pltpu.VMEM((BLOCK, SLOTS * BLOCK), f32),
            pltpu.VMEM((4 * BLOCK, SLOTS * BLOCK), jnp.bfloat16),
            pltpu.VMEM((4 * BLOCK, 2 * BLOCK), f32),
            pltpu.VMEM((BLOCK, BLOCK), f32),
            pltpu.VMEM((8, BLOCK), f32),
            pltpu.VMEM((GROUPED, BLOCK), f32),
            pltpu.VMEM((BLOCK, BLOCK), f32),
            pltpu.VMEM((2, TEAM, PIECE, BLOCK), f32),
            pltpu.VMEM((2, LINE, PIECE, BLOCK), f32),
            pltpu.VMEM((2, TEAM, PIECE, BLOCK), f32),
            pltpu.VMEM((BLOCK, TEST), f32),
            pltpu.VMEM((TEAM, PIECE, TEST), f32),
            pltpu.VMEM((LINE, PIECE, TEST), f32),
            pltpu.VMEM((TEAM, PIECE, TEST), f32),
            pltpu.VMEM((BLOCK, BLOCK), f32),
            pltpu.VMEM((2, BLOCK, BLOCK), f32),
            dma((2, SLOTS)),
            dma,
            dma,
            dma((PARTS,)),
            dma((PARTS,)),
            dma((2, 3)),
            dma((3,)),
            dma((3,)),
            dma((3,)),
            dma((2,)),
            dma,
        ],
        compiler_params=pltpu.CompilerParams(
            collective_id=0, has_side_effects=True, vmem_limit_bytes=56 * 1024 * 1024
        ),
        cost_estimate=pl.CostEstimate(
            flops=4 * 2 * 512 * 8192 * 256, bytes_accessed=16 * 2**20, transcendentals=0
        ),
        name="iterate",
    )(kernel_rows, start_block, test_kernel, cutoff)
    return pl.pallas_call(project, out_shape=(narrow, broad), name="project")(image, inverse, kept)


def solution(mesh):
    in_specs = (P(("row", "col"), None), P(("row", "col"), None), P(("row", "col"), None), P())
    out_specs = (P(("row", "col"), None), P(("row", "col"), None))
    return jax.shard_map(
        per_device, mesh=mesh, in_specs=in_specs, out_specs=out_specs, check_vma=False
    )
```
